32 devices in a mesh: line: 8 (over y, x, core), seg: 4 (over z).
Axes of the slice: x: 2, y: 2, z: 4, core: 2. Of those that a mesh axis runs over, the one named last changes fastest.
Arguments:
- points: float32 [8, 4, 3, 32768], P('line', 'seg'), may hold values from -1 to 1
- rows: int32 [8, 4, 2, 3072], P('line', 'seg'), may hold values from -1 to 32767, as said below
- cells: int32 [8, 4, 2, 24], P('line', 'seg'), may hold values from -1 to 15, as said below
- pose: float32 [12, 8], P(None, 'line'), as said below
Outputs:
- matched: float32 [8, 4, 2, 5, 3072], P('line', 'seg')
- fitted_pose: float32 [12, 8], P(None, 'line')
- final_spread: float32 [1], replicated
The draws below stay inside these ranges and needn't reach their ends.
Inputs may be any that keep to these rules, and one draw needn't show every extreme that they name: In each block of 128 slots the filled slots come first; every slot of an empty block is empty; rows toward the lower line lie in the lower margin (below 8192), rows toward the upper line in the upper margin (24576 or more); the lists of line 0 toward the lower side and of line 8 - 1 toward the upper side are empty. `cells`: empty blocks come after the others; in segment 0 of every line all blocks toward an existing adjacent line are filled. `pose`: every 3x3 part is within about 0.5 of the identity.
All inputs are finite; a program needn't handle non-finite values.
Results may differ from the reference program's by a relative error of at most 0.0003.
Values sent between devices are 32-bit elements; how exact they have to be, the bound alone decides.
No kernel may reach another device: no remote copies, remote signals or barrier semaphores. Data moves between devices by JAX's collectives and lax.ppermute only.
A program may use at most 64 MiB of HBM per device.

```python
import jax
import jax.numpy as jnp
from jax import lax

NCELL = 16
CT = 512
NPTS = 32768
NBLK = 24
BLOCK = 128
ITERS = 2
SLOTS = 3072
LINES = 8
SEGS = 4


def route_tables(key):
    margin = NCELL * CT
    base = jax.random.fold_in(key, 11)
    key_count, key_cell, key_fill, key_rows = jax.random.split(base, 4)
    block_count = jax.random.randint(key_count, (LINES, SEGS, 2, 1), NBLK // 3, NBLK + 1)
    seg_index = jnp.arange(SEGS).reshape(1, SEGS, 1, 1)
    block_count = jnp.where(seg_index == 0, NBLK, block_count)
    line_index = jnp.arange(LINES).reshape(LINES, 1, 1, 1)
    side_index = jnp.arange(2).reshape(1, 1, 2, 1)
    edge_lists = (line_index == 0) & (side_index == 0) | (line_index == LINES - 1) & (side_index == 1)
    block_index = jnp.arange(NBLK).reshape(1, 1, 1, NBLK)
    live_blocks = (block_index < block_count) & jnp.logical_not(edge_lists)
    cell_draw = jax.random.randint(key_cell, (LINES, SEGS, 2, NBLK), 0, NCELL)
    top_cell = (line_index == 0) & (seg_index == 0) & (side_index == 1) & (block_index == 0)
    cell_draw = jnp.where(top_cell, NCELL - 1, cell_draw)
    cell_ids = jnp.where(live_blocks, cell_draw, -1).astype(jnp.int32)
    fill_count = jax.random.randint(key_fill, (LINES, SEGS, 2, NBLK, 1), 32, BLOCK + 1)
    slot_index = jnp.arange(BLOCK).reshape(1, 1, 1, 1, BLOCK)
    slot_live = (slot_index < fill_count) & live_blocks[..., None]
    row_draw = jax.random.randint(key_rows, (LINES, SEGS, 2, NBLK, BLOCK), 0, margin)
    side_full = jnp.arange(2).reshape(1, 1, 2, 1, 1)
    row_draw = jnp.where(side_full == 1, row_draw + (NPTS - margin), row_draw)
    top_row = top_cell[..., None] & (slot_index == 0)
    row_draw = jnp.where(top_row, NPTS - 1, row_draw)
    row_ids = jnp.where(slot_live, row_draw, -1).reshape(LINES, SEGS, 2, NBLK * BLOCK).astype(jnp.int32)
    return (row_ids, cell_ids)


def draw_rows(key, part):
    return route_tables(key)[0]


def draw_cells(key, part):
    return route_tables(key)[1]


def draw_pose(key, part):
    noise = jax.random.normal(jax.random.fold_in(key, 5), (12, LINES), jnp.float32)
    scales = jnp.array([0.1] * 9 + [0.2] * 3, jnp.float32)[:, None]
    identity = jnp.array([1, 0, 0, 0, 1, 0, 0, 0, 1, 0, 0, 0], jnp.float32)[:, None]
    return identity + scales * noise


def levels(rng, dims, shards, smallest, top_value):
    factor_of, own = 1.0, jax.random.fold_in(rng, 6)
    for position, shards_of in shards:
        draws = jnp.exp(jax.random.uniform(jax.random.fold_in(own, position), (shards_of,), jnp.float32, smallest / len(shards), top_value / len(shards)))
        factor_of = factor_of * jnp.repeat(draws, dims[position] // shards_of).reshape([-1 if axis == position else 1 for axis in range(len(dims))])
    return factor_of


def setup_inputs(seed: int = 0) -> dict:
    streams_of = jax.random.split(jax.random.key(seed), 5)
    points = jnp.clip(jax.random.uniform(streams_of[0], (LINES, SEGS, 3, NPTS), jnp.float32, -1.0, 1.0) * levels(streams_of[0], (LINES, SEGS, 3, NPTS), ((0, 8), (1, 4)), -0.4, 0.0), -1.0, 1.0)
    rows = draw_rows(jax.random.fold_in(streams_of[4], 71), 0)
    cells = draw_cells(jax.random.fold_in(streams_of[4], 71), 0)
    pose = draw_pose(jax.random.fold_in(streams_of[4], 71), 0)
    return dict(points=points, rows=rows, cells=cells, pose=pose)


OUTLIER_MASS = 1.0
SPREAD_START = 0.05
PRIOR_TOP = 0.05
PRIOR_BOTTOM = 1.0
REGULARIZE = 1.0

def match_block(source_block, cell_id, world_points, spread):
    first_column = (jnp.maximum(cell_id, 0) * CT).astype(jnp.int32)
    target = lax.dynamic_slice_in_dim(world_points, first_column, CT, 1)
    distance = (source_block[0][:, None] - target[0][None, :]) ** 2
    distance = distance + (source_block[1][:, None] - target[1][None, :]) ** 2
    distance = distance + (source_block[2][:, None] - target[2][None, :]) ** 2
    weight = jnp.exp(-distance / (2.0 * spread))
    total_weight = jnp.sum(weight, axis=1)
    posterior = weight / (total_weight + OUTLIER_MASS)[:, None]
    pulled = lax.dot_general(target.astype(jnp.float32), posterior.astype(jnp.float32), (((1,), (1,)), ((), ())), precision=lax.Precision.HIGHEST, preferred_element_type=jnp.float32)
    share_row = total_weight / (total_weight + OUTLIER_MASS)
    energy_row = jnp.sum(posterior * distance, axis=1)
    merged_rows = jnp.concatenate([pulled, share_row[None, :], energy_row[None, :]], axis=0)
    return jnp.where(cell_id >= 0, merged_rows, jnp.zeros_like(merged_rows))

def solve_pose(gram_matrix, cross_matrix, pose_column):
    old_pose = jnp.concatenate([pose_column[:9].reshape(3, 3), pose_column[9:].reshape(3, 1)], axis=1)
    left_side = gram_matrix + REGULARIZE * jnp.eye(4, dtype=gram_matrix.dtype)
    right_side = cross_matrix + REGULARIZE * old_pose
    factor = jnp.linalg.cholesky(left_side)
    solved = jax.scipy.linalg.cho_solve((factor, True), right_side.T)
    new_pose = solved.T
    return jnp.concatenate([new_pose[:, :3].reshape(9), new_pose[:, 3]])

def reference(points, rows, cells, pose):
    margin = NCELL * CT
    live_slots = rows >= 0
    safe_rows = jnp.where(live_slots, rows, 0)

    def pick(segment_points, segment_rows):
        taken = jnp.take(segment_points, segment_rows.reshape(-1), axis=1)
        return taken.reshape(3, 2, SLOTS).transpose(1, 0, 2)
    raw_source = jax.vmap(jax.vmap(pick))(points, safe_rows)
    ones_row = jnp.ones(raw_source.shape[:3] + (1,) + raw_source.shape[4:], raw_source.dtype)
    extended = jnp.concatenate([raw_source, ones_row], axis=3)
    spread = jnp.float32(SPREAD_START)
    pose_now = pose
    result = None
    for iteration in range(ITERS):
        linear_part = pose_now[:9].T.reshape(LINES, 3, 3)
        offset_part = pose_now[9:].T
        world_points = jnp.einsum('lkm,lgmn->lgkn', linear_part, points, precision=lax.Precision.HIGHEST) + offset_part[:, None, :, None]
        moved_source = jnp.einsum('lkm,lgdms->lgdks', linear_part, raw_source, precision=lax.Precision.HIGHEST) + offset_part[:, None, None, :, None]

        def device(index):
            line_pos = index // SEGS
            seg_pos = index % SEGS
            lower_line = jnp.maximum(line_pos - 1, 0)
            upper_line = jnp.minimum(line_pos + 1, LINES - 1)
            targets = jnp.stack([world_points[lower_line, seg_pos][:, NPTS - margin:], world_points[upper_line, seg_pos][:, :margin]])
            blocks = moved_source[line_pos, seg_pos].reshape(2, 3, NBLK, BLOCK).transpose(0, 2, 1, 3)
            block_cells = cells[line_pos, seg_pos]

            def direction(target_world, direction_blocks, direction_cells):
                return jax.vmap(lambda block_points, block_cell: match_block(block_points, block_cell, target_world, spread))(direction_blocks, direction_cells)
            output = jax.vmap(direction)(targets, blocks, block_cells)
            return output.transpose(0, 2, 1, 3).reshape(2, 5, SLOTS)
        result = lax.map(device, jnp.arange(LINES * SEGS, dtype=jnp.int32)).reshape(LINES, SEGS, 2, 5, SLOTS)
        result = result * live_slots[:, :, :, None, :].astype(result.dtype)
        pulled = result[:, :, :, :3]
        share_all = result[:, :, :, 3]
        energy_all = result[:, :, :, 4]
        gram_lines = jnp.einsum('lgdks,lgdms->lkm', extended * share_all[:, :, :, None, :], extended, precision=lax.Precision.HIGHEST)
        cross_lines = jnp.einsum('lgdks,lgdms->lkm', pulled, extended, precision=lax.Precision.HIGHEST)
        pose_now = jax.vmap(solve_pose)(gram_lines, cross_lines, pose_now.T).T
        spread = (jnp.sum(energy_all) + PRIOR_TOP) / (3.0 * jnp.sum(share_all) + PRIOR_BOTTOM)
    return (result, pose_now, spread.reshape(1))
```

```python
import functools
import math

import jax
import jax.numpy as jnp
from jax import lax
from jax.experimental import pallas as pl
from jax.experimental.pallas import tpu as pltpu
from jax.sharding import PartitionSpec as P

NCELL = 16
CT = 512
BLOCK = 128
MARGIN = NCELL * CT
MROWS = MARGIN // 128
TILES = CT // 128
GROUPS = BLOCK // 8
UNROLL = 2

OUTLIER_MASS = 1.0
SPREAD_START = 0.05
PRIOR_TOP = 0.05
PRIOR_BOTTOM = 1.0
REGULARIZE = 1.0
LOG2E = math.log2(math.e)

F32 = jnp.float32
TILE = (8, 128)
ONE = 24
SHARE = ONE + 3
ENERGY = ONE + 4
QUAD = 32


def iota(axis):
    return lax.broadcasted_iota(jnp.int32, TILE, axis)


def spread_out(value):
    return jnp.broadcast_to(value, TILE)


def gather_kernel(low_ref, up_ref, rows_ref, source_ref):
    slot_rows = rows_ref.shape[0]
    count = slot_rows // 8
    upward = (iota(0) & 1) == 1
    high, low, live = [], [], []
    for v in range(count):
        row = rows_ref[8 * v : 8 * v + 8, :]
        live.append((row >= 0).astype(F32))
        spot = jnp.maximum(row, 0) & (MARGIN - 1)
        high.append(spot >> 7)
        low.append(spot & 127)

    def step(r, carry):
        table = []
        for k in range(3):
            a = spread_out(low_ref[k, pl.ds(r, 1), :])
            b = spread_out(up_ref[k, pl.ds(r, 1), :])
            table.append(jnp.where(upward, b, a))
        out = []
        for v in range(count):
            hit = high[v] == r
            for k in range(3):
                got = jnp.take_along_axis(table[k], low[v], axis=1, mode="promise_in_bounds")
                out.append(jnp.where(hit, got, carry[3 * v + k]))
        return tuple(out)

    done = lax.fori_loop(0, MROWS, step, tuple(jnp.zeros(TILE, F32) for _ in range(3 * count)), unroll=4)
    for v in range(count):
        for k in range(3):
            source_ref[k, 8 * v : 8 * v + 8, :] = done[3 * v + k]
        source_ref[3, 8 * v : 8 * v + 8, :] = live[v]


def gather(points, rows):
    last = points.shape[1] // MROWS - 1
    slot_rows = rows.shape[0]
    return pl.pallas_call(
        gather_kernel,
        grid=(1,),
        in_specs=[
            pl.BlockSpec((3, MROWS, 128), lambda i: (0, 0, 0)),
            pl.BlockSpec((3, MROWS, 128), lambda i: (0, last, 0)),
            pl.BlockSpec((slot_rows, 128), lambda i: (0, 0)),
        ],
        out_specs=pl.BlockSpec((4, slot_rows, 128), lambda i: (0, 0, 0)),
        out_shape=jax.ShapeDtypeStruct((4, slot_rows, 128), F32),
        name="gather_sources",
    )(points, points, rows)


def apply_pose(coefs, xyz):
    out = []
    for k in range(3):
        total = coefs[3 * k] * xyz[0]
        total = total + coefs[3 * k + 1] * xyz[1]
        total = total + coefs[3 * k + 2] * xyz[2]
        out.append(total + coefs[9 + k])
    return out


def match(own, nbrs, negc, dirs, cells_ref, source_ref, margin_refs, world_ref, moved_ref, column_ref, out_ref):
    slot_rows = source_ref.shape[1]
    for v in range(slot_rows // 8):
        xyz = [source_ref[k, 8 * v : 8 * v + 8, :] for k in range(3)]
        for k, value in enumerate(apply_pose(own, xyz)):
            moved_ref[k, 8 * v : 8 * v + 8, :] = value
    for k in range(3):
        column_ref[k] = jnp.transpose(moved_ref[k])
    for side in range(2):
        for v in range(MROWS // 8):
            xyz = [margin_refs[side][k * MROWS + 8 * v : k * MROWS + 8 * v + 8, :] for k in range(3)]
            for k, value in enumerate(apply_pose(nbrs[side], xyz)):
                world_ref[side, k, 8 * v : 8 * v + 8, :] = value
    lane, sub = iota(1), iota(0)
    if out_ref is not None:
        out_ref[...] = jnp.zeros(out_ref.shape, F32)

    def one_block(side, row, cell):
        first = jnp.maximum(cell, 0) * TILES
        target = [
            [spread_out(world_ref[side, k, pl.ds(first + t, 1), :]) for t in range(TILES)] for k in range(3)
        ]
        pick = jnp.full(TILE, row, jnp.int32)
        parts = []
        for g in range(GROUPS):
            m = [
                jnp.take_along_axis(column_ref[k, 8 * g : 8 * g + 8, :], pick, axis=1, mode="promise_in_bounds")
                for k in range(3)
            ]
            sums = None
            for t in range(TILES):
                d = [m[k] - target[k][t] for k in range(3)]
                dist = d[0] * d[0] + d[1] * d[1] + d[2] * d[2]
                weight = jnp.exp2(dist * negc)
                terms = [weight * target[k][t] for k in range(3)] + [weight, weight * dist]
                sums = terms if sums is None else [a + b for a, b in zip(sums, terms)]
            part = jnp.zeros(TILE, F32)
            for q in range(5):
                part = jnp.where(lane == q, jnp.sum(sums[q], axis=1, keepdims=True), part)
            parts.append(part)
        flat = jnp.transpose(jnp.concatenate(parts, axis=0))[:8, :]
        result = flat * (1.0 / (spread_out(flat[3:4, :]) + OUTLIER_MASS))
        xt = [spread_out(source_ref[k, pl.ds(row, 1), :]) for k in range(4)]
        result = result * xt[3]
        return result, xt

    x_left = (sub < 3).astype(F32)
    y_left = ((sub == 3) | (sub == 4)).astype(F32)
    z_left = (sub == 5).astype(F32)
    x_right = (sub == 0).astype(F32)
    y_right = ((sub == 1) | (sub == 3)).astype(F32)
    z_right = ((sub == 2) | (sub == 4) | (sub == 5)).astype(F32)

    def add_block(carry, side, row, cell):
        result, xt = one_block(side, row, cell)
        if out_ref is not None:
            for q in range(5):
                out_ref[q, pl.ds(row, 1), :] = result[q : q + 1, :]
        factor = (x_left * xt[0] + y_left * xt[1] + z_left * xt[2]) * (
            x_right * xt[0] + y_right * xt[1] + z_right * xt[2]
        )
        share = spread_out(result[3:4, :])
        return (
            carry[0] + result * xt[0],
            carry[1] + result * xt[1],
            carry[2] + result * xt[2],
            carry[3] + result,
            carry[4] + share * factor,
        )

    carry = tuple(jnp.zeros(TILE, F32) for _ in range(5))
    blocks = cells_ref.shape[1]
    for side in range(2):
        d = dirs[side]

        def filled(b, n, d=d):
            return n + (cells_ref[d, b] >= 0).astype(jnp.int32)

        live_blocks = lax.fori_loop(0, blocks, filled, jnp.int32(0))

        def step(i, carry, side=side, d=d):
            for u in range(UNROLL):
                b = i * UNROLL + u
                carry = add_block(carry, side, 2 * b + d, cells_ref[d, b])
            return carry

        carry = lax.fori_loop(0, (live_blocks + UNROLL - 1) // UNROLL, step, carry)
    return carry


def pack_sums(sums, out_ref):
    lane, sub = iota(1), iota(0)
    total = jnp.zeros(TILE, F32)
    for c in range(5):
        total = total + jnp.where(lane == 8 * c + sub, jnp.sum(sums[c], axis=1, keepdims=True), 0.0)
    row = jnp.sum(total, axis=0, keepdims=True)
    out_ref[...] = jnp.broadcast_to(row, out_ref.shape)


def pose_of_row(row):
    return [spread_out(row[:, j : j + 1]) for j in range(12)]


def sides_of(line):
    odd = line & 1
    return [1 - odd, odd]


def first_kernel(cells_ref, pose_ref, source_ref, margin_a, margin_b, sums_ref, world_ref, moved_ref, column_ref):
    line = lax.axis_index("line")
    own = pose_of_row(pose_ref[...])
    nbrs = [pose_of_row(margin[3 * MROWS : 3 * MROWS + 1, :]) for margin in (margin_a, margin_b)]
    negc = F32(-LOG2E / (2.0 * SPREAD_START))
    sums = match(
        own, nbrs, negc, sides_of(line), cells_ref, source_ref, (margin_a, margin_b), world_ref, moved_ref, column_ref, None
    )
    pack_sums(sums, sums_ref)


def solve(totals, old):
    def at(q):
        return spread_out(totals[:, q : q + 1])

    gram = {}
    for n, (a, b) in enumerate([(0, 0), (0, 1), (0, 2), (1, 1), (1, 2), (2, 2)]):
        gram[a, b] = at(QUAD + n)
    for a in range(3):
        gram[a, 3] = at(8 * a + 3)
    gram[3, 3] = at(SHARE)
    for a in range(4):
        gram[a, a] = gram[a, a] + REGULARIZE
    lower, diag, inverse = {}, [], []
    for j in range(4):
        scaled = [lower[j, k] * diag[k] for k in range(j)]
        pivot = gram[j, j]
        for k in range(j):
            pivot = pivot - lower[j, k] * scaled[k]
        diag.append(pivot)
        inverse.append(1.0 / pivot)
        for i in range(j + 1, 4):
            value = gram[j, i]
            for k in range(j):
                value = value - lower[i, k] * scaled[k]
            lower[i, j] = value * inverse[j]
    new = [None] * 12
    for k in range(3):
        right = []
        for m in range(4):
            j = 3 * k + m if m < 3 else 9 + k
            value = at(8 * m + k) + REGULARIZE * spread_out(old[:, j : j + 1])
            for n in range(m):
                value = value - lower[m, n] * right[n]
            right.append(value)
        found = [None] * 4
        for m in reversed(range(4)):
            value = right[m] * inverse[m]
            for n in range(m + 1, 4):
                value = value - lower[n, m] * found[n]
            found[m] = value
        for m in range(4):
            new[3 * k + m if m < 3 else 9 + k] = found[m]
    return new


def line_sum(all_ref, line, segs):
    return jnp.sum(all_ref[pl.ds(line * segs, segs), :], axis=0, keepdims=True)


def new_spread(all_ref):
    everything = jnp.sum(all_ref[...], axis=0, keepdims=True)
    top = spread_out(everything[:, ENERGY : ENERGY + 1]) + PRIOR_TOP
    return top / (3.0 * spread_out(everything[:, SHARE : SHARE + 1]) + PRIOR_BOTTOM)


def pose_row(new, sub):
    lane = iota(1)
    row = jnp.zeros(TILE, F32)
    for j in range(12):
        row = jnp.where(lane == j, spread_out(new[j][sub : sub + 1, :]), row)
    return row


def second_kernel(
    lines, segs, cells_ref, pose_ref, all_ref, source_ref, margin_a, margin_b,
    sums_ref, pose_out_ref, out_ref, world_ref, moved_ref, column_ref,
):
    line = lax.axis_index("line")
    dirs = sides_of(line)
    partner = [jnp.clip(line + 2 * d - 1, 0, lines - 1) for d in dirs]
    sub = iota(0)

    def stacked(a, b, c):
        return jnp.where(sub == 0, spread_out(a), jnp.where(sub == 1, spread_out(b), spread_out(c)))

    totals = stacked(*[line_sum(all_ref, n, segs) for n in (line, partner[0], partner[1])])
    old = stacked(pose_ref[...], margin_a[3 * MROWS : 3 * MROWS + 1, :], margin_b[3 * MROWS : 3 * MROWS + 1, :])
    new = solve(totals, old)
    negc = (-0.5 * LOG2E) / new_spread(all_ref)
    own, near_a, near_b = [[spread_out(value[n : n + 1, :]) for value in new] for n in range(3)]
    pose_out_ref[...] = pose_row(new, 0)[:1, :]
    sums = match(
        own, [near_a, near_b], negc, dirs, cells_ref, source_ref, (margin_a, margin_b), world_ref, moved_ref, column_ref, out_ref
    )
    pack_sums(sums, sums_ref)


def last_kernel(segs, pose_ref, all_ref, fitted_ref, spread_ref):
    line = lax.axis_index("line")
    totals = spread_out(line_sum(all_ref, line, segs))
    new = solve(totals, spread_out(pose_ref[...]))
    fitted_ref[...] = pose_row(new, 0)[:1, :12]
    spread_ref[...] = new_spread(all_ref)[:1, :1]


def vmem(count):
    return [pl.BlockSpec(memory_space=pltpu.VMEM)] * count


SMEM = pl.BlockSpec(memory_space=pltpu.SMEM)
PARAMS = pltpu.CompilerParams(vmem_limit_bytes=32 * 1024 * 1024)


def scratch():
    return [
        pltpu.VMEM((2, 3, MROWS, 128), F32),
        pltpu.VMEM((3, 128, 128), F32),
        pltpu.VMEM((3, 128, 128), F32),
    ]


def exchange(sums):
    return lax.all_to_all(sums, ("line", "seg"), 0, 0)


def on_device(lines, segs, points, rows, cells, pose):
    own_points = points.reshape(3, -1, 128)
    slots = rows.shape[-1]
    blocks = slots // BLOCK
    row_list = rows.reshape(2, blocks, 128).transpose(1, 0, 2).reshape(2 * blocks, 128)
    cell_ids = cells.reshape(2, blocks)
    devices = lines * segs
    odd = lax.axis_index("line") & 1
    tail = own_points.shape[1] - MROWS
    pose_line = jnp.pad(pose.reshape(1, 12), ((0, 0), (0, 116)))
    pose_tile = jnp.pad(pose_line, ((0, 7), (0, 0)))

    def margin_at(first):
        part = lax.dynamic_slice_in_dim(own_points, first, MROWS, 1)
        return jnp.concatenate([part.reshape(3 * MROWS, 128), pose_tile], axis=0)

    pairs_a = [(i, i ^ 1) for i in range(lines) if i ^ 1 < lines]
    pairs_b = [(i, ((i + 1) ^ 1) - 1) for i in range(lines)]
    pairs_b = [(i, j) for i, j in pairs_b if 0 <= j < lines]
    margin_a = lax.ppermute(margin_at(jnp.where(odd == 1, 0, tail)), "line", pairs_a)
    margin_b = lax.ppermute(margin_at(jnp.where(odd == 1, tail, 0)), "line", pairs_b)
    source = gather(own_points, row_list)
    sums_shape = jax.ShapeDtypeStruct((devices, 128), F32)
    pair_ops = 2 * blocks * BLOCK * CT
    cost = pl.CostEstimate(flops=18 * pair_ops, bytes_accessed=1 << 20, transcendentals=pair_ops)
    sums = pl.pallas_call(
        first_kernel,
        in_specs=[SMEM] + vmem(4),
        out_specs=vmem(1)[0],
        out_shape=sums_shape,
        scratch_shapes=scratch(),
        compiler_params=PARAMS,
        cost_estimate=cost,
        name="match_first",
    )(cell_ids, pose_line, source, margin_a, margin_b)
    everyone = exchange(sums)
    sums, pose_line, result = pl.pallas_call(
        functools.partial(second_kernel, lines, segs),
        in_specs=[SMEM] + vmem(5),
        out_specs=vmem(3),
        out_shape=[
            sums_shape,
            jax.ShapeDtypeStruct((1, 128), F32),
            jax.ShapeDtypeStruct((5, 2 * blocks, 128), F32),
        ],
        scratch_shapes=scratch(),
        compiler_params=PARAMS,
        cost_estimate=cost,
        name="match_second",
    )(cell_ids, pose_line, everyone, source, margin_a, margin_b)
    everyone = exchange(sums)
    fitted, spread = pl.pallas_call(
        functools.partial(last_kernel, segs),
        in_specs=vmem(2),
        out_specs=vmem(2),
        out_shape=[jax.ShapeDtypeStruct((1, 12), F32), jax.ShapeDtypeStruct((1, 1), F32)],
        name="solve_last",
    )(pose_line, everyone)
    result = result.reshape(5, blocks, 2, 128).transpose(2, 0, 1, 3).reshape(1, 1, 2, 5, slots)
    return (result, fitted.reshape(12, 1), spread.reshape(1))


def solution(mesh):
    return jax.shard_map(
        functools.partial(on_device, mesh.shape["line"], mesh.shape["seg"]),
        mesh=mesh,
        in_specs=(
            P("line", "seg", None, None),
            P("line", "seg", None, None),
            P("line", "seg", None, None),
            P(None, "line"),
        ),
        out_specs=(P("line", "seg", None, None, None), P(None, "line"), P()),
        check_vma=False,
    )
```

```python
import functools
import math

import jax
import jax.numpy as jnp
from jax import lax
from jax.experimental import pallas as pl
from jax.experimental.pallas import tpu as pltpu
from jax.sharding import PartitionSpec as P

NCELL = 16
CT = 512
BLOCK = 128
MARGIN = NCELL * CT
MROWS = MARGIN // 128
TILES = CT // 128
GROUPS = BLOCK // 8
UNROLL = 8
QUICK_LIMIT = 1000.0

OUTLIER_MASS = 1.0
SPREAD_START = 0.05
PRIOR_TOP = 0.05
PRIOR_BOTTOM = 1.0
REGULARIZE = 1.0
LOG2E = math.log2(math.e)

F32 = jnp.float32
BF16 = jnp.bfloat16
TILE = (8, 128)
ONE = 24
SHARE = ONE + 3
ENERGY = ONE + 4
QUAD = 32


def iota(axis):
    return lax.broadcasted_iota(jnp.int32, TILE, axis)


def spread_out(value):
    return jnp.broadcast_to(value, TILE)


def gather_kernel(low_ref, up_ref, rows_ref, source_ref):
    slot_rows = rows_ref.shape[0]
    count = slot_rows // 8
    upward = (iota(0) & 1) == 1
    high, low, live = [], [], []
    for v in range(count):
        row = rows_ref[8 * v : 8 * v + 8, :]
        live.append((row >= 0).astype(F32))
        spot = jnp.maximum(row, 0) & (MARGIN - 1)
        high.append(spot >> 7)
        low.append(spot & 127)

    def step(r, carry):
        table = []
        for k in range(3):
            a = spread_out(low_ref[k, pl.ds(r, 1), :])
            b = spread_out(up_ref[k, pl.ds(r, 1), :])
            table.append(jnp.where(upward, b, a))
        out = []
        for v in range(count):
            hit = high[v] == r
            for k in range(3):
                got = jnp.take_along_axis(table[k], low[v], axis=1, mode="promise_in_bounds")
                out.append(jnp.where(hit, got, carry[3 * v + k]))
        return tuple(out)

    done = lax.fori_loop(0, MROWS, step, tuple(jnp.zeros(TILE, F32) for _ in range(3 * count)), unroll=4)
    for v in range(count):
        for k in range(3):
            source_ref[k, 8 * v : 8 * v + 8, :] = done[3 * v + k]
        source_ref[3, 8 * v : 8 * v + 8, :] = live[v]


def gather(points, rows):
    last = points.shape[1] // MROWS - 1
    slot_rows = rows.shape[0]
    return pl.pallas_call(
        gather_kernel,
        grid=(1,),
        in_specs=[
            pl.BlockSpec((3, MROWS, 128), lambda i: (0, 0, 0)),
            pl.BlockSpec((3, MROWS, 128), lambda i: (0, last, 0)),
            pl.BlockSpec((slot_rows, 128), lambda i: (0, 0)),
        ],
        out_specs=pl.BlockSpec((4, slot_rows, 128), lambda i: (0, 0, 0)),
        out_shape=jax.ShapeDtypeStruct((4, slot_rows, 128), F32),
        name="gather_sources",
    )(points, points, rows)


def apply_pose(coefs, xyz):
    out = []
    for k in range(3):
        total = coefs[3 * k] * xyz[0]
        total = total + coefs[3 * k + 1] * xyz[1]
        total = total + coefs[3 * k + 2] * xyz[2]
        out.append(total + coefs[9 + k])
    return out


def column(coefs, first, stride):
    sub = iota(0)
    out = jnp.zeros(TILE, F32)
    for k in range(3):
        out = jnp.where(sub == k, coefs[first + stride * k], out)
    return out


def columns(coefs):
    return [column(coefs, k, 3) for k in range(3)] + [column(coefs, 9, 1)]


def squared_length(value):
    square = value * value
    return spread_out(square[0:1, :]) + spread_out(square[1:2, :]) + spread_out(square[2:3, :])


def three_parts(value):
    high = value.astype(BF16).astype(F32)
    rest = value - high
    middle = rest.astype(BF16).astype(F32)
    return high, middle, rest - middle


def combine(cols, xyz):
    return cols[0] * xyz[0] + cols[1] * xyz[1] + cols[2] * xyz[2]


def prepare(near, margin_refs, phi_ref):
    sub = iota(0)

    def step(r, longest):
        for side in range(2):
            xyz = [spread_out(margin_refs[side][pl.ds(k * MROWS + r, 1), :]) for k in range(3)]
            y = combine(near[side], xyz)
            length = squared_length(y)
            longest = jnp.maximum(longest, length)
            high, middle, low = three_parts(jnp.where(sub == 3, length, jnp.where(sub == 4, 1.0, y)))
            spot = pl.ds(pl.multiple_of(r * 128, 128), 128)
            for i, pair in enumerate(((high, middle), (low, high), (middle, high))):
                phi_ref[side, 16 * i : 16 * i + 16, spot] = jnp.concatenate(pair, axis=0).astype(BF16)
        return longest

    return lax.fori_loop(0, MROWS, step, jnp.zeros(TILE, F32), unroll=4)


def longest_source(own, near, dirs, source_ref):
    longest = jnp.zeros(TILE, F32)
    for v in range(source_ref.shape[1] // 8):
        rows = slice(8 * v, 8 * v + 8)
        xyz = [source_ref[k, rows, :] for k in range(3)]
        moved = apply_pose(own, xyz)
        for side in range(2):
            square = sum((moved[k] - near[side][9 + k]) ** 2 for k in range(3))
            listed = (iota(0) & 1) == dirs[side]
            longest = jnp.maximum(longest, jnp.where(listed, square * source_ref[3, rows, :], 0.0))
    return longest


def quick_block(negc, exact, own, near, phi_ref, source_ref, side, row, cell):
    sub = iota(0)
    xt = [spread_out(source_ref[k, pl.ds(row, 1), :]) for k in range(4)]
    m = combine(own, xt) + (own[3] - near[side][3])
    length = squared_length(m)
    coef = jnp.where(sub == 3, negc, jnp.where(sub == 4, negc * length, (-2.0 * negc) * m))
    high, middle, low = three_parts(coef)
    stack = jnp.concatenate([high, high, high, middle, middle, low], axis=0)
    phi = phi_ref[side, :, pl.ds(pl.multiple_of(jnp.maximum(cell, 0) * CT, CT), CT)]
    power = jnp.dot(jnp.transpose(stack).astype(BF16), phi, preferred_element_type=F32)
    weight = jnp.exp2(power)
    top = weight.astype(BF16)
    last = (((1,), (1,)), ((), ()))
    sums = lax.dot_general(phi[:32], top, last, preferred_element_type=F32)
    if exact:
        rest = (weight - top.astype(F32)).astype(BF16)
        sums = sums + lax.dot_general(phi[:32], rest, last, preferred_element_type=F32)
    sums = sums[0:8] + sums[8:16] + sums[16:24]
    total = spread_out(sums[4:5, :])
    around = combine([spread_out(m[k : k + 1, :]) for k in range(3)], [spread_out(sums[k : k + 1, :]) for k in range(3)])
    energy = spread_out(sums[3:4, :]) - 2.0 * around + length * total
    raw = jnp.where(sub < 3, sums + near[side][3] * total, jnp.where(sub == 3, total, jnp.where(sub == 4, energy, 0.0)))
    return raw * (xt[3] / (total + OUTLIER_MASS)), xt


def match(exact, own, nbrs, negc, dirs, cells_ref, source_ref, margin_refs, scratch_refs, out_ref):
    phi_ref, sums_ref, world_ref, moved_ref, column_ref = scratch_refs
    own_cols, near_cols = columns(own), [columns(near) for near in nbrs]
    size = prepare(near_cols, margin_refs, phi_ref) + longest_source(own, nbrs, dirs, source_ref)
    quick = jnp.max(size * -negc) <= QUICK_LIMIT
    if out_ref is not None:
        out_ref[...] = jnp.zeros(out_ref.shape, F32)

    @pl.when(quick)
    def _():
        def block(side, row, cell):
            return quick_block(negc, exact, own_cols, near_cols, phi_ref, source_ref, side, row, cell)

        run_blocks(block, UNROLL, dirs, cells_ref, sums_ref, out_ref)

    @pl.when(jnp.logical_not(quick))
    def _():
        block = careful_setup(own, nbrs, negc, source_ref, margin_refs, world_ref, moved_ref, column_ref)
        run_blocks(block, 1, dirs, cells_ref, sums_ref, out_ref)

    return [sums_ref[n] for n in range(5)]


def run_blocks(one_block, unroll, dirs, cells_ref, sums_ref, out_ref):
    sub = iota(0)
    x_left = (sub < 3).astype(F32)
    y_left = ((sub == 3) | (sub == 4)).astype(F32)
    z_left = (sub == 5).astype(F32)
    x_right = (sub == 0).astype(F32)
    y_right = ((sub == 1) | (sub == 3)).astype(F32)
    z_right = ((sub == 2) | (sub == 4) | (sub == 5)).astype(F32)

    def add_block(carry, row, result, xt):
        if out_ref is not None:
            for q in range(5):
                out_ref[q, pl.ds(row, 1), :] = result[q : q + 1, :]
        factor = combine([x_left, y_left, z_left], xt) * combine([x_right, y_right, z_right], xt)
        share = spread_out(result[3:4, :])
        return (
            carry[0] + result * xt[0],
            carry[1] + result * xt[1],
            carry[2] + result * xt[2],
            carry[3] + result,
            carry[4] + share * factor,
        )

    carry = tuple(jnp.zeros(TILE, F32) for _ in range(5))
    blocks = cells_ref.shape[1]
    for side in range(2):
        d = dirs[side]

        def filled(b, n, d=d):
            return n + (cells_ref[d, b] >= 0).astype(jnp.int32)

        live_blocks = lax.fori_loop(0, blocks, filled, jnp.int32(0))

        def step(i, carry, side=side, d=d):
            places = [i * unroll + u for u in range(unroll)]
            found = [one_block(side, 2 * b + d, cells_ref[d, b]) for b in places]
            for b, (result, xt) in zip(places, found):
                carry = add_block(carry, 2 * b + d, result, xt)
            return carry

        carry = lax.fori_loop(0, (live_blocks + unroll - 1) // unroll, step, carry)
    for n in range(5):
        sums_ref[n] = carry[n]


def careful_setup(own, nbrs, negc, source_ref, margin_refs, world_ref, moved_ref, column_ref):
    slot_rows = source_ref.shape[1]
    for v in range(slot_rows // 8):
        xyz = [source_ref[k, 8 * v : 8 * v + 8, :] for k in range(3)]
        for k, value in enumerate(apply_pose(own, xyz)):
            moved_ref[k, 8 * v : 8 * v + 8, :] = value
    for k in range(3):
        column_ref[k] = jnp.transpose(moved_ref[k])
    for side in range(2):
        for v in range(MROWS // 8):
            xyz = [margin_refs[side][k * MROWS + 8 * v : k * MROWS + 8 * v + 8, :] for k in range(3)]
            for k, value in enumerate(apply_pose(nbrs[side], xyz)):
                world_ref[side, k, 8 * v : 8 * v + 8, :] = value
    lane = iota(1)

    def one_block(side, row, cell):
        first = jnp.maximum(cell, 0) * TILES
        target = [
            [spread_out(world_ref[side, k, pl.ds(first + t, 1), :]) for t in range(TILES)] for k in range(3)
        ]
        pick = jnp.full(TILE, row, jnp.int32)
        parts = []
        for g in range(GROUPS):
            m = [
                jnp.take_along_axis(column_ref[k, 8 * g : 8 * g + 8, :], pick, axis=1, mode="promise_in_bounds")
                for k in range(3)
            ]
            sums = None
            for t in range(TILES):
                d = [m[k] - target[k][t] for k in range(3)]
                dist = d[0] * d[0] + d[1] * d[1] + d[2] * d[2]
                weight = jnp.exp2(dist * negc)
                terms = [weight * target[k][t] for k in range(3)] + [weight, weight * dist]
                sums = terms if sums is None else [a + b for a, b in zip(sums, terms)]
            part = jnp.zeros(TILE, F32)
            for q in range(5):
                part = jnp.where(lane == q, jnp.sum(sums[q], axis=1, keepdims=True), part)
            parts.append(part)
        flat = jnp.transpose(jnp.concatenate(parts, axis=0))[:8, :]
        xt = [spread_out(source_ref[k, pl.ds(row, 1), :]) for k in range(4)]
        return flat * (xt[3] / (spread_out(flat[3:4, :]) + OUTLIER_MASS)), xt

    return one_block


def pack_sums(sums, out_ref):
    lane, sub = iota(1), iota(0)
    total = jnp.zeros(TILE, F32)
    for c in range(5):
        total = total + jnp.where(lane == 8 * c + sub, jnp.sum(sums[c], axis=1, keepdims=True), 0.0)
    row = jnp.sum(total, axis=0, keepdims=True)
    out_ref[...] = jnp.broadcast_to(row, out_ref.shape)


def pose_of_row(row):
    return [spread_out(row[:, j : j + 1]) for j in range(12)]


def sides_of(line):
    odd = line & 1
    return [1 - odd, odd]


def first_kernel(cells_ref, pose_ref, source_ref, margin_a, margin_b, sums_ref, *scratch_refs):
    line = lax.axis_index("line")
    own = pose_of_row(pose_ref[...])
    nbrs = [pose_of_row(margin[3 * MROWS : 3 * MROWS + 1, :]) for margin in (margin_a, margin_b)]
    negc = jnp.full(TILE, -LOG2E / (2.0 * SPREAD_START), F32)
    sums = match(
        False, own, nbrs, negc, sides_of(line), cells_ref, source_ref, (margin_a, margin_b), scratch_refs, None
    )
    pack_sums(sums, sums_ref)


def solve(totals, old):
    def at(q):
        return spread_out(totals[:, q : q + 1])

    gram = {}
    for n, (a, b) in enumerate([(0, 0), (0, 1), (0, 2), (1, 1), (1, 2), (2, 2)]):
        gram[a, b] = at(QUAD + n)
    for a in range(3):
        gram[a, 3] = at(8 * a + 3)
    gram[3, 3] = at(SHARE)
    for a in range(4):
        gram[a, a] = gram[a, a] + REGULARIZE
    lower, diag, inverse = {}, [], []
    for j in range(4):
        scaled = [lower[j, k] * diag[k] for k in range(j)]
        pivot = gram[j, j]
        for k in range(j):
            pivot = pivot - lower[j, k] * scaled[k]
        diag.append(pivot)
        inverse.append(1.0 / pivot)
        for i in range(j + 1, 4):
            value = gram[j, i]
            for k in range(j):
                value = value - lower[i, k] * scaled[k]
            lower[i, j] = value * inverse[j]
    new = [None] * 12
    for k in range(3):
        right = []
        for m in range(4):
            j = 3 * k + m if m < 3 else 9 + k
            value = at(8 * m + k) + REGULARIZE * spread_out(old[:, j : j + 1])
            for n in range(m):
                value = value - lower[m, n] * right[n]
            right.append(value)
        found = [None] * 4
        for m in reversed(range(4)):
            value = right[m] * inverse[m]
            for n in range(m + 1, 4):
                value = value - lower[n, m] * found[n]
            found[m] = value
        for m in range(4):
            new[3 * k + m if m < 3 else 9 + k] = found[m]
    return new


def line_sum(all_ref, line, segs):
    return jnp.sum(all_ref[pl.ds(line * segs, segs), :], axis=0, keepdims=True)


def new_spread(all_ref):
    everything = jnp.sum(all_ref[...], axis=0, keepdims=True)
    top = spread_out(everything[:, ENERGY : ENERGY + 1]) + PRIOR_TOP
    return top / (3.0 * spread_out(everything[:, SHARE : SHARE + 1]) + PRIOR_BOTTOM)


def pose_row(new, sub):
    lane = iota(1)
    row = jnp.zeros(TILE, F32)
    for j in range(12):
        row = jnp.where(lane == j, spread_out(new[j][sub : sub + 1, :]), row)
    return row


def second_kernel(
    lines, segs, cells_ref, pose_ref, all_ref, source_ref, margin_a, margin_b,
    sums_ref, pose_out_ref, out_ref, *scratch_refs,
):
    line = lax.axis_index("line")
    dirs = sides_of(line)
    partner = [jnp.clip(line + 2 * d - 1, 0, lines - 1) for d in dirs]
    sub = iota(0)

    def stacked(a, b, c):
        return jnp.where(sub == 0, spread_out(a), jnp.where(sub == 1, spread_out(b), spread_out(c)))

    totals = stacked(*[line_sum(all_ref, n, segs) for n in (line, partner[0], partner[1])])
    old = stacked(pose_ref[...], margin_a[3 * MROWS : 3 * MROWS + 1, :], margin_b[3 * MROWS : 3 * MROWS + 1, :])
    new = solve(totals, old)
    negc = (-0.5 * LOG2E) / new_spread(all_ref)
    own, near_a, near_b = [[spread_out(value[n : n + 1, :]) for value in new] for n in range(3)]
    pose_out_ref[...] = pose_row(new, 0)[:1, :]
    sums = match(
        True, own, [near_a, near_b], negc, dirs, cells_ref, source_ref, (margin_a, margin_b), scratch_refs, out_ref
    )
    pack_sums(sums, sums_ref)


def last_kernel(segs, pose_ref, all_ref, fitted_ref, spread_ref):
    line = lax.axis_index("line")
    totals = spread_out(line_sum(all_ref, line, segs))
    new = solve(totals, spread_out(pose_ref[...]))
    fitted_ref[...] = pose_row(new, 0)[:1, :12]
    spread_ref[...] = new_spread(all_ref)[:1, :1]


def vmem(count):
    return [pl.BlockSpec(memory_space=pltpu.VMEM)] * count


SMEM = pl.BlockSpec(memory_space=pltpu.SMEM)
PARAMS = pltpu.CompilerParams(vmem_limit_bytes=32 * 1024 * 1024)


def scratch():
    return [
        pltpu.VMEM((2, 48, MARGIN), BF16),
        pltpu.VMEM((5, 8, 128), F32),
        pltpu.VMEM((2, 3, MROWS, 128), F32),
        pltpu.VMEM((3, 128, 128), F32),
        pltpu.VMEM((3, 128, 128), F32),
    ]


def exchange(sums):
    return lax.all_to_all(sums, ("line", "seg"), 0, 0)


def on_device(lines, segs, points, rows, cells, pose):
    own_points = points.reshape(3, -1, 128)
    slots = rows.shape[-1]
    blocks = slots // BLOCK
    row_list = rows.reshape(2, blocks, 128).transpose(1, 0, 2).reshape(2 * blocks, 128)
    cell_ids = cells.reshape(2, blocks)
    devices = lines * segs
    odd = lax.axis_index("line") & 1
    tail = own_points.shape[1] - MROWS
    pose_line = jnp.pad(pose.reshape(1, 12), ((0, 0), (0, 116)))
    pose_tile = jnp.pad(pose_line, ((0, 7), (0, 0)))

    def margin_at(first):
        part = lax.dynamic_slice_in_dim(own_points, first, MROWS, 1)
        return jnp.concatenate([part.reshape(3 * MROWS, 128), pose_tile], axis=0)

    pairs_a = [(i, i ^ 1) for i in range(lines) if i ^ 1 < lines]
    pairs_b = [(i, ((i + 1) ^ 1) - 1) for i in range(lines)]
    pairs_b = [(i, j) for i, j in pairs_b if 0 <= j < lines]
    margin_a = lax.ppermute(margin_at(jnp.where(odd == 1, 0, tail)), "line", pairs_a)
    margin_b = lax.ppermute(margin_at(jnp.where(odd == 1, tail, 0)), "line", pairs_b)
    source = gather(own_points, row_list)
    sums_shape = jax.ShapeDtypeStruct((devices, 128), F32)
    pair_ops = 2 * blocks * BLOCK * CT
    cost = pl.CostEstimate(flops=18 * pair_ops, bytes_accessed=1 << 20, transcendentals=pair_ops)
    sums = pl.pallas_call(
        first_kernel,
        in_specs=[SMEM] + vmem(4),
        out_specs=vmem(1)[0],
        out_shape=sums_shape,
        scratch_shapes=scratch(),
        compiler_params=PARAMS,
        cost_estimate=cost,
        name="match_first",
    )(cell_ids, pose_line, source, margin_a, margin_b)
    everyone = exchange(sums)
    sums, pose_line, result = pl.pallas_call(
        functools.partial(second_kernel, lines, segs),
        in_specs=[SMEM] + vmem(5),
        out_specs=vmem(3),
        out_shape=[
            sums_shape,
            jax.ShapeDtypeStruct((1, 128), F32),
            jax.ShapeDtypeStruct((5, 2 * blocks, 128), F32),
        ],
        scratch_shapes=scratch(),
        compiler_params=PARAMS,
        cost_estimate=cost,
        name="match_second",
    )(cell_ids, pose_line, everyone, source, margin_a, margin_b)
    everyone = exchange(sums)
    fitted, spread = pl.pallas_call(
        functools.partial(last_kernel, segs),
        in_specs=vmem(2),
        out_specs=vmem(2),
        out_shape=[jax.ShapeDtypeStruct((1, 12), F32), jax.ShapeDtypeStruct((1, 1), F32)],
        name="solve_last",
    )(pose_line, everyone)
    result = result.reshape(5, blocks, 2, 128).transpose(2, 0, 1, 3).reshape(1, 1, 2, 5, slots)
    return (result, fitted.reshape(12, 1), spread.reshape(1))


def solution(mesh):
    return jax.shard_map(
        functools.partial(on_device, mesh.shape["line"], mesh.shape["seg"]),
        mesh=mesh,
        in_specs=(
            P("line", "seg", None, None),
            P("line", "seg", None, None),
            P("line", "seg", None, None),
            P(None, "line"),
        ),
        out_specs=(P("line", "seg", None, None, None), P(None, "line"), P()),
        check_vma=False,
    )
```

```python
import functools
import math

import jax
import jax.numpy as jnp
from jax import lax
from jax.experimental import pallas as pl
from jax.experimental.pallas import tpu as pltpu
from jax.sharding import PartitionSpec as P

NCELL = 16
CT = 512
BLOCK = 128
MARGIN = NCELL * CT
MROWS = MARGIN // 128
TILES = CT // 128
GROUPS = BLOCK // 8
UNROLL = 48
QUICK_LIMIT = 1000.0
ENERGY_LIMIT = 400.0

OUTLIER_MASS = 1.0
SPREAD_START = 0.05
PRIOR_TOP = 0.05
PRIOR_BOTTOM = 1.0
REGULARIZE = 1.0
LOG2E = math.log2(math.e)

F32 = jnp.float32
BF16 = jnp.bfloat16
TILE = (8, 128)
ONE = 24
SHARE = ONE + 3
ENERGY = ONE + 4
QUAD = 32


def iota(axis):
    return lax.broadcasted_iota(jnp.int32, TILE, axis)


def spread_out(value):
    return jnp.broadcast_to(value, TILE)


def gather_kernel(low_ref, up_ref, rows_ref, source_ref):
    slot_rows = rows_ref.shape[0]
    count = slot_rows // 8
    upward = (iota(0) & 1) == 1
    high, low, live = [], [], []
    for v in range(count):
        row = rows_ref[8 * v : 8 * v + 8, :]
        live.append((row >= 0).astype(F32))
        spot = jnp.maximum(row, 0) & (MARGIN - 1)
        high.append(spot >> 7)
        low.append(spot & 127)

    def step(r, carry):
        table = []
        for k in range(3):
            a = spread_out(low_ref[k, pl.ds(r, 1), :])
            b = spread_out(up_ref[k, pl.ds(r, 1), :])
            table.append(jnp.where(upward, b, a))
        out = []
        for v in range(count):
            hit = high[v] == r
            for k in range(3):
                got = jnp.take_along_axis(table[k], low[v], axis=1, mode="promise_in_bounds")
                out.append(jnp.where(hit, got, carry[3 * v + k]))
        return tuple(out)

    done = lax.fori_loop(0, MROWS, step, tuple(jnp.zeros(TILE, F32) for _ in range(3 * count)), unroll=4)
    for v in range(count):
        for k in range(3):
            source_ref[k, 8 * v : 8 * v + 8, :] = done[3 * v + k]
        source_ref[3, 8 * v : 8 * v + 8, :] = live[v]


def gather(points, rows):
    last = points.shape[1] // MROWS - 1
    slot_rows = rows.shape[0]
    return pl.pallas_call(
        gather_kernel,
        grid=(1,),
        in_specs=[
            pl.BlockSpec((3, MROWS, 128), lambda i: (0, 0, 0)),
            pl.BlockSpec((3, MROWS, 128), lambda i: (0, last, 0)),
            pl.BlockSpec((slot_rows, 128), lambda i: (0, 0)),
        ],
        out_specs=pl.BlockSpec((4, slot_rows, 128), lambda i: (0, 0, 0)),
        out_shape=jax.ShapeDtypeStruct((4, slot_rows, 128), F32),
        name="gather_sources",
    )(points, points, rows)


def apply_pose(coefs, xyz):
    out = []
    for k in range(3):
        total = coefs[3 * k] * xyz[0]
        total = total + coefs[3 * k + 1] * xyz[1]
        total = total + coefs[3 * k + 2] * xyz[2]
        out.append(total + coefs[9 + k])
    return out


def column(coefs, first, stride):
    sub = iota(0)
    out = jnp.zeros(TILE, F32)
    for k in range(3):
        out = jnp.where(sub == k, coefs[first + stride * k], out)
    return out


def columns(coefs):
    return [column(coefs, k, 3) for k in range(3)] + [column(coefs, 9, 1)]


def squared_length(value):
    square = value * value
    return spread_out(square[0:1, :]) + spread_out(square[1:2, :]) + spread_out(square[2:3, :])


def three_parts(value):
    high = value.astype(BF16).astype(F32)
    rest = value - high
    middle = rest.astype(BF16).astype(F32)
    return high, middle, rest - middle


def combine(cols, xyz):
    return cols[0] * xyz[0] + cols[1] * xyz[1] + cols[2] * xyz[2]


def prepare(near, margin_refs, phi_ref):
    sub = iota(0)

    def step(r, longest):
        for side in range(2):
            xyz = [spread_out(margin_refs[side][pl.ds(k * MROWS + r, 1), :]) for k in range(3)]
            y = combine(near[side], xyz)
            length = squared_length(y)
            longest = jnp.maximum(longest, length)
            high, middle, low = three_parts(jnp.where(sub == 3, length, jnp.where(sub == 4, 1.0, y)))
            spot = pl.ds(pl.multiple_of(r * 128, 128), 128)
            for i, pair in enumerate(((high, middle), (low, high), (middle, high))):
                phi_ref[side, 16 * i : 16 * i + 16, spot] = jnp.concatenate(pair, axis=0).astype(BF16)
        return longest

    return lax.fori_loop(0, MROWS, step, jnp.zeros(TILE, F32), unroll=4)


def longest_source(own, near, dirs, source_ref):
    longest = jnp.zeros(TILE, F32)
    for v in range(source_ref.shape[1] // 8):
        rows = slice(8 * v, 8 * v + 8)
        xyz = [source_ref[k, rows, :] for k in range(3)]
        moved = apply_pose(own, xyz)
        for side in range(2):
            square = sum((moved[k] - near[side][9 + k]) ** 2 for k in range(3))
            listed = (iota(0) & 1) == dirs[side]
            longest = jnp.maximum(longest, jnp.where(listed, square * source_ref[3, rows, :], 0.0))
    return longest


def weigh(negc, own, near, phi_ref, source_ref, side, row, cell):
    sub = iota(0)
    xt = [spread_out(source_ref[k, pl.ds(row, 1), :]) for k in range(4)]
    m = combine(own, xt) + (own[3] - near[side][3])
    length = squared_length(m)
    coef = jnp.where(sub == 3, negc, jnp.where(sub == 4, negc * length, (-2.0 * negc) * m))
    high, middle, low = three_parts(coef)
    stack = jnp.concatenate([high, high, high, middle, middle, low], axis=0)
    spot = pl.ds(pl.multiple_of(jnp.maximum(cell, 0) * CT, CT), CT)
    power = jnp.dot(jnp.transpose(stack).astype(BF16), phi_ref[side, :, spot], preferred_element_type=F32)
    weight = jnp.exp2(power)
    top = weight.astype(BF16)
    rest = (weight - top.astype(F32)).astype(BF16)
    return xt, m, length, spot, top, rest


def weighted_sums(phi_ref, side, spot, top, rest):
    last = (((1,), (1,)), ((), ()))
    features = phi_ref[side, :32, spot]
    sums = lax.dot_general(features, top, last, preferred_element_type=F32)
    sums = sums + lax.dot_general(features, rest, last, preferred_element_type=F32)
    return sums[0:8] + sums[8:16] + sums[16:24]


def finish(near, side, xt, m, length, sums):
    sub = iota(0)
    total = spread_out(sums[4:5, :])
    around = combine([spread_out(m[k : k + 1, :]) for k in range(3)], [spread_out(sums[k : k + 1, :]) for k in range(3)])
    energy = spread_out(sums[3:4, :]) - 2.0 * around + length * total
    raw = jnp.where(sub < 3, sums + near[side][3] * total, jnp.where(sub == 3, total, jnp.where(sub == 4, energy, 0.0)))
    return raw * (xt[3] / (total + OUTLIER_MASS)), xt


def quick_blocks(negc, own, near, phi_ref, source_ref, places):
    ahead = weigh(negc, own, near, phi_ref, source_ref, *places[0])
    found = []
    for n, (side, _, _) in enumerate(places):
        xt, m, length, spot, top, rest = ahead
        if n + 1 < len(places):
            ahead = weigh(negc, own, near, phi_ref, source_ref, *places[n + 1])
        found.append(finish(near, side, xt, m, length, weighted_sums(phi_ref, side, spot, top, rest)))
    return found


def match(own, nbrs, negc, dirs, cells_ref, source_ref, margin_refs, scratch_refs, out_ref):
    phi_ref, sums_ref, world_ref, moved_ref, column_ref = scratch_refs
    blocks = cells_ref.shape[1]
    own_cols, near_cols = columns(own), [columns(near) for near in nbrs]
    size = prepare(near_cols, margin_refs, phi_ref) + longest_source(own, nbrs, dirs, source_ref)
    places = [(side, 2 * b + dirs[side], cells_ref[dirs[side], b]) for side in range(2) for b in range(blocks)]
    carry = [jnp.zeros(TILE, F32) for _ in range(5)]
    for first in range(0, len(places), UNROLL):
        chosen = places[first : first + UNROLL]
        found = quick_blocks(negc, own_cols, near_cols, phi_ref, source_ref, chosen)
        for (_, row, _), (result, xt) in zip(chosen, found):
            carry = add_block(carry, row, result, xt, out_ref)
    for n in range(5):
        sums_ref[n] = carry[n]
    share, energy = [jnp.sum(carry[3][q : q + 1, :]) for q in (3, 4)]
    longest = jnp.max(size)
    bad = (jnp.max(size * -negc) > QUICK_LIMIT) | (longest * share > ENERGY_LIMIT * energy)

    @pl.when(bad)
    def _():
        one_block = careful_setup(own, nbrs, negc, source_ref, margin_refs, world_ref, moved_ref, column_ref)
        carry = tuple(jnp.zeros(TILE, F32) for _ in range(5))
        for side in range(2):
            d = dirs[side]

            def step(b, carry, side=side, d=d):
                result, xt = one_block(side, 2 * b + d, cells_ref[d, b])
                return tuple(add_block(carry, 2 * b + d, result, xt, out_ref))

            carry = lax.fori_loop(0, blocks, step, carry)
        for n in range(5):
            sums_ref[n] = carry[n]

    return [sums_ref[n] for n in range(5)]


def add_block(carry, row, result, xt, out_ref):
    sub = iota(0)
    if out_ref is not None:
        for q in range(5):
            out_ref[q, pl.ds(row, 1), :] = result[q : q + 1, :]
    left = jnp.where(sub < 3, xt[0], jnp.where(sub < 5, xt[1], xt[2]))
    right = jnp.where(sub == 0, xt[0], jnp.where((sub == 1) | (sub == 3), xt[1], xt[2]))
    share = spread_out(result[3:4, :])
    return [
        carry[0] + result * xt[0],
        carry[1] + result * xt[1],
        carry[2] + result * xt[2],
        carry[3] + result,
        carry[4] + share * (left * right),
    ]


def careful_setup(own, nbrs, negc, source_ref, margin_refs, world_ref, moved_ref, column_ref):
    slot_rows = source_ref.shape[1]
    for v in range(slot_rows // 8):
        xyz = [source_ref[k, 8 * v : 8 * v + 8, :] for k in range(3)]
        for k, value in enumerate(apply_pose(own, xyz)):
            moved_ref[k, 8 * v : 8 * v + 8, :] = value
    for k in range(3):
        column_ref[k] = jnp.transpose(moved_ref[k])
    for side in range(2):
        for v in range(MROWS // 8):
            xyz = [margin_refs[side][k * MROWS + 8 * v : k * MROWS + 8 * v + 8, :] for k in range(3)]
            for k, value in enumerate(apply_pose(nbrs[side], xyz)):
                world_ref[side, k, 8 * v : 8 * v + 8, :] = value
    lane = iota(1)

    def one_block(side, row, cell):
        first = jnp.maximum(cell, 0) * TILES
        target = [
            [spread_out(world_ref[side, k, pl.ds(first + t, 1), :]) for t in range(TILES)] for k in range(3)
        ]
        pick = jnp.full(TILE, row, jnp.int32)
        parts = []
        for g in range(GROUPS):
            m = [
                jnp.take_along_axis(column_ref[k, 8 * g : 8 * g + 8, :], pick, axis=1, mode="promise_in_bounds")
                for k in range(3)
            ]
            sums = None
            for t in range(TILES):
                d = [m[k] - target[k][t] for k in range(3)]
                dist = d[0] * d[0] + d[1] * d[1] + d[2] * d[2]
                weight = jnp.exp2(dist * negc)
                terms = [weight * target[k][t] for k in range(3)] + [weight, weight * dist]
                sums = terms if sums is None else [a + b for a, b in zip(sums, terms)]
            part = jnp.zeros(TILE, F32)
            for q in range(5):
                part = jnp.where(lane == q, jnp.sum(sums[q], axis=1, keepdims=True), part)
            parts.append(part)
        flat = jnp.transpose(jnp.concatenate(parts, axis=0))[:8, :]
        xt = [spread_out(source_ref[k, pl.ds(row, 1), :]) for k in range(4)]
        return flat * (xt[3] / (spread_out(flat[3:4, :]) + OUTLIER_MASS)), xt

    return one_block


def pack_sums(sums, out_ref):
    lane, sub = iota(1), iota(0)
    total = jnp.zeros(TILE, F32)
    for c in range(5):
        total = total + jnp.where(lane == 8 * c + sub, jnp.sum(sums[c], axis=1, keepdims=True), 0.0)
    row = jnp.sum(total, axis=0, keepdims=True)
    out_ref[...] = jnp.broadcast_to(row, out_ref.shape)


def pose_of_row(row):
    return [spread_out(row[:, j : j + 1]) for j in range(12)]


def sides_of(line):
    odd = line & 1
    return [1 - odd, odd]


def first_kernel(cells_ref, pose_ref, source_ref, margin_a, margin_b, sums_ref, *scratch_refs):
    line = lax.axis_index("line")
    own = pose_of_row(pose_ref[...])
    nbrs = [pose_of_row(margin[3 * MROWS : 3 * MROWS + 1, :]) for margin in (margin_a, margin_b)]
    negc = jnp.full(TILE, -LOG2E / (2.0 * SPREAD_START), F32)
    sums = match(
        own, nbrs, negc, sides_of(line), cells_ref, source_ref, (margin_a, margin_b), scratch_refs, None
    )
    pack_sums(sums, sums_ref)


def solve(totals, old):
    def at(q):
        return spread_out(totals[:, q : q + 1])

    gram = {}
    for n, (a, b) in enumerate([(0, 0), (0, 1), (0, 2), (1, 1), (1, 2), (2, 2)]):
        gram[a, b] = at(QUAD + n)
    for a in range(3):
        gram[a, 3] = at(8 * a + 3)
    gram[3, 3] = at(SHARE)
    for a in range(4):
        gram[a, a] = gram[a, a] + REGULARIZE
    lower, diag, inverse = {}, [], []
    for j in range(4):
        scaled = [lower[j, k] * diag[k] for k in range(j)]
        pivot = gram[j, j]
        for k in range(j):
            pivot = pivot - lower[j, k] * scaled[k]
        diag.append(pivot)
        inverse.append(1.0 / pivot)
        for i in range(j + 1, 4):
            value = gram[j, i]
            for k in range(j):
                value = value - lower[i, k] * scaled[k]
            lower[i, j] = value * inverse[j]
    new = [None] * 12
    for k in range(3):
        right = []
        for m in range(4):
            j = 3 * k + m if m < 3 else 9 + k
            value = at(8 * m + k) + REGULARIZE * spread_out(old[:, j : j + 1])
            for n in range(m):
                value = value - lower[m, n] * right[n]
            right.append(value)
        found = [None] * 4
        for m in reversed(range(4)):
            value = right[m] * inverse[m]
            for n in range(m + 1, 4):
                value = value - lower[n, m] * found[n]
            found[m] = value
        for m in range(4):
            new[3 * k + m if m < 3 else 9 + k] = found[m]
    return new


def line_sum(all_ref, line, segs):
    return jnp.sum(all_ref[pl.ds(line * segs, segs), :], axis=0, keepdims=True)


def new_spread(all_ref):
    everything = jnp.sum(all_ref[...], axis=0, keepdims=True)
    top = spread_out(everything[:, ENERGY : ENERGY + 1]) + PRIOR_TOP
    return top / (3.0 * spread_out(everything[:, SHARE : SHARE + 1]) + PRIOR_BOTTOM)


def pose_row(new, sub):
    lane = iota(1)
    row = jnp.zeros(TILE, F32)
    for j in range(12):
        row = jnp.where(lane == j, spread_out(new[j][sub : sub + 1, :]), row)
    return row


def second_kernel(
    lines, segs, cells_ref, pose_ref, all_ref, source_ref, margin_a, margin_b,
    sums_ref, pose_out_ref, out_ref, *scratch_refs,
):
    line = lax.axis_index("line")
    dirs = sides_of(line)
    partner = [jnp.clip(line + 2 * d - 1, 0, lines - 1) for d in dirs]
    sub = iota(0)

    def stacked(a, b, c):
        return jnp.where(sub == 0, spread_out(a), jnp.where(sub == 1, spread_out(b), spread_out(c)))

    totals = stacked(*[line_sum(all_ref, n, segs) for n in (line, partner[0], partner[1])])
    old = stacked(pose_ref[...], margin_a[3 * MROWS : 3 * MROWS + 1, :], margin_b[3 * MROWS : 3 * MROWS + 1, :])
    new = solve(totals, old)
    negc = (-0.5 * LOG2E) / new_spread(all_ref)
    own, near_a, near_b = [[spread_out(value[n : n + 1, :]) for value in new] for n in range(3)]
    pose_out_ref[...] = pose_row(new, 0)[:1, :]
    sums = match(
        own, [near_a, near_b], negc, dirs, cells_ref, source_ref, (margin_a, margin_b), scratch_refs, out_ref
    )
    pack_sums(sums, sums_ref)


def last_kernel(segs, pose_ref, all_ref, fitted_ref, spread_ref):
    line = lax.axis_index("line")
    totals = spread_out(line_sum(all_ref, line, segs))
    new = solve(totals, spread_out(pose_ref[...]))
    fitted_ref[...] = pose_row(new, 0)[:1, :12]
    spread_ref[...] = new_spread(all_ref)[:1, :1]


def vmem(count):
    return [pl.BlockSpec(memory_space=pltpu.VMEM)] * count


SMEM = pl.BlockSpec(memory_space=pltpu.SMEM)
PARAMS = pltpu.CompilerParams(vmem_limit_bytes=32 * 1024 * 1024)


def scratch():
    return [
        pltpu.VMEM((2, 48, MARGIN), BF16),
        pltpu.VMEM((5, 8, 128), F32),
        pltpu.VMEM((2, 3, MROWS, 128), F32),
        pltpu.VMEM((3, 128, 128), F32),
        pltpu.VMEM((3, 128, 128), F32),
    ]


def pair_cost(cells):
    pairs = cells.size * BLOCK * CT
    return pl.CostEstimate(flops=400 * pairs, bytes_accessed=1 << 20, transcendentals=pairs)


def first_call(cells, pose_line, source, margin_a, margin_b, devices):
    return pl.pallas_call(
        first_kernel,
        in_specs=[SMEM] + vmem(4),
        out_specs=vmem(1)[0],
        out_shape=jax.ShapeDtypeStruct((devices, 128), F32),
        scratch_shapes=scratch(),
        compiler_params=PARAMS,
        cost_estimate=pair_cost(cells),
        name="match_first",
    )(cells, pose_line, source, margin_a, margin_b)


def second_call(cells, pose_line, everyone, source, margin_a, margin_b, lines, segs):
    return pl.pallas_call(
        functools.partial(second_kernel, lines, segs),
        in_specs=[SMEM] + vmem(5),
        out_specs=vmem(3),
        out_shape=[
            jax.ShapeDtypeStruct((lines * segs, 128), F32),
            jax.ShapeDtypeStruct((1, 128), F32),
            jax.ShapeDtypeStruct((5,) + source.shape[1:], F32),
        ],
        scratch_shapes=scratch(),
        compiler_params=PARAMS,
        cost_estimate=pair_cost(cells),
        name="match_second",
    )(cells, pose_line, everyone, source, margin_a, margin_b)


def exchange(sums):
    return lax.all_to_all(sums, ("line", "seg"), 0, 0)


def on_device(lines, segs, points, rows, cells, pose):
    own_points = points.reshape(3, -1, 128)
    slots = rows.shape[-1]
    blocks = slots // BLOCK
    row_list = rows.reshape(2, blocks, 128).transpose(1, 0, 2).reshape(2 * blocks, 128)
    cell_ids = cells.reshape(2, blocks)
    devices = lines * segs
    odd = lax.axis_index("line") & 1
    tail = own_points.shape[1] - MROWS
    pose_line = jnp.pad(pose.reshape(1, 12), ((0, 0), (0, 116)))
    pose_tile = jnp.pad(pose_line, ((0, 7), (0, 0)))

    def margin_at(first):
        part = lax.dynamic_slice_in_dim(own_points, first, MROWS, 1)
        return jnp.concatenate([part.reshape(3 * MROWS, 128), pose_tile], axis=0)

    pairs_a = [(i, i ^ 1) for i in range(lines) if i ^ 1 < lines]
    pairs_b = [(i, ((i + 1) ^ 1) - 1) for i in range(lines)]
    pairs_b = [(i, j) for i, j in pairs_b if 0 <= j < lines]
    margin_a = lax.ppermute(margin_at(jnp.where(odd == 1, 0, tail)), "line", pairs_a)
    margin_b = lax.ppermute(margin_at(jnp.where(odd == 1, tail, 0)), "line", pairs_b)
    source = gather(own_points, row_list)
    sums = first_call(cell_ids, pose_line, source, margin_a, margin_b, devices)
    everyone = exchange(sums)
    sums, pose_line, result = second_call(cell_ids, pose_line, everyone, source, margin_a, margin_b, lines, segs)
    everyone = exchange(sums)
    fitted, spread = pl.pallas_call(
        functools.partial(last_kernel, segs),
        in_specs=vmem(2),
        out_specs=vmem(2),
        out_shape=[jax.ShapeDtypeStruct((1, 12), F32), jax.ShapeDtypeStruct((1, 1), F32)],
        name="solve_last",
    )(pose_line, everyone)
    result = result.reshape(5, blocks, 2, 128).transpose(2, 0, 1, 3).reshape(1, 1, 2, 5, slots)
    return (result, fitted.reshape(12, 1), spread.reshape(1))


def solution(mesh):
    return jax.shard_map(
        functools.partial(on_device, mesh.shape["line"], mesh.shape["seg"]),
        mesh=mesh,
        in_specs=(
            P("line", "seg", None, None),
            P("line", "seg", None, None),
            P("line", "seg", None, None),
            P(None, "line"),
        ),
        out_specs=(P("line", "seg", None, None, None), P(None, "line"), P()),
        check_vma=False,
    )
```

```python
import functools
import math

import jax
import jax.numpy as jnp
from jax import lax
from jax.experimental import pallas as pl
from jax.experimental.pallas import tpu as pltpu
from jax.sharding import PartitionSpec as P

NCELL = 16
CT = 512
BLOCK = 128
MARGIN = NCELL * CT
MROWS = MARGIN // 128
TILES = CT // 128
GROUPS = BLOCK // 8
WIDE = 4
QUICK_LIMIT = 1000.0
ENERGY_LIMIT = 400.0

OUTLIER_MASS = 1.0
SPREAD_START = 0.05
PRIOR_TOP = 0.05
PRIOR_BOTTOM = 1.0
REGULARIZE = 1.0
LOG2E = math.log2(math.e)

F32 = jnp.float32
BF16 = jnp.bfloat16
TILE = (8, 128)
ONE = 24
SHARE = ONE + 3
ENERGY = ONE + 4
QUAD = 32
POSE = 64


def iota(axis):
    return lax.broadcasted_iota(jnp.int32, TILE, axis)


def spread_out(value):
    return jnp.broadcast_to(value, TILE)


def gather_kernel(points_ref, rows_ref, source_ref, table_ref, turned_ref, sems):
    slot_rows = rows_ref.shape[0]
    blocks = slot_rows // 2
    starts = [0, points_ref.shape[1] - MROWS]
    copies = [
        pltpu.make_async_copy(points_ref.at[:, pl.ds(starts[d], MROWS), :], table_ref.at[d], sems.at[d]) for d in range(2)
    ]
    for copy in copies:
        copy.start()
    for v in range(slot_rows // 8):
        source_ref[3, 8 * v : 8 * v + 8, :] = (rows_ref[8 * v : 8 * v + 8, :] >= 0).astype(F32)
    group = MROWS // 8
    for d in range(2):
        copies[d].wait()
        for k in range(3):
            parts = [three_parts(table_ref[d, k, 8 * v : 8 * v + 8, :]) for v in range(group)]
            stack = jnp.concatenate([parts[v][p] for p in range(3) for v in range(group)], axis=0)
            turned_ref[d, 128 * k : 128 * k + 128, :] = jnp.transpose(stack).astype(BF16)
        for first in range(0, blocks, WIDE):
            chosen = range(first, min(first + WIDE, blocks))
            spots = [jnp.maximum(rows_ref[2 * b + d : 2 * b + d + 1, :], 0) & (MARGIN - 1) for b in chosen]
            hits = []
            for spot in spots:
                high = spread_out(spot >> 7)
                hits.append(
                    jnp.concatenate([(high == iota(0) + 8 * v).astype(F32) for v in range(group)], axis=0).astype(BF16)
                )
            hit = jnp.concatenate(hits, axis=1)
            picked = jnp.dot(turned_ref[d], jnp.concatenate([hit] * 3, axis=0), preferred_element_type=F32)
            for n, b in enumerate(chosen):
                low = spread_out(spots[n] & 127)
                sums = [jnp.zeros(TILE, F32)] * 3
                for v in range(16):
                    here = low == iota(0) + 8 * v
                    for k in range(3):
                        part = picked[128 * k + 8 * v : 128 * k + 8 * v + 8, 128 * n : 128 * n + 128]
                        sums[k] = jnp.where(here, part, sums[k])
                for k in range(3):
                    source_ref[k, 2 * b + d : 2 * b + d + 1, :] = jnp.sum(sums[k], axis=0, keepdims=True)


def gather(points, rows):
    slot_rows = rows.shape[0]
    return pl.pallas_call(
        gather_kernel,
        in_specs=[pl.BlockSpec(memory_space=pl.ANY)] + vmem(1),
        out_specs=vmem(1)[0],
        out_shape=jax.ShapeDtypeStruct((4, slot_rows, 128), F32),
        scratch_shapes=[
            pltpu.VMEM((2, 3, MROWS, 128), F32),
            pltpu.VMEM((2, 3 * 128, 3 * MROWS), BF16),
            pltpu.SemaphoreType.DMA((2,)),
        ],
        compiler_params=PARAMS,
        name="gather_sources",
    )(points, rows)


def apply_pose(coefs, xyz):
    out = []
    for k in range(3):
        total = coefs[3 * k] * xyz[0]
        total = total + coefs[3 * k + 1] * xyz[1]
        total = total + coefs[3 * k + 2] * xyz[2]
        out.append(total + coefs[9 + k])
    return out


def column(coefs, first, stride):
    sub = iota(0)
    out = jnp.zeros(TILE, F32)
    for k in range(3):
        out = jnp.where(sub == k, coefs[first + stride * k], out)
    return out


def columns(coefs):
    return [column(coefs, k, 3) for k in range(3)] + [column(coefs, 9, 1)]


def squared_length(value):
    square = value * value
    return spread_out(square[0:1, :]) + spread_out(square[1:2, :]) + spread_out(square[2:3, :])


def three_parts(value):
    high = value.astype(BF16).astype(F32)
    rest = value - high
    middle = rest.astype(BF16).astype(F32)
    return high, middle, rest - middle


def combine(cols, xyz):
    return cols[0] * xyz[0] + cols[1] * xyz[1] + cols[2] * xyz[2]


def prepare(near, margin_ref, phi_ref, r):
    sub = iota(0)
    y = combine(near, [spread_out(margin_ref[k * MROWS + r : k * MROWS + r + 1, :]) for k in range(3)])
    length = squared_length(y)
    high, middle, low = three_parts(jnp.where(sub == 3, length, jnp.where(sub == 4, 1.0, y)))
    for i, pair in enumerate(((high, middle), (low, high), (middle, high))):
        phi_ref[16 * i : 16 * i + 16, 128 * r : 128 * r + 128] = jnp.concatenate(pair, axis=0).astype(BF16)
    return length


def longest_source(own, near, dirs, source_ref):
    longest = jnp.zeros(TILE, F32)
    for v in range(source_ref.shape[1] // 8):
        rows = slice(8 * v, 8 * v + 8)
        xyz = [source_ref[k, rows, :] for k in range(3)]
        moved = apply_pose(own, xyz)
        for side in range(2):
            square = sum((moved[k] - near[side][9 + k]) ** 2 for k in range(3))
            listed = (iota(0) & 1) == dirs[side]
            longest = jnp.maximum(longest, jnp.where(listed, square * source_ref[3, rows, :], 0.0))
    return longest


def weigh(negc, own, near, phi_refs, source_ref, side, row, cell):
    sub = iota(0)
    xt = [spread_out(source_ref[k, pl.ds(row, 1), :]) for k in range(4)]
    m = combine(own, xt) + (own[3] - near[side][3])
    length = squared_length(m)
    coef = jnp.where(sub == 3, negc, jnp.where(sub == 4, negc * length, (-2.0 * negc) * m))
    high, middle, low = three_parts(coef)
    stack = jnp.concatenate([high, high, high, middle, middle, low], axis=0)
    spot = pl.ds(pl.multiple_of(jnp.maximum(cell, 0) * CT, CT), CT)
    power = jnp.dot(jnp.transpose(stack).astype(BF16), phi_refs[side][:, spot], preferred_element_type=F32)
    weight = jnp.exp2(power)
    top = weight.astype(BF16)
    rest = (weight - top.astype(F32)).astype(BF16)
    return xt, m, length, spot, top, rest


def weighted_sums(phi_refs, side, spot, top, rest):
    last = (((1,), (1,)), ((), ()))
    features = phi_refs[side][:32, spot]
    sums = lax.dot_general(features, top, last, preferred_element_type=F32)
    sums = sums + lax.dot_general(features, rest, last, preferred_element_type=F32)
    return sums[0:8] + sums[8:16] + sums[16:24]


def finish(near, side, xt, m, length, sums):
    sub = iota(0)
    total = spread_out(sums[4:5, :])
    around = combine([spread_out(m[k : k + 1, :]) for k in range(3)], [spread_out(sums[k : k + 1, :]) for k in range(3)])
    energy = spread_out(sums[3:4, :]) - 2.0 * around + length * total
    raw = jnp.where(sub < 3, sums + near[side][3] * total, jnp.where(sub == 3, total, jnp.where(sub == 4, energy, 0.0)))
    return raw * (xt[3] / (total + OUTLIER_MASS)), xt


def match(own, nbrs, negc, dirs, cells_hbm, source_ref, margin_refs, scratch_refs, sums_ref, pose_row, out):
    phi_refs, (cells_ref, cells_sem, world_ref, moved_ref, column_ref) = scratch_refs[:2], scratch_refs[2:7]
    blocks = cells_ref.shape[1]
    fetch = pltpu.make_async_copy(cells_hbm, cells_ref, cells_sem)
    fetch.start()
    out_ref = None if out is None else out[1]
    own_cols, near_cols = columns(own), [columns(near) for near in nbrs]
    longest = jnp.zeros(TILE, F32)
    for r in range(MROWS):
        longest = jnp.maximum(longest, prepare(near_cols[0], margin_refs[0], phi_refs[0], r))
    fetch.wait()
    places = [(side, 2 * b + dirs[side], cells_ref[dirs[side], b]) for side in range(2) for b in range(blocks)]
    later = list(range(MROWS))
    each = -(-MROWS // max(1, blocks - 2))
    carry = [jnp.zeros(TILE, F32) for _ in range(5)]
    found = []
    ahead = None
    for n in range(-1, len(places)):
        block, ahead = ahead, None
        if n + 1 < len(places):
            ahead = weigh(negc, own_cols, near_cols, phi_refs, source_ref, *places[n + 1])
        for r in later[:each]:
            longest = jnp.maximum(longest, prepare(near_cols[1], margin_refs[1], phi_refs[1], r))
        later = later[each:]
        if block is not None:
            side, row, _ = places[n]
            xt, m, length, spot, top, rest = block
            found.append((row, *finish(near_cols, side, xt, m, length, weighted_sums(phi_refs, side, spot, top, rest))))
    for row, result, xt in found:
        carry = add_block(carry, row, result, xt, out_ref)
    if out is not None:
        save = pltpu.make_async_copy(out[1], out[0], out[2])
        save.start()
    pack_sums(carry, pose_row, sums_ref)
    size = spread_out(jnp.max(longest)) + spread_out(jnp.max(longest_source(own, nbrs, dirs, source_ref)))
    whole = jnp.sum(carry[3], axis=1, keepdims=True)
    share, energy = [spread_out(whole[q : q + 1, :]) for q in (3, 4)]
    bad = (size * -negc > QUICK_LIMIT) | (size * share > ENERGY_LIMIT * energy)

    @pl.when(jnp.max(bad.astype(F32)) > 0.0)
    def _():
        if out is not None:
            save.wait()
        one_block = careful_setup(own, nbrs, negc, source_ref, margin_refs, world_ref, moved_ref, column_ref)
        carry = tuple(jnp.zeros(TILE, F32) for _ in range(5))
        for side in range(2):
            d = dirs[side]

            def step(b, carry, side=side, d=d):
                result, xt = one_block(side, 2 * b + d, cells_ref[d, b])
                return tuple(add_block(carry, 2 * b + d, result, xt, out_ref))

            carry = lax.fori_loop(0, blocks, step, carry)
        pack_sums(carry, pose_row, sums_ref)
        if out is not None:
            save.start()

    if out is not None:
        save.wait()


def add_block(carry, row, result, xt, out_ref):
    sub = iota(0)
    if out_ref is not None:
        for q in range(5):
            out_ref[q, pl.ds(row, 1), :] = result[q : q + 1, :]
    left = jnp.where(sub < 3, xt[0], jnp.where(sub < 5, xt[1], xt[2]))
    right = jnp.where(sub == 0, xt[0], jnp.where((sub == 1) | (sub == 3), xt[1], xt[2]))
    share = spread_out(result[3:4, :])
    return [
        carry[0] + result * xt[0],
        carry[1] + result * xt[1],
        carry[2] + result * xt[2],
        carry[3] + result,
        carry[4] + share * (left * right),
    ]


def careful_setup(own, nbrs, negc, source_ref, margin_refs, world_ref, moved_ref, column_ref):
    slot_rows = source_ref.shape[1]
    for v in range(slot_rows // 8):
        xyz = [source_ref[k, 8 * v : 8 * v + 8, :] for k in range(3)]
        for k, value in enumerate(apply_pose(own, xyz)):
            moved_ref[k, 8 * v : 8 * v + 8, :] = value
    for k in range(3):
        column_ref[k] = jnp.transpose(moved_ref[k])
    for side in range(2):
        for v in range(MROWS // 8):
            xyz = [margin_refs[side][k * MROWS + 8 * v : k * MROWS + 8 * v + 8, :] for k in range(3)]
            for k, value in enumerate(apply_pose(nbrs[side], xyz)):
                world_ref[side, k, 8 * v : 8 * v + 8, :] = value
    lane = iota(1)

    def one_block(side, row, cell):
        first = jnp.maximum(cell, 0) * TILES
        target = [
            [spread_out(world_ref[side, k, pl.ds(first + t, 1), :]) for t in range(TILES)] for k in range(3)
        ]
        pick = jnp.full(TILE, row, jnp.int32)
        parts = []
        for g in range(GROUPS):
            m = [
                jnp.take_along_axis(column_ref[k, 8 * g : 8 * g + 8, :], pick, axis=1, mode="promise_in_bounds")
                for k in range(3)
            ]
            sums = None
            for t in range(TILES):
                d = [m[k] - target[k][t] for k in range(3)]
                dist = d[0] * d[0] + d[1] * d[1] + d[2] * d[2]
                weight = jnp.exp2(dist * negc)
                terms = [weight * target[k][t] for k in range(3)] + [weight, weight * dist]
                sums = terms if sums is None else [a + b for a, b in zip(sums, terms)]
            part = jnp.zeros(TILE, F32)
            for q in range(5):
                part = jnp.where(lane == q, jnp.sum(sums[q], axis=1, keepdims=True), part)
            parts.append(part)
        flat = jnp.transpose(jnp.concatenate(parts, axis=0))[:8, :]
        xt = [spread_out(source_ref[k, pl.ds(row, 1), :]) for k in range(4)]
        return flat * (xt[3] / (spread_out(flat[3:4, :]) + OUTLIER_MASS)), xt

    return one_block


def pack_sums(sums, pose_row, out_ref):
    lane, sub = iota(1), iota(0)
    total = jnp.zeros(TILE, F32)
    for c in range(5):
        total = total + jnp.where(lane == 8 * c + sub, jnp.sum(sums[c], axis=1, keepdims=True), 0.0)
    row = jnp.sum(total, axis=0, keepdims=True)
    out_ref[...] = jnp.broadcast_to(row + pose_row, out_ref.shape)


def pose_of_row(row):
    return [spread_out(row[:, j : j + 1]) for j in range(12)]


def sides_of(line):
    odd = line & 1
    return [1 - odd, odd]


def first_kernel(cells_hbm, pose_ref, source_ref, margin_a, margin_b, sums_ref, *scratch_refs):
    line = lax.axis_index("line")
    own = pose_of_row(pose_ref[...])
    nbrs = [pose_of_row(margin[3 * MROWS : 3 * MROWS + 1, :]) for margin in (margin_a, margin_b)]
    negc = jnp.full(TILE, -LOG2E / (2.0 * SPREAD_START), F32)
    margins = (margin_a, margin_b)
    match(own, nbrs, negc, sides_of(line), cells_hbm, source_ref, margins, scratch_refs, sums_ref, 0.0, None)


def solve(totals, old):
    def at(q):
        return spread_out(totals[:, q : q + 1])

    gram = {}
    for n, (a, b) in enumerate([(0, 0), (0, 1), (0, 2), (1, 1), (1, 2), (2, 2)]):
        gram[a, b] = at(QUAD + n)
    for a in range(3):
        gram[a, 3] = at(8 * a + 3)
    gram[3, 3] = at(SHARE)
    for a in range(4):
        gram[a, a] = gram[a, a] + REGULARIZE
    lower, diag, inverse = {}, [], []
    for j in range(4):
        scaled = [lower[j, k] * diag[k] for k in range(j)]
        pivot = gram[j, j]
        for k in range(j):
            pivot = pivot - lower[j, k] * scaled[k]
        diag.append(pivot)
        inverse.append(1.0 / pivot)
        for i in range(j + 1, 4):
            value = gram[j, i]
            for k in range(j):
                value = value - lower[i, k] * scaled[k]
            lower[i, j] = value * inverse[j]
    new = [None] * 12
    for k in range(3):
        right = []
        for m in range(4):
            j = 3 * k + m if m < 3 else 9 + k
            value = at(8 * m + k) + REGULARIZE * spread_out(old[:, j : j + 1])
            for n in range(m):
                value = value - lower[m, n] * right[n]
            right.append(value)
        found = [None] * 4
        for m in reversed(range(4)):
            value = right[m] * inverse[m]
            for n in range(m + 1, 4):
                value = value - lower[n, m] * found[n]
            found[m] = value
        for m in range(4):
            new[3 * k + m if m < 3 else 9 + k] = found[m]
    return new


def line_sum(all_ref, line, segs):
    return jnp.sum(all_ref[pl.ds(line * segs, segs), :], axis=0, keepdims=True)


def new_spread(all_ref):
    everything = jnp.sum(all_ref[...], axis=0, keepdims=True)
    top = spread_out(everything[:, ENERGY : ENERGY + 1]) + PRIOR_TOP
    return top / (3.0 * spread_out(everything[:, SHARE : SHARE + 1]) + PRIOR_BOTTOM)


def pose_row(new, first):
    lane = lax.broadcasted_iota(jnp.int32, (1, 128), 1)
    row = jnp.zeros((1, 128), F32)
    for j in range(12):
        row = jnp.where(lane == first + j, new[j][:1, :], row)
    return row


def second_kernel(
    lines, segs, cells_hbm, pose_ref, all_ref, source_ref, margin_a, margin_b,
    sums_ref, out_hbm, *scratch_refs,
):
    line = lax.axis_index("line")
    dirs = sides_of(line)
    partner = [jnp.clip(line + 2 * d - 1, 0, lines - 1) for d in dirs]
    sub = iota(0)

    def stacked(a, b, c):
        return jnp.where(sub == 0, spread_out(a), jnp.where(sub == 1, spread_out(b), spread_out(c)))

    totals = stacked(*[line_sum(all_ref, n, segs) for n in (line, partner[0], partner[1])])
    old = stacked(pose_ref[...], margin_a[3 * MROWS : 3 * MROWS + 1, :], margin_b[3 * MROWS : 3 * MROWS + 1, :])
    new = solve(totals, old)
    negc = (-0.5 * LOG2E) / new_spread(all_ref)
    own, near_a, near_b = [[spread_out(value[n : n + 1, :]) for value in new] for n in range(3)]
    margins = (margin_a, margin_b)
    out_ref, out_sem = scratch_refs[7:9]
    match(
        own, [near_a, near_b], negc, dirs, cells_hbm, source_ref, margins, scratch_refs, sums_ref,
        pose_row(new, POSE), (out_hbm, out_ref, out_sem),
    )


def last_kernel(segs, all_ref, fitted_ref, spread_ref):
    line = lax.axis_index("line")
    totals = spread_out(line_sum(all_ref, line, segs))
    old = all_ref[pl.ds(line * segs, 1), :][:, POSE : POSE + 12]
    new = solve(totals, jnp.broadcast_to(old, (8, 12)))
    fitted_ref[...] = pose_row(new, 0)[:, :12]
    spread_ref[...] = new_spread(all_ref)[:1, :1]


def vmem(count):
    return [pl.BlockSpec(memory_space=pltpu.VMEM)] * count


ANY = pl.BlockSpec(memory_space=pl.ANY)
PARAMS = pltpu.CompilerParams(vmem_limit_bytes=32 * 1024 * 1024)


def scratch(cells):
    return [
        pltpu.VMEM((48, MARGIN), BF16),
        pltpu.VMEM((48, MARGIN), BF16),
        pltpu.SMEM(cells.shape, jnp.int32),
        pltpu.SemaphoreType.DMA,
        pltpu.VMEM((2, 3, MROWS, 128), F32),
        pltpu.VMEM((3, 128, 128), F32),
        pltpu.VMEM((3, 128, 128), F32),
    ]


def pair_cost(cells):
    pairs = cells.size * BLOCK * CT
    return pl.CostEstimate(flops=400 * pairs, bytes_accessed=1 << 20, transcendentals=pairs)


def first_call(cells, pose_line, source, margin_a, margin_b, devices):
    return pl.pallas_call(
        first_kernel,
        in_specs=[ANY] + vmem(4),
        out_specs=vmem(1)[0],
        out_shape=jax.ShapeDtypeStruct((devices, 128), F32),
        scratch_shapes=scratch(cells),
        compiler_params=PARAMS,
        cost_estimate=pair_cost(cells),
        name="match_first",
    )(cells, pose_line, source, margin_a, margin_b)


def second_call(cells, pose_line, everyone, source, margin_a, margin_b, lines, segs):
    result = (5,) + source.shape[1:]
    return pl.pallas_call(
        functools.partial(second_kernel, lines, segs),
        in_specs=[ANY] + vmem(5),
        out_specs=vmem(1) + [ANY],
        out_shape=[jax.ShapeDtypeStruct((lines * segs, 128), F32), jax.ShapeDtypeStruct(result, F32)],
        scratch_shapes=scratch(cells) + [pltpu.VMEM(result, F32), pltpu.SemaphoreType.DMA],
        compiler_params=PARAMS,
        cost_estimate=pair_cost(cells),
        name="match_second",
    )(cells, pose_line, everyone, source, margin_a, margin_b)


def exchange(sums):
    return lax.all_to_all(sums, ("line", "seg"), 0, 0)


def on_device(lines, segs, points, rows, cells, pose):
    own_points = points.reshape(3, -1, 128)
    slots = rows.shape[-1]
    blocks = slots // BLOCK
    row_list = rows.reshape(2, blocks, 128).transpose(1, 0, 2).reshape(2 * blocks, 128)
    cell_ids = cells.reshape(2, blocks)
    devices = lines * segs
    odd = lax.axis_index("line") & 1
    tail = own_points.shape[1] - MROWS
    pose_line = jnp.pad(pose.reshape(1, 12), ((0, 0), (0, 116)))
    pose_tile = jnp.pad(pose_line, ((0, 7), (0, 0)))

    def margin_at(first):
        part = lax.dynamic_slice_in_dim(own_points, first, MROWS, 1)
        return jnp.concatenate([part.reshape(3 * MROWS, 128), pose_tile], axis=0)

    pairs_a = [(i, i ^ 1) for i in range(lines) if i ^ 1 < lines]
    pairs_b = [(i, ((i + 1) ^ 1) - 1) for i in range(lines)]
    pairs_b = [(i, j) for i, j in pairs_b if 0 <= j < lines]
    margin_a = lax.ppermute(margin_at(jnp.where(odd == 1, 0, tail)), "line", pairs_a)
    margin_b = lax.ppermute(margin_at(jnp.where(odd == 1, tail, 0)), "line", pairs_b)
    source = gather(own_points, row_list)
    sums = first_call(cell_ids, pose_line, source, margin_a, margin_b, devices)
    everyone = exchange(sums)
    sums, result = second_call(cell_ids, pose_line, everyone, source, margin_a, margin_b, lines, segs)
    everyone = exchange(sums)
    fitted, spread = pl.pallas_call(
        functools.partial(last_kernel, segs),
        in_specs=vmem(1),
        out_specs=vmem(2),
        out_shape=[jax.ShapeDtypeStruct((1, 12), F32), jax.ShapeDtypeStruct((1, 1), F32)],
        compiler_params=PARAMS,
        name="solve_last",
    )(everyone)
    result = result.reshape(5, blocks, 2, 128).transpose(2, 0, 1, 3).reshape(1, 1, 2, 5, slots)
    return (result, fitted.reshape(12, 1), spread.reshape(1))


def solution(mesh):
    return jax.shard_map(
        functools.partial(on_device, mesh.shape["line"], mesh.shape["seg"]),
        mesh=mesh,
        in_specs=(
            P("line", "seg", None, None),
            P("line", "seg", None, None),
            P("line", "seg", None, None),
            P(None, "line"),
        ),
        out_specs=(P("line", "seg", None, None, None), P(None, "line"), P()),
        check_vma=False,
    )
```

```python
import functools
import math

import jax
import jax.numpy as jnp
from jax import lax
from jax.experimental import pallas as pl
from jax.experimental.pallas import tpu as pltpu
from jax.sharding import PartitionSpec as P

NCELL = 16
CT = 512
BLOCK = 128
MARGIN = NCELL * CT
MROWS = MARGIN // 128
TILES = CT // 128
GROUPS = BLOCK // 8
WIDE = 4
QUICK_LIMIT = 1000.0
ENERGY_LIMIT = 400.0

OUTLIER_MASS = 1.0
SPREAD_START = 0.05
PRIOR_TOP = 0.05
PRIOR_BOTTOM = 1.0
REGULARIZE = 1.0
LOG2E = math.log2(math.e)

F32 = jnp.float32
BF16 = jnp.bfloat16
TILE = (8, 128)
ONE = 24
SHARE = ONE + 3
ENERGY = ONE + 4
QUAD = 32
POSE = 64


def iota(axis):
    return lax.broadcasted_iota(jnp.int32, TILE, axis)


def spread_out(value):
    return jnp.broadcast_to(value, TILE)


def pack_kernel(points_hbm, pose_hbm, cells_hbm, sent_a, sent_b, cells_ref, pose_ref, sems):
    odd = lax.axis_index("line") & 1
    tail = points_hbm.shape[1] - MROWS
    copies = [
        pltpu.make_async_copy(pose_hbm, pose_ref, sems.at[6]),
        pltpu.make_async_copy(cells_hbm, cells_ref, sems.at[7]),
    ]
    for n, (sent, first) in enumerate(((sent_a, (1 - odd) * tail), (sent_b, odd * tail))):
        spot = pl.ds(pl.multiple_of(first, MROWS), MROWS)
        for k in range(3):
            copies.append(
                pltpu.make_async_copy(points_hbm.at[k, spot, :], sent.at[pl.ds(MROWS * k, MROWS), :], sems.at[3 * n + k])
            )
    for copy in copies:
        copy.start()
    for sent in (sent_a, sent_b):
        sent[3 * MROWS :, :] = jnp.zeros(TILE, F32)
    copies[0].wait()
    for sent in (sent_a, sent_b):
        sent[3 * MROWS : 3 * MROWS + 1, :12] = pose_ref[...]
    for copy in copies[1:]:
        copy.wait()


def pack_call(points, pose, cells):
    return pl.pallas_call(
        pack_kernel,
        in_specs=[HBM] * 3,
        out_specs=vmem(3),
        out_shape=[jax.ShapeDtypeStruct((3 * MROWS + 8, 128), F32)] * 2 + [jax.ShapeDtypeStruct(cells.shape, jnp.int32)],
        scratch_shapes=[pltpu.VMEM((1, 12), F32), pltpu.SemaphoreType.DMA((8,))],
        compiler_params=PARAMS,
        name="pack_margins",
    )(points, pose, cells)


def turn_margin(margin_ref, turned_ref):
    group = MROWS // 8
    for k in range(3):
        parts = [three_parts(margin_ref[MROWS * k + 8 * v : MROWS * k + 8 * v + 8, :]) for v in range(group)]
        stack = jnp.concatenate([parts[v][p] for p in range(3) for v in range(group)], axis=0)
        turned_ref[128 * k : 128 * k + 128, :] = jnp.transpose(stack).astype(BF16)


def pick_rows(rows_ref, turned_ref, rows):
    spots = [jnp.maximum(rows_ref[pl.ds(row, 1), :], 0) & (MARGIN - 1) for row in rows]
    hits = []
    for spot in spots:
        high = spread_out(spot >> 7)
        hit = [(high == iota(0) + 8 * v).astype(F32) for v in range(MROWS // 8)]
        hits.append(jnp.concatenate(hit, axis=0).astype(BF16))
    hit = jnp.concatenate(hits, axis=1)
    return spots, jnp.dot(turned_ref[...], jnp.concatenate([hit] * 3, axis=0), preferred_element_type=F32)


def pick_lanes(source_ref, rows, spots, picked):
    for n, row in enumerate(rows):
        low = spread_out(spots[n] & 127)
        sums = [jnp.zeros(TILE, F32)] * 3
        for v in range(16):
            here = low == iota(0) + 8 * v
            for k in range(3):
                part = picked[128 * k + 8 * v : 128 * k + 8 * v + 8, 128 * n : 128 * n + 128]
                sums[k] = jnp.where(here, part, sums[k])
        for k in range(3):
            source_ref[k, pl.ds(row, 1), :] = jnp.sum(sums[k], axis=0, keepdims=True)


def apply_pose(coefs, xyz):
    out = []
    for k in range(3):
        total = coefs[3 * k] * xyz[0]
        total = total + coefs[3 * k + 1] * xyz[1]
        total = total + coefs[3 * k + 2] * xyz[2]
        out.append(total + coefs[9 + k])
    return out


def column(coefs, first, stride):
    sub = iota(0)
    out = jnp.zeros(TILE, F32)
    for k in range(3):
        out = jnp.where(sub == k, coefs[first + stride * k], out)
    return out


def columns(coefs):
    return [column(coefs, k, 3) for k in range(3)] + [column(coefs, 9, 1)]


def squared_length(value):
    square = value * value
    return spread_out(square[0:1, :]) + spread_out(square[1:2, :]) + spread_out(square[2:3, :])


def three_parts(value):
    high = value.astype(BF16).astype(F32)
    rest = value - high
    middle = rest.astype(BF16).astype(F32)
    return high, middle, rest - middle


def combine(cols, xyz):
    return cols[0] * xyz[0] + cols[1] * xyz[1] + cols[2] * xyz[2]


def prepare(near, margin_ref, phi_ref, r):
    sub = iota(0)
    y = combine(near, [spread_out(margin_ref[k * MROWS + r : k * MROWS + r + 1, :]) for k in range(3)])
    length = squared_length(y)
    high, middle, low = three_parts(jnp.where(sub == 3, length, jnp.where(sub == 4, 1.0, y)))
    for i, pair in enumerate(((high, middle), (low, high), (middle, high))):
        phi_ref[16 * i : 16 * i + 16, 128 * r : 128 * r + 128] = jnp.concatenate(pair, axis=0).astype(BF16)
    return length


def longest_source(own, near, dirs, source_ref):
    longest = jnp.zeros(TILE, F32)
    for v in range(source_ref.shape[1] // 8):
        rows = slice(8 * v, 8 * v + 8)
        xyz = [source_ref[k, rows, :] for k in range(3)]
        moved = apply_pose(own, xyz)
        for side in range(2):
            square = sum((moved[k] - near[side][9 + k]) ** 2 for k in range(3))
            listed = (iota(0) & 1) == dirs[side]
            longest = jnp.maximum(longest, jnp.where(listed, square * source_ref[3, rows, :], 0.0))
    return longest


def weigh(negc, own, near, phi_refs, source_ref, side, row, cell):
    sub = iota(0)
    xt = [spread_out(source_ref[k, pl.ds(row, 1), :]) for k in range(4)]
    m = combine(own, xt) + (own[3] - near[side][3])
    length = squared_length(m)
    coef = jnp.where(sub == 3, negc, jnp.where(sub == 4, negc * length, (-2.0 * negc) * m))
    high, middle, low = three_parts(coef)
    stack = jnp.concatenate([high, high, high, middle, middle, low], axis=0)
    spot = pl.ds(pl.multiple_of(jnp.maximum(cell, 0) * CT, CT), CT)
    power = jnp.dot(jnp.transpose(stack).astype(BF16), phi_refs[side][:, spot], preferred_element_type=F32)
    weight = jnp.exp2(power)
    top = weight.astype(BF16)
    rest = (weight - top.astype(F32)).astype(BF16)
    return xt, m, length, spot, top, rest


def weighted_sums(phi_refs, side, spot, top, rest):
    last = (((1,), (1,)), ((), ()))
    features = phi_refs[side][:32, spot]
    sums = lax.dot_general(features, top, last, preferred_element_type=F32)
    sums = sums + lax.dot_general(features, rest, last, preferred_element_type=F32)
    return sums[0:8] + sums[8:16] + sums[16:24]


def finish(near, side, xt, m, length, sums):
    sub = iota(0)
    total = spread_out(sums[4:5, :])
    around = combine([spread_out(m[k : k + 1, :]) for k in range(3)], [spread_out(sums[k : k + 1, :]) for k in range(3)])
    energy = spread_out(sums[3:4, :]) - 2.0 * around + length * total
    raw = jnp.where(sub < 3, sums + near[side][3] * total, jnp.where(sub == 3, total, jnp.where(sub == 4, energy, 0.0)))
    return raw * (xt[3] / (total + OUTLIER_MASS)), xt


class Lists:
    def __init__(self, dirs, cells_hbm, source_ref, scratch_refs):
        self.dirs = dirs
        self.source_ref = source_ref
        self.cells_ref, cells_sem = scratch_refs[:2]
        self.phi_refs = scratch_refs[2:4]
        self.world_ref, self.moved_ref, self.column_ref = scratch_refs[4:7]
        self.fetch = pltpu.make_async_copy(cells_hbm, self.cells_ref, cells_sem)
        self.fetch.start()

    def places(self, side):
        d = self.dirs[side]
        return [(side, 2 * b + d, self.cells_ref[d, b]) for b in range(self.cells_ref.shape[1])]


def quick(lists, own, nbrs, negc, places, side_work, carry, out_ref):
    own_cols, near_cols = columns(own), [columns(near) for near in nbrs]
    near_cols += [near_cols[0]] * (2 - len(near_cols))
    phi_refs = lists.phi_refs
    found = []
    ahead = None
    each = -(-len(side_work) // max(1, lists.cells_ref.shape[1] - 2))
    for n in range(-1, len(places)):
        block, ahead = ahead, None
        if n + 1 < len(places):
            ahead = weigh(negc, own_cols, near_cols, phi_refs, lists.source_ref, *places[n + 1])
        for work in side_work[:each]:
            work()
        side_work = side_work[each:]
        if block is not None:
            side, row, _ = places[n]
            xt, m, length, spot, top, rest = block
            found.append((row, *finish(near_cols, side, xt, m, length, weighted_sums(phi_refs, side, spot, top, rest))))
    for row, result, xt in found:
        carry = add_block(carry, row, result, xt, out_ref)
    return carry


def no_sums():
    return [jnp.zeros(TILE, F32) for _ in range(5)]


def close(lists, own, nbrs, negc, margin_refs, carry, longest, pose_row, sums_ref, out):
    out_ref = None if out is None else out[1]
    if out is not None:
        save = pltpu.make_async_copy(out[1], out[0], out[2])
        save.start()
    pack_sums(carry, pose_row, sums_ref)
    size = spread_out(jnp.max(longest)) + spread_out(jnp.max(longest_source(own, nbrs, lists.dirs, lists.source_ref)))
    whole = jnp.sum(carry[3], axis=1, keepdims=True)
    share, energy = [spread_out(whole[q : q + 1, :]) for q in (3, 4)]
    bad = (size * -negc > QUICK_LIMIT) | (size * share > ENERGY_LIMIT * energy)

    @pl.when(jnp.max(bad.astype(F32)) > 0.0)
    def _():
        if out is not None:
            save.wait()
        one_block = careful_setup(
            own, nbrs, negc, lists.source_ref, margin_refs, lists.world_ref, lists.moved_ref, lists.column_ref
        )
        carry = tuple(no_sums())
        for side in range(2):
            d = lists.dirs[side]

            def step(b, carry, side=side, d=d):
                result, xt = one_block(side, 2 * b + d, lists.cells_ref[d, b])
                return tuple(add_block(carry, 2 * b + d, result, xt, out_ref))

            carry = lax.fori_loop(0, lists.cells_ref.shape[1], step, carry)
        pack_sums(carry, pose_row, sums_ref)
        if out is not None:
            save.start()

    if out is not None:
        save.wait()


def add_block(carry, row, result, xt, out_ref):
    sub = iota(0)
    if out_ref is not None:
        for q in range(5):
            out_ref[q, pl.ds(row, 1), :] = result[q : q + 1, :]
    left = jnp.where(sub < 3, xt[0], jnp.where(sub < 5, xt[1], xt[2]))
    right = jnp.where(sub == 0, xt[0], jnp.where((sub == 1) | (sub == 3), xt[1], xt[2]))
    share = spread_out(result[3:4, :])
    return [
        carry[0] + result * xt[0],
        carry[1] + result * xt[1],
        carry[2] + result * xt[2],
        carry[3] + result,
        carry[4] + share * (left * right),
    ]


def careful_setup(own, nbrs, negc, source_ref, margin_refs, world_ref, moved_ref, column_ref):
    slot_rows = source_ref.shape[1]
    for v in range(slot_rows // 8):
        xyz = [source_ref[k, 8 * v : 8 * v + 8, :] for k in range(3)]
        for k, value in enumerate(apply_pose(own, xyz)):
            moved_ref[k, 8 * v : 8 * v + 8, :] = value
    for k in range(3):
        column_ref[k] = jnp.transpose(moved_ref[k])
    for side in range(2):
        for v in range(MROWS // 8):
            xyz = [margin_refs[side][k * MROWS + 8 * v : k * MROWS + 8 * v + 8, :] for k in range(3)]
            for k, value in enumerate(apply_pose(nbrs[side], xyz)):
                world_ref[side, k, 8 * v : 8 * v + 8, :] = value
    lane = iota(1)

    def one_block(side, row, cell):
        first = jnp.maximum(cell, 0) * TILES
        target = [
            [spread_out(world_ref[side, k, pl.ds(first + t, 1), :]) for t in range(TILES)] for k in range(3)
        ]
        pick = jnp.full(TILE, row, jnp.int32)
        parts = []
        for g in range(GROUPS):
            m = [
                jnp.take_along_axis(column_ref[k, 8 * g : 8 * g + 8, :], pick, axis=1, mode="promise_in_bounds")
                for k in range(3)
            ]
            sums = None
            for t in range(TILES):
                d = [m[k] - target[k][t] for k in range(3)]
                dist = d[0] * d[0] + d[1] * d[1] + d[2] * d[2]
                weight = jnp.exp2(dist * negc)
                terms = [weight * target[k][t] for k in range(3)] + [weight, weight * dist]
                sums = terms if sums is None else [a + b for a, b in zip(sums, terms)]
            part = jnp.zeros(TILE, F32)
            for q in range(5):
                part = jnp.where(lane == q, jnp.sum(sums[q], axis=1, keepdims=True), part)
            parts.append(part)
        flat = jnp.transpose(jnp.concatenate(parts, axis=0))[:8, :]
        xt = [spread_out(source_ref[k, pl.ds(row, 1), :]) for k in range(4)]
        return flat * (xt[3] / (spread_out(flat[3:4, :]) + OUTLIER_MASS)), xt

    return one_block


def pack_sums(sums, pose_row, out_ref):
    lane, sub = iota(1), iota(0)
    total = jnp.zeros(TILE, F32)
    for c in range(5):
        total = total + jnp.where(lane == 8 * c + sub, jnp.sum(sums[c], axis=1, keepdims=True), 0.0)
    row = jnp.sum(total, axis=0, keepdims=True)
    out_ref[...] = jnp.broadcast_to(row + pose_row, out_ref.shape)


def pose_of_row(row):
    return [spread_out(row[:, j : j + 1]) for j in range(12)]


def sides_of(line):
    odd = line & 1
    return [1 - odd, odd]


def features(near, margin_ref, phi_ref, longest):
    cols = columns(near)

    def make(r):
        longest[0] = jnp.maximum(longest[0], prepare(cols, margin_ref, phi_ref, r))

    return [functools.partial(make, r) for r in range(MROWS)]


def first_negc():
    return jnp.full(TILE, -LOG2E / (2.0 * SPREAD_START), F32)


def pose_in(margin_ref):
    return pose_of_row(margin_ref[3 * MROWS : 3 * MROWS + 1, :])


def partner_kernel(
    cells_hbm, rows_ref, sent_a, sent_b, margin_a, source_ref, part_ref, turned_a, turned_b, *scratch_refs
):
    dirs = sides_of(lax.axis_index("line"))
    lists = Lists(dirs, cells_hbm, source_ref, scratch_refs)
    own, near = pose_in(sent_a), pose_in(margin_a)
    slot_rows = rows_ref.shape[0]
    blocks = slot_rows // 2
    for v in range(slot_rows // 8):
        source_ref[3, 8 * v : 8 * v + 8, :] = (rows_ref[8 * v : 8 * v + 8, :] >= 0).astype(F32)

    def gather_tasks(side, turned_ref):
        tasks = []
        for first in range(0, blocks, WIDE):
            rows = [2 * b + dirs[side] for b in range(first, min(first + WIDE, blocks))]
            held = []
            tasks.append(lambda rows=rows, held=held: held.extend(pick_rows(rows_ref, turned_ref, rows)))
            tasks.append(lambda rows=rows, held=held: pick_lanes(source_ref, rows, *held))
        return tasks

    turn_margin(sent_a, turned_a)
    turn_margin(sent_b, turned_b)
    longest = [jnp.zeros(TILE, F32)]
    tasks = gather_tasks(0, turned_a)
    for n in range(0, len(tasks) + 2, 2):
        for task in tasks[n : n + 1] + tasks[max(n - 1, 0) : n]:
            task()
    for task in features(near, margin_a, lists.phi_refs[0], longest):
        task()
    lists.fetch.wait()
    carry = quick(lists, own, [near], first_negc(), lists.places(0), gather_tasks(1, turned_b), no_sums(), None)
    for n, value in enumerate(carry + longest):
        part_ref[n] = value


def other_kernel(cells_hbm, sent_a, source_ref, part_ref, margin_a, margin_b, sums_ref, *scratch_refs):
    lists = Lists(sides_of(lax.axis_index("line")), cells_hbm, source_ref, scratch_refs)
    own = pose_in(sent_a)
    nbrs = [pose_in(margin) for margin in (margin_a, margin_b)]
    longest = [part_ref[5]]
    for task in features(nbrs[1], margin_b, lists.phi_refs[1], longest):
        task()
    lists.fetch.wait()
    carry = quick(lists, own, nbrs, first_negc(), lists.places(1), [], [part_ref[n] for n in range(5)], None)
    close(lists, own, nbrs, first_negc(), (margin_a, margin_b), carry, longest[0], 0.0, sums_ref, None)


def solve(totals, old):
    def at(q):
        return spread_out(totals[:, q : q + 1])

    gram = {}
    for n, (a, b) in enumerate([(0, 0), (0, 1), (0, 2), (1, 1), (1, 2), (2, 2)]):
        gram[a, b] = at(QUAD + n)
    for a in range(3):
        gram[a, 3] = at(8 * a + 3)
    gram[3, 3] = at(SHARE)
    for a in range(4):
        gram[a, a] = gram[a, a] + REGULARIZE
    lower, diag, inverse = {}, [], []
    for j in range(4):
        scaled = [lower[j, k] * diag[k] for k in range(j)]
        pivot = gram[j, j]
        for k in range(j):
            pivot = pivot - lower[j, k] * scaled[k]
        diag.append(pivot)
        inverse.append(1.0 / pivot)
        for i in range(j + 1, 4):
            value = gram[j, i]
            for k in range(j):
                value = value - lower[i, k] * scaled[k]
            lower[i, j] = value * inverse[j]
    new = [None] * 12
    for k in range(3):
        right = []
        for m in range(4):
            j = 3 * k + m if m < 3 else 9 + k
            value = at(8 * m + k) + REGULARIZE * spread_out(old[:, j : j + 1])
            for n in range(m):
                value = value - lower[m, n] * right[n]
            right.append(value)
        found = [None] * 4
        for m in reversed(range(4)):
            value = right[m] * inverse[m]
            for n in range(m + 1, 4):
                value = value - lower[n, m] * found[n]
            found[m] = value
        for m in range(4):
            new[3 * k + m if m < 3 else 9 + k] = found[m]
    return new


def line_sum(all_ref, line, segs):
    return jnp.sum(all_ref[pl.ds(line * segs, segs), :], axis=0, keepdims=True)


def new_spread(all_ref):
    everything = jnp.sum(all_ref[...], axis=0, keepdims=True)
    top = spread_out(everything[:, ENERGY : ENERGY + 1]) + PRIOR_TOP
    return top / (3.0 * spread_out(everything[:, SHARE : SHARE + 1]) + PRIOR_BOTTOM)


def pose_row(new, first):
    lane = lax.broadcasted_iota(jnp.int32, (1, 128), 1)
    row = jnp.zeros((1, 128), F32)
    for j in range(12):
        row = jnp.where(lane == first + j, new[j][:1, :], row)
    return row


def second_kernel(
    lines, segs, cells_hbm, sent_a, all_ref, source_ref, margin_a, margin_b,
    sums_ref, out_hbm, out_ref, out_sem, *scratch_refs,
):
    line = lax.axis_index("line")
    dirs = sides_of(line)
    lists = Lists(dirs, cells_hbm, source_ref, scratch_refs)
    partner = [jnp.clip(line + 2 * d - 1, 0, lines - 1) for d in dirs]
    sub = iota(0)

    def stacked(a, b, c):
        return jnp.where(sub == 0, spread_out(a), jnp.where(sub == 1, spread_out(b), spread_out(c)))

    totals = stacked(*[line_sum(all_ref, n, segs) for n in (line, partner[0], partner[1])])
    old = stacked(*[ref[3 * MROWS : 3 * MROWS + 1, :] for ref in (sent_a, margin_a, margin_b)])
    new = solve(totals, old)
    negc = (-0.5 * LOG2E) / new_spread(all_ref)
    own, *nbrs = [[spread_out(value[n : n + 1, :]) for value in new] for n in range(3)]
    longest = [jnp.zeros(TILE, F32)]
    for task in features(nbrs[0], margin_a, lists.phi_refs[0], longest):
        task()
    lists.fetch.wait()
    places = lists.places(0) + lists.places(1)
    later = features(nbrs[1], margin_b, lists.phi_refs[1], longest)
    carry = quick(lists, own, nbrs, negc, places, later, no_sums(), out_ref)
    margins = (margin_a, margin_b)
    close(lists, own, nbrs, negc, margins, carry, longest[0], pose_row(new, POSE), sums_ref, (out_hbm, out_ref, out_sem))


def last_kernel(segs, all_ref, fitted_ref, spread_ref):
    line = lax.axis_index("line")
    totals = spread_out(line_sum(all_ref, line, segs))
    old = all_ref[pl.ds(line * segs, 1), :][:, POSE : POSE + 12]
    new = solve(totals, jnp.broadcast_to(old, (8, 12)))
    fitted_ref[...] = pose_row(new, 0)[:, :12]
    spread_ref[...] = new_spread(all_ref)[:1, :1]


def vmem(count):
    return [pl.BlockSpec(memory_space=pltpu.VMEM)] * count


ANY = pl.BlockSpec(memory_space=pl.ANY)
HBM = pl.BlockSpec(memory_space=pltpu.HBM)
PARAMS = pltpu.CompilerParams(vmem_limit_bytes=32 * 1024 * 1024)


def scratch(cells):
    return [
        pltpu.SMEM(cells.shape, jnp.int32),
        pltpu.SemaphoreType.DMA,
        pltpu.VMEM((48, MARGIN), BF16),
        pltpu.VMEM((48, MARGIN), BF16),
        pltpu.VMEM((2, 3, MROWS, 128), F32),
        pltpu.VMEM((3, 128, 128), F32),
        pltpu.VMEM((3, 128, 128), F32),
    ]


def in_hbm(value):
    return pltpu.with_memory_space_constraint(value, pltpu.HBM)


def pair_cost(cells, sides):
    pairs = cells.size // 2 * sides * BLOCK * CT
    return pl.CostEstimate(flops=400 * pairs, bytes_accessed=1 << 20, transcendentals=pairs)


def partner_call(cells, rows, sent_a, sent_b, margin_a):
    return pl.pallas_call(
        partner_kernel,
        in_specs=[ANY] + vmem(4),
        out_specs=vmem(2),
        out_shape=[
            jax.ShapeDtypeStruct((4,) + rows.shape, F32),
            jax.ShapeDtypeStruct((6,) + TILE, F32),
        ],
        scratch_shapes=[pltpu.VMEM((3 * 128, 3 * MROWS), BF16)] * 2 + scratch(cells),
        compiler_params=PARAMS,
        cost_estimate=pair_cost(cells, 1),
        name="match_partner",
    )(cells, rows, sent_a, sent_b, margin_a)


def other_call(cells, sent_a, source, part, margin_a, margin_b, devices):
    return pl.pallas_call(
        other_kernel,
        in_specs=[ANY] + vmem(5),
        out_specs=vmem(1)[0],
        out_shape=jax.ShapeDtypeStruct((devices, 128), F32),
        scratch_shapes=scratch(cells),
        compiler_params=PARAMS,
        cost_estimate=pair_cost(cells, 1),
        name="match_other",
    )(cells, sent_a, source, part, margin_a, margin_b)


def second_call(cells, sent_a, everyone, source, margin_a, margin_b, lines, segs):
    result = (5,) + source.shape[1:]
    return pl.pallas_call(
        functools.partial(second_kernel, lines, segs),
        in_specs=[ANY] + vmem(5),
        out_specs=vmem(1) + [ANY],
        out_shape=[jax.ShapeDtypeStruct((lines * segs, 128), F32), jax.ShapeDtypeStruct(result, F32)],
        scratch_shapes=[pltpu.VMEM(result, F32), pltpu.SemaphoreType.DMA] + scratch(cells),
        compiler_params=PARAMS,
        cost_estimate=pair_cost(cells, 2),
        name="match_second",
    )(cells, sent_a, everyone, source, margin_a, margin_b)


def exchange(sums):
    return lax.all_to_all(sums, ("line", "seg"), 0, 0)


def on_device(lines, segs, points, rows, cells, pose):
    own_points = points.reshape(3, -1, 128)
    slots = rows.shape[-1]
    blocks = slots // BLOCK
    row_list = rows.reshape(2, blocks, 128).transpose(1, 0, 2).reshape(2 * blocks, 128)
    cell_ids = cells.reshape(2, blocks)
    sent_a, sent_b, cell_ids = pack_call(in_hbm(own_points), in_hbm(pose.reshape(1, 12)), in_hbm(cell_ids))
    pairs_a = [(i, i ^ 1) for i in range(lines)]
    pairs_b = [(i, (((i + 1) ^ 1) - 1) % lines) for i in range(lines)]
    margin_a = lax.ppermute(sent_a, "line", pairs_a)
    margin_b = lax.ppermute(sent_b, "line", pairs_b)
    source, part = partner_call(cell_ids, row_list, sent_a, sent_b, margin_a)
    sums = other_call(cell_ids, sent_a, source, part, margin_a, margin_b, lines * segs)
    everyone = exchange(sums)
    sums, result = second_call(cell_ids, sent_a, everyone, source, margin_a, margin_b, lines, segs)
    everyone = exchange(sums)
    fitted, spread = pl.pallas_call(
        functools.partial(last_kernel, segs),
        in_specs=vmem(1),
        out_specs=vmem(2),
        out_shape=[jax.ShapeDtypeStruct((1, 12), F32), jax.ShapeDtypeStruct((1, 1), F32)],
        compiler_params=PARAMS,
        name="solve_last",
    )(everyone)
    result = result.reshape(5, blocks, 2, 128).transpose(2, 0, 1, 3).reshape(1, 1, 2, 5, slots)
    return (result, fitted.reshape(12, 1), spread.reshape(1))


def solution(mesh):
    return jax.shard_map(
        functools.partial(on_device, mesh.shape["line"], mesh.shape["seg"]),
        mesh=mesh,
        in_specs=(
            P("line", "seg", None, None),
            P("line", "seg", None, None),
            P("line", "seg", None, None),
            P(None, "line"),
        ),
        out_specs=(P("line", "seg", None, None, None), P(None, "line"), P()),
        check_vma=False,
    )
```

```python
import functools
import math

import jax
import jax.numpy as jnp
from jax import lax
from jax.experimental import pallas as pl
from jax.experimental.pallas import tpu as pltpu
from jax.sharding import PartitionSpec as P

NCELL = 16
CT = 512
BLOCK = 128
MARGIN = NCELL * CT
MROWS = MARGIN // 128
TILES = CT // 128
GROUPS = BLOCK // 8
WIDE = 4
QUICK_LIMIT = 1000.0
ENERGY_LIMIT = 400.0

OUTLIER_MASS = 1.0
SPREAD_START = 0.05
PRIOR_TOP = 0.05
PRIOR_BOTTOM = 1.0
REGULARIZE = 1.0
LOG2E = math.log2(math.e)

F32 = jnp.float32
BF16 = jnp.bfloat16
TILE = (8, 128)
ONE = 24
SHARE = ONE + 3
ENERGY = ONE + 4
QUAD = 32
POSE = 64


def iota(axis):
    return lax.broadcasted_iota(jnp.int32, TILE, axis)


def spread_out(value):
    return jnp.broadcast_to(value, TILE)


def pack_kernel(points_hbm, pose_hbm, cells_hbm, sent_a, sent_b, cells_ref, pose_ref, sems):
    odd = lax.axis_index("line") & 1
    tail = points_hbm.shape[1] - MROWS
    copies = [
        pltpu.make_async_copy(pose_hbm, pose_ref, sems.at[6]),
        pltpu.make_async_copy(cells_hbm, cells_ref, sems.at[7]),
    ]
    for n, (sent, first) in enumerate(((sent_a, (1 - odd) * tail), (sent_b, odd * tail))):
        spot = pl.ds(pl.multiple_of(first, MROWS), MROWS)
        for k in range(3):
            copies.append(
                pltpu.make_async_copy(points_hbm.at[k, spot, :], sent.at[pl.ds(MROWS * k, MROWS), :], sems.at[3 * n + k])
            )
    for copy in copies:
        copy.start()
    for sent in (sent_a, sent_b):
        sent[3 * MROWS :, :] = jnp.zeros(TILE, F32)
    copies[0].wait()
    for sent in (sent_a, sent_b):
        sent[3 * MROWS : 3 * MROWS + 1, :12] = pose_ref[...]
    for copy in copies[1:]:
        copy.wait()


def pack_call(points, pose, cells):
    return pl.pallas_call(
        pack_kernel,
        in_specs=[HBM] * 3,
        out_specs=vmem(3),
        out_shape=[jax.ShapeDtypeStruct((3 * MROWS + 8, 128), F32)] * 2 + [jax.ShapeDtypeStruct(cells.shape, jnp.int32)],
        scratch_shapes=[pltpu.VMEM((1, 12), F32), pltpu.SemaphoreType.DMA((8,))],
        compiler_params=PARAMS,
        name="pack_margins",
    )(points, pose, cells)


def turn_margin(margin_ref, turned_ref):
    group = MROWS // 8
    for k in range(3):
        parts = [three_parts(margin_ref[MROWS * k + 8 * v : MROWS * k + 8 * v + 8, :]) for v in range(group)]
        stack = jnp.concatenate([parts[v][p] for p in range(3) for v in range(group)], axis=0)
        turned_ref[128 * k : 128 * k + 128, :] = jnp.transpose(stack).astype(BF16)


def pick_rows(rows_ref, turned_ref, rows):
    spots = [jnp.maximum(rows_ref[pl.ds(row, 1), :], 0) & (MARGIN - 1) for row in rows]
    hits = []
    for spot in spots:
        high = spread_out(spot >> 7)
        hit = [(high == iota(0) + 8 * v).astype(F32) for v in range(MROWS // 8)]
        hits.append(jnp.concatenate(hit, axis=0).astype(BF16))
    hit = jnp.concatenate(hits, axis=1)
    return spots, jnp.dot(turned_ref[...], jnp.concatenate([hit] * 3, axis=0), preferred_element_type=F32)


def pick_lanes(source_ref, rows, spots, picked):
    for n, row in enumerate(rows):
        low = spread_out(spots[n] & 127)
        sums = [jnp.zeros(TILE, F32)] * 3
        for v in range(16):
            here = low == iota(0) + 8 * v
            for k in range(3):
                part = picked[128 * k + 8 * v : 128 * k + 8 * v + 8, 128 * n : 128 * n + 128]
                sums[k] = jnp.where(here, part, sums[k])
        for k in range(3):
            source_ref[k, pl.ds(row, 1), :] = jnp.sum(sums[k], axis=0, keepdims=True)


def apply_pose(coefs, xyz):
    out = []
    for k in range(3):
        total = coefs[3 * k] * xyz[0]
        total = total + coefs[3 * k + 1] * xyz[1]
        total = total + coefs[3 * k + 2] * xyz[2]
        out.append(total + coefs[9 + k])
    return out


def column(coefs, first, stride):
    sub = iota(0)
    out = jnp.zeros(TILE, F32)
    for k in range(3):
        out = jnp.where(sub == k, coefs[first + stride * k], out)
    return out


def columns(coefs):
    return [column(coefs, k, 3) for k in range(3)] + [column(coefs, 9, 1)]


def squared_length(value):
    square = value * value
    return spread_out(square[0:1, :]) + spread_out(square[1:2, :]) + spread_out(square[2:3, :])


def three_parts(value):
    high = value.astype(BF16).astype(F32)
    rest = value - high
    middle = rest.astype(BF16).astype(F32)
    return high, middle, rest - middle


def combine(cols, xyz):
    return cols[0] * xyz[0] + cols[1] * xyz[1] + cols[2] * xyz[2]


def prepare(near, margin_ref, phi_ref, r):
    sub = iota(0)
    y = combine(near, [spread_out(margin_ref[k * MROWS + r : k * MROWS + r + 1, :]) for k in range(3)])
    length = squared_length(y)
    high, middle, low = three_parts(jnp.where(sub == 3, length, jnp.where(sub == 4, 1.0, y)))
    for i, pair in enumerate(((high, middle), (low, high), (middle, high))):
        phi_ref[16 * i : 16 * i + 16, 128 * r : 128 * r + 128] = jnp.concatenate(pair, axis=0).astype(BF16)
    return length


def longest_source(own, near, dirs, source_ref):
    longest = jnp.zeros(TILE, F32)
    for v in range(source_ref.shape[1] // 8):
        rows = slice(8 * v, 8 * v + 8)
        xyz = [source_ref[k, rows, :] for k in range(3)]
        moved = apply_pose(own, xyz)
        for side in range(2):
            square = sum((moved[k] - near[side][9 + k]) ** 2 for k in range(3))
            listed = (iota(0) & 1) == dirs[side]
            longest = jnp.maximum(longest, jnp.where(listed, square * source_ref[3, rows, :], 0.0))
    return longest


def coefficients(negc, own, near, source_ref, place):
    side, row, _ = place
    sub = iota(0)
    xt = [spread_out(source_ref[k, pl.ds(row, 1), :]) for k in range(4)]
    m = combine(own, xt) + (own[3] - near[side][3])
    length = squared_length(m)
    coef = jnp.where(sub == 3, negc, jnp.where(sub == 4, negc * length, (-2.0 * negc) * m))
    high, middle, low = three_parts(coef)
    stack = jnp.concatenate([high, high, high, middle, middle, low], axis=0)
    return jnp.transpose(stack).astype(BF16), xt, m, length


def weigh(phi_refs, place, coef):
    side, _, cell = place
    spot = pl.ds(pl.multiple_of(jnp.maximum(cell, 0) * CT, CT), CT)
    power = jnp.dot(coef, phi_refs[side][:, spot], preferred_element_type=F32)
    weight = jnp.transpose(jnp.exp2(power))
    top = weight.astype(BF16)
    rest = (weight - top.astype(F32)).astype(BF16)
    return phi_refs[side][:32, spot], jnp.concatenate([top, rest], axis=1)


def weighted_sums(features, weights):
    sums = jnp.dot(features, weights, preferred_element_type=F32)
    sums = sums[:, :BLOCK] + sums[:, BLOCK:]
    return sums[0:8] + sums[8:16] + sums[16:24]


def finish(near, side, xt, m, length, sums):
    sub = iota(0)
    total = spread_out(sums[4:5, :])
    around = combine([spread_out(m[k : k + 1, :]) for k in range(3)], [spread_out(sums[k : k + 1, :]) for k in range(3)])
    energy = spread_out(sums[3:4, :]) - 2.0 * around + length * total
    raw = jnp.where(sub < 3, sums + near[side][3] * total, jnp.where(sub == 3, total, jnp.where(sub == 4, energy, 0.0)))
    return raw * (xt[3] / (total + OUTLIER_MASS)), xt


class Lists:
    def __init__(self, cells_hbm, source_ref, margin_refs, scratch_refs):
        self.dirs = sides_of(lax.axis_index("line"))
        self.source_ref = source_ref
        self.margin_refs = margin_refs
        self.cells_ref, cells_sem = scratch_refs[:2]
        self.phi_refs = scratch_refs[2:4]
        self.world_ref, self.moved_ref, self.column_ref = scratch_refs[4:7]
        self.fetch = pltpu.make_async_copy(cells_hbm, self.cells_ref, cells_sem)
        self.fetch.start()

    def places(self, side):
        d = self.dirs[side]
        return [(side, 2 * b + d, self.cells_ref[d, b]) for b in range(self.cells_ref.shape[1])]


def quick(lists, own, nbrs, negc, sides, carry, longest, out_ref):
    own_cols, near_cols = columns(own), {side: columns(nbrs[side]) for side in sides}
    longest = [longest]

    def features(side, rows):
        for r in rows:
            length = prepare(near_cols[side], lists.margin_refs[side], lists.phi_refs[side], r)
            longest[0] = jnp.maximum(longest[0], length)

    features(sides[0], range(MROWS))
    lists.fetch.wait()
    places = [place for side in sides for place in lists.places(side)]
    each = -(-MROWS // max(1, len(places) // len(sides) - 2))
    coefs = [coefficients(negc, own_cols, near_cols, lists.source_ref, place) for place in places]
    found = []
    ahead = None
    for n in range(-1, len(places)):
        block, ahead = ahead, None
        if n + 1 < len(places):
            ahead = weigh(lists.phi_refs, places[n + 1], coefs[n + 1][0])
        for side in sides[1:]:
            features(side, range(min((n + 1) * each, MROWS), min((n + 2) * each, MROWS)))
        if block is not None:
            found.append(weighted_sums(*block))
    for (side, row, _), (_, xt, m, length), sums in zip(places, coefs, found):
        result, xt = finish(near_cols, side, xt, m, length, sums)
        carry = add_block(carry, row, result, xt, out_ref)
    return carry, longest[0]


def no_sums():
    return [jnp.zeros(TILE, F32) for _ in range(5)]


def close(lists, own, nbrs, negc, carry, longest, pose_row, sums_ref, out):
    out_ref = None if out is None else out[1]
    if out is not None:
        save = pltpu.make_async_copy(out[1], out[0], out[2])
        save.start()
    pack_sums(carry, pose_row, sums_ref)
    size = spread_out(jnp.max(longest)) + spread_out(jnp.max(longest_source(own, nbrs, lists.dirs, lists.source_ref)))
    whole = jnp.sum(carry[3], axis=1, keepdims=True)
    share, energy = [spread_out(whole[q : q + 1, :]) for q in (3, 4)]
    bad = (size * -negc > QUICK_LIMIT) | (size * share > ENERGY_LIMIT * energy)

    @pl.when(jnp.max(bad.astype(F32)) > 0.0)
    def _():
        if out is not None:
            save.wait()
        one_block = careful_setup(
            own, nbrs, negc, lists.source_ref, lists.margin_refs, lists.world_ref, lists.moved_ref, lists.column_ref
        )
        carry = tuple(no_sums())
        for side in range(2):
            d = lists.dirs[side]

            def step(b, carry, side=side, d=d):
                result, xt = one_block(side, 2 * b + d, lists.cells_ref[d, b])
                return tuple(add_block(carry, 2 * b + d, result, xt, out_ref))

            carry = lax.fori_loop(0, lists.cells_ref.shape[1], step, carry)
        pack_sums(carry, pose_row, sums_ref)
        if out is not None:
            save.start()

    if out is not None:
        save.wait()


def add_block(carry, row, result, xt, out_ref):
    sub = iota(0)
    if out_ref is not None:
        for q in range(5):
            out_ref[q, pl.ds(row, 1), :] = result[q : q + 1, :]
    left = jnp.where(sub < 3, xt[0], jnp.where(sub < 5, xt[1], xt[2]))
    right = jnp.where(sub == 0, xt[0], jnp.where((sub == 1) | (sub == 3), xt[1], xt[2]))
    share = spread_out(result[3:4, :])
    return [
        carry[0] + result * xt[0],
        carry[1] + result * xt[1],
        carry[2] + result * xt[2],
        carry[3] + result,
        carry[4] + share * (left * right),
    ]


def careful_setup(own, nbrs, negc, source_ref, margin_refs, world_ref, moved_ref, column_ref):
    slot_rows = source_ref.shape[1]
    for v in range(slot_rows // 8):
        xyz = [source_ref[k, 8 * v : 8 * v + 8, :] for k in range(3)]
        for k, value in enumerate(apply_pose(own, xyz)):
            moved_ref[k, 8 * v : 8 * v + 8, :] = value
    for k in range(3):
        column_ref[k] = jnp.transpose(moved_ref[k])
    for side in range(2):
        for v in range(MROWS // 8):
            xyz = [margin_refs[side][k * MROWS + 8 * v : k * MROWS + 8 * v + 8, :] for k in range(3)]
            for k, value in enumerate(apply_pose(nbrs[side], xyz)):
                world_ref[side, k, 8 * v : 8 * v + 8, :] = value
    lane = iota(1)

    def one_block(side, row, cell):
        first = jnp.maximum(cell, 0) * TILES
        target = [
            [spread_out(world_ref[side, k, pl.ds(first + t, 1), :]) for t in range(TILES)] for k in range(3)
        ]
        pick = jnp.full(TILE, row, jnp.int32)
        parts = []
        for g in range(GROUPS):
            m = [
                jnp.take_along_axis(column_ref[k, 8 * g : 8 * g + 8, :], pick, axis=1, mode="promise_in_bounds")
                for k in range(3)
            ]
            sums = None
            for t in range(TILES):
                d = [m[k] - target[k][t] for k in range(3)]
                dist = d[0] * d[0] + d[1] * d[1] + d[2] * d[2]
                weight = jnp.exp2(dist * negc)
                terms = [weight * target[k][t] for k in range(3)] + [weight, weight * dist]
                sums = terms if sums is None else [a + b for a, b in zip(sums, terms)]
            part = jnp.zeros(TILE, F32)
            for q in range(5):
                part = jnp.where(lane == q, jnp.sum(sums[q], axis=1, keepdims=True), part)
            parts.append(part)
        flat = jnp.transpose(jnp.concatenate(parts, axis=0))[:8, :]
        xt = [spread_out(source_ref[k, pl.ds(row, 1), :]) for k in range(4)]
        return flat * (xt[3] / (spread_out(flat[3:4, :]) + OUTLIER_MASS)), xt

    return one_block


def pack_sums(sums, pose_row, out_ref):
    lane, sub = iota(1), iota(0)
    total = jnp.zeros(TILE, F32)
    for c in range(5):
        total = total + jnp.where(lane == 8 * c + sub, jnp.sum(sums[c], axis=1, keepdims=True), 0.0)
    row = jnp.sum(total, axis=0, keepdims=True)
    out_ref[...] = jnp.broadcast_to(row + pose_row, out_ref.shape)


def pose_of_row(row):
    return [spread_out(row[:, j : j + 1]) for j in range(12)]


def sides_of(line):
    odd = line & 1
    return [1 - odd, odd]


def pose_in(margin_ref):
    return pose_of_row(margin_ref[3 * MROWS : 3 * MROWS + 1, :])


def gather_kernel(rows_ref, sent_a, sent_b, source_ref, turned_a, turned_b):
    dirs = sides_of(lax.axis_index("line"))
    slot_rows = rows_ref.shape[0]
    blocks = slot_rows // 2
    for v in range(slot_rows // 8):
        source_ref[3, 8 * v : 8 * v + 8, :] = (rows_ref[8 * v : 8 * v + 8, :] >= 0).astype(F32)
    turn_margin(sent_a, turned_a)
    turn_margin(sent_b, turned_b)
    last = None
    for side, turned_ref in enumerate((turned_a, turned_b)):
        for first in range(0, blocks, WIDE):
            rows = [2 * b + dirs[side] for b in range(first, min(first + WIDE, blocks))]
            found = rows, *pick_rows(rows_ref, turned_ref, rows)
            if last is not None:
                pick_lanes(source_ref, *last)
            last = found
    pick_lanes(source_ref, *last)


def partner_kernel(cells_hbm, sent_a, source_ref, margin_a, part_ref, *scratch_refs):
    lists = Lists(cells_hbm, source_ref, (margin_a, None), scratch_refs)
    nothing = jnp.zeros(TILE, F32)
    carry, longest = quick(lists, pose_in(sent_a), [pose_in(margin_a)], first_negc(), [0], no_sums(), nothing, None)
    for n, value in enumerate(carry + [longest]):
        part_ref[n] = value


def other_kernel(cells_hbm, sent_a, source_ref, part_ref, margin_a, margin_b, sums_ref, *scratch_refs):
    lists = Lists(cells_hbm, source_ref, (margin_a, margin_b), scratch_refs)
    own = pose_in(sent_a)
    nbrs = [pose_in(margin) for margin in (margin_a, margin_b)]
    part = [part_ref[n] for n in range(6)]
    carry, longest = quick(lists, own, nbrs, first_negc(), [1], part[:5], part[5], None)
    close(lists, own, nbrs, first_negc(), carry, longest, 0.0, sums_ref, None)


def first_negc():
    return jnp.full(TILE, -LOG2E / (2.0 * SPREAD_START), F32)


def solve(totals, old):
    def at(q):
        return spread_out(totals[:, q : q + 1])

    gram = {}
    for n, (a, b) in enumerate([(0, 0), (0, 1), (0, 2), (1, 1), (1, 2), (2, 2)]):
        gram[a, b] = at(QUAD + n)
    for a in range(3):
        gram[a, 3] = at(8 * a + 3)
    gram[3, 3] = at(SHARE)
    for a in range(4):
        gram[a, a] = gram[a, a] + REGULARIZE
    lower, diag, inverse = {}, [], []
    for j in range(4):
        scaled = [lower[j, k] * diag[k] for k in range(j)]
        pivot = gram[j, j]
        for k in range(j):
            pivot = pivot - lower[j, k] * scaled[k]
        diag.append(pivot)
        inverse.append(1.0 / pivot)
        for i in range(j + 1, 4):
            value = gram[j, i]
            for k in range(j):
                value = value - lower[i, k] * scaled[k]
            lower[i, j] = value * inverse[j]
    new = [None] * 12
    for k in range(3):
        right = []
        for m in range(4):
            j = 3 * k + m if m < 3 else 9 + k
            value = at(8 * m + k) + REGULARIZE * spread_out(old[:, j : j + 1])
            for n in range(m):
                value = value - lower[m, n] * right[n]
            right.append(value)
        found = [None] * 4
        for m in reversed(range(4)):
            value = right[m] * inverse[m]
            for n in range(m + 1, 4):
                value = value - lower[n, m] * found[n]
            found[m] = value
        for m in range(4):
            new[3 * k + m if m < 3 else 9 + k] = found[m]
    return new


def line_sum(all_ref, line, segs):
    return jnp.sum(all_ref[pl.ds(line * segs, segs), :], axis=0, keepdims=True)


def new_spread(all_ref):
    everything = jnp.sum(all_ref[...], axis=0, keepdims=True)
    top = spread_out(everything[:, ENERGY : ENERGY + 1]) + PRIOR_TOP
    return top / (3.0 * spread_out(everything[:, SHARE : SHARE + 1]) + PRIOR_BOTTOM)


def pose_row(new, first):
    lane = lax.broadcasted_iota(jnp.int32, (1, 128), 1)
    row = jnp.zeros((1, 128), F32)
    for j in range(12):
        row = jnp.where(lane == first + j, new[j][:1, :], row)
    return row


def second_kernel(
    lines, segs, cells_hbm, sent_a, all_ref, source_ref, margin_a, margin_b,
    sums_ref, out_hbm, out_ref, out_sem, *scratch_refs,
):
    line = lax.axis_index("line")
    lists = Lists(cells_hbm, source_ref, (margin_a, margin_b), scratch_refs)
    partner = [jnp.clip(line + 2 * d - 1, 0, lines - 1) for d in lists.dirs]
    sub = iota(0)

    def stacked(a, b, c):
        return jnp.where(sub == 0, spread_out(a), jnp.where(sub == 1, spread_out(b), spread_out(c)))

    totals = stacked(*[line_sum(all_ref, n, segs) for n in (line, partner[0], partner[1])])
    old = stacked(*[ref[3 * MROWS : 3 * MROWS + 1, :] for ref in (sent_a, margin_a, margin_b)])
    new = solve(totals, old)
    negc = (-0.5 * LOG2E) / new_spread(all_ref)
    own, *nbrs = [[spread_out(value[n : n + 1, :]) for value in new] for n in range(3)]
    carry, longest = quick(lists, own, nbrs, negc, [0, 1], no_sums(), jnp.zeros(TILE, F32), out_ref)
    close(lists, own, nbrs, negc, carry, longest, pose_row(new, POSE), sums_ref, (out_hbm, out_ref, out_sem))


def last_kernel(segs, all_ref, fitted_ref, spread_ref):
    line = lax.axis_index("line")
    totals = spread_out(line_sum(all_ref, line, segs))
    old = all_ref[pl.ds(line * segs, 1), :][:, POSE : POSE + 12]
    new = solve(totals, jnp.broadcast_to(old, (8, 12)))
    fitted_ref[...] = pose_row(new, 0)[:, :12]
    spread_ref[...] = new_spread(all_ref)[:1, :1]


def vmem(count):
    return [pl.BlockSpec(memory_space=pltpu.VMEM)] * count


ANY = pl.BlockSpec(memory_space=pl.ANY)
HBM = pl.BlockSpec(memory_space=pltpu.HBM)
PARAMS = pltpu.CompilerParams(vmem_limit_bytes=32 * 1024 * 1024)


def scratch(cells):
    return [
        pltpu.SMEM(cells.shape, jnp.int32),
        pltpu.SemaphoreType.DMA,
        pltpu.VMEM((48, MARGIN), BF16),
        pltpu.VMEM((48, MARGIN), BF16),
        pltpu.VMEM((2, 3, MROWS, 128), F32),
        pltpu.VMEM((3, 128, 128), F32),
        pltpu.VMEM((3, 128, 128), F32),
    ]


def in_hbm(value):
    return pltpu.with_memory_space_constraint(value, pltpu.HBM)


def pair_cost(cells, sides):
    pairs = cells.size // 2 * sides * BLOCK * CT
    return pl.CostEstimate(flops=400 * pairs, bytes_accessed=1 << 20, transcendentals=pairs)


def gather_call(rows, sent_a, sent_b):
    return pl.pallas_call(
        gather_kernel,
        in_specs=vmem(3),
        out_specs=vmem(1)[0],
        out_shape=jax.ShapeDtypeStruct((4,) + rows.shape, F32),
        scratch_shapes=[pltpu.VMEM((3 * 128, 3 * MROWS), BF16)] * 2,
        compiler_params=PARAMS,
        cost_estimate=pl.CostEstimate(flops=10**9, bytes_accessed=1 << 20, transcendentals=0),
        name="gather_sources",
    )(rows, sent_a, sent_b)


def partner_call(cells, sent_a, source, margin_a):
    return pl.pallas_call(
        partner_kernel,
        in_specs=[ANY] + vmem(3),
        out_specs=vmem(1)[0],
        out_shape=jax.ShapeDtypeStruct((6,) + TILE, F32),
        scratch_shapes=scratch(cells),
        compiler_params=PARAMS,
        cost_estimate=pair_cost(cells, 1),
        name="match_partner",
    )(cells, sent_a, source, margin_a)


def other_call(cells, sent_a, source, part, margin_a, margin_b, devices):
    return pl.pallas_call(
        other_kernel,
        in_specs=[ANY] + vmem(5),
        out_specs=vmem(1)[0],
        out_shape=jax.ShapeDtypeStruct((devices, 128), F32),
        scratch_shapes=scratch(cells),
        compiler_params=PARAMS,
        cost_estimate=pair_cost(cells, 1),
        name="match_other",
    )(cells, sent_a, source, part, margin_a, margin_b)


def second_call(cells, sent_a, everyone, source, margin_a, margin_b, lines, segs):
    result = (5,) + source.shape[1:]
    return pl.pallas_call(
        functools.partial(second_kernel, lines, segs),
        in_specs=[ANY] + vmem(5),
        out_specs=vmem(1) + [ANY],
        out_shape=[jax.ShapeDtypeStruct((lines * segs, 128), F32), jax.ShapeDtypeStruct(result, F32)],
        scratch_shapes=[pltpu.VMEM(result, F32), pltpu.SemaphoreType.DMA] + scratch(cells),
        compiler_params=PARAMS,
        cost_estimate=pair_cost(cells, 2),
        name="match_second",
    )(cells, sent_a, everyone, source, margin_a, margin_b)


def exchange(sums):
    return lax.all_to_all(sums, ("line", "seg"), 0, 0)


def on_device(lines, segs, points, rows, cells, pose):
    own_points = points.reshape(3, -1, 128)
    slots = rows.shape[-1]
    blocks = slots // BLOCK
    row_list = rows.reshape(2, blocks, 128).transpose(1, 0, 2).reshape(2 * blocks, 128)
    cell_ids = cells.reshape(2, blocks)
    sent_a, sent_b, cell_ids = pack_call(in_hbm(own_points), in_hbm(pose.reshape(1, 12)), in_hbm(cell_ids))
    pairs_a = [(i, i ^ 1) for i in range(lines)]
    pairs_b = [(i, (((i + 1) ^ 1) - 1) % lines) for i in range(lines)]
    margin_a = lax.ppermute(sent_a, "line", pairs_a)
    margin_b = lax.ppermute(sent_b, "line", pairs_b)
    source = gather_call(row_list, sent_a, sent_b)
    part = partner_call(cell_ids, sent_a, source, margin_a)
    sums = other_call(cell_ids, sent_a, source, part, margin_a, margin_b, lines * segs)
    everyone = exchange(sums)
    sums, result = second_call(cell_ids, sent_a, everyone, source, margin_a, margin_b, lines, segs)
    everyone = exchange(sums)
    fitted, spread = pl.pallas_call(
        functools.partial(last_kernel, segs),
        in_specs=vmem(1),
        out_specs=vmem(2),
        out_shape=[jax.ShapeDtypeStruct((1, 12), F32), jax.ShapeDtypeStruct((1, 1), F32)],
        compiler_params=PARAMS,
        name="solve_last",
    )(everyone)
    result = result.reshape(5, blocks, 2, 128).transpose(2, 0, 1, 3).reshape(1, 1, 2, 5, slots)
    return (result, fitted.reshape(12, 1), spread.reshape(1))


def solution(mesh):
    return jax.shard_map(
        functools.partial(on_device, mesh.shape["line"], mesh.shape["seg"]),
        mesh=mesh,
        in_specs=(
            P("line", "seg", None, None),
            P("line", "seg", None, None),
            P("line", "seg", None, None),
            P(None, "line"),
        ),
        out_specs=(P("line", "seg", None, None, None), P(None, "line"), P()),
        check_vma=False,
    )
```

```python
import functools
import math

import jax
import jax.numpy as jnp
from jax import lax
from jax.experimental import pallas as pl
from jax.experimental.pallas import tpu as pltpu
from jax.sharding import PartitionSpec as P

NCELL = 16
CT = 512
BLOCK = 128
MARGIN = NCELL * CT
MROWS = MARGIN // 128
TILES = CT // 128
GROUPS = BLOCK // 8
LEAD = 48
LAG = 3
WIDE = 4
QUICK_LIMIT = 1000.0
ENERGY_LIMIT = 400.0

OUTLIER_MASS = 1.0
SPREAD_START = 0.05
PRIOR_TOP = 0.05
PRIOR_BOTTOM = 1.0
REGULARIZE = 1.0
LOG2E = math.log2(math.e)

F32 = jnp.float32
BF16 = jnp.bfloat16
TILE = (8, 128)
ONE = 24
SHARE = ONE + 3
ENERGY = ONE + 4
QUAD = 32
POSE = 64


def iota(axis):
    return lax.broadcasted_iota(jnp.int32, TILE, axis)


def spread_out(value):
    return jnp.broadcast_to(value, TILE)


def pack_kernel(points_hbm, pose_hbm, cells_hbm, sent_a, sent_b, cells_ref, pose_ref, sems):
    odd = lax.axis_index("line") & 1
    tail = points_hbm.shape[1] - MROWS
    copies = [
        pltpu.make_async_copy(pose_hbm, pose_ref, sems.at[6]),
        pltpu.make_async_copy(cells_hbm, cells_ref, sems.at[7]),
    ]
    for n, (sent, first) in enumerate(((sent_a, (1 - odd) * tail), (sent_b, odd * tail))):
        spot = pl.ds(pl.multiple_of(first, MROWS), MROWS)
        for k in range(3):
            copies.append(
                pltpu.make_async_copy(points_hbm.at[k, spot, :], sent.at[pl.ds(MROWS * k, MROWS), :], sems.at[3 * n + k])
            )
    for copy in copies:
        copy.start()
    for sent in (sent_a, sent_b):
        sent[3 * MROWS :, :] = jnp.zeros(TILE, F32)
    copies[0].wait()
    for sent in (sent_a, sent_b):
        sent[3 * MROWS : 3 * MROWS + 1, :12] = pose_ref[...]
    for copy in copies[1:]:
        copy.wait()


def pack_call(points, pose, cells):
    return pl.pallas_call(
        pack_kernel,
        in_specs=[HBM] * 3,
        out_specs=vmem(2) + [SMEM],
        out_shape=[jax.ShapeDtypeStruct((3 * MROWS + 8, 128), F32)] * 2 + [pltpu.SMEM(cells.shape, jnp.int32)],
        scratch_shapes=[pltpu.VMEM((1, 12), F32), pltpu.SemaphoreType.DMA((8,))],
        compiler_params=PARAMS,
        name="pack_margins",
    )(points, pose, cells)


def pick_columns(rows_ref, margin_parts, rows):
    spots = [jnp.maximum(rows_ref[pl.ds(row, 1), :], 0) & (MARGIN - 1) for row in rows]
    hits = []
    for spot in spots:
        low = spread_out(spot & 127)
        hit = [(low == iota(0) + 8 * v).astype(F32) for v in range(16)]
        hits.append(jnp.concatenate(hit, axis=0).astype(BF16))
    hit = jnp.concatenate(hits, axis=1)
    return spots, jnp.dot(margin_parts, jnp.concatenate([hit] * 3, axis=0), preferred_element_type=F32)


def pick_rows(source_ref, rows, spots, picked):
    for n, row in enumerate(rows):
        high = spread_out(spots[n] >> 7)
        sums = [jnp.zeros(TILE, F32)] * 3
        for v in range(MROWS // 8):
            here = high == iota(0) + 8 * v
            for k in range(3):
                first = MROWS * k + 8 * v
                sums[k] = jnp.where(here, picked[first : first + 8, 128 * n : 128 * n + 128], sums[k])
        for k in range(3):
            source_ref[k, pl.ds(row, 1), :] = jnp.sum(sums[k], axis=0, keepdims=True)


def apply_pose(coefs, xyz):
    out = []
    for k in range(3):
        total = coefs[3 * k] * xyz[0]
        total = total + coefs[3 * k + 1] * xyz[1]
        total = total + coefs[3 * k + 2] * xyz[2]
        out.append(total + coefs[9 + k])
    return out


def column(coefs, first, stride):
    sub = iota(0)
    out = jnp.zeros(TILE, F32)
    for k in range(3):
        out = jnp.where(sub == k, coefs[first + stride * k], out)
    return out


def columns(coefs):
    return [column(coefs, k, 3) for k in range(3)] + [column(coefs, 9, 1)]


def squared_length(value):
    square = value * value
    return spread_out(square[0:1, :]) + spread_out(square[1:2, :]) + spread_out(square[2:3, :])


def three_parts(value):
    high = value.astype(BF16).astype(F32)
    rest = value - high
    middle = rest.astype(BF16).astype(F32)
    return high, middle, rest - middle


def combine(cols, xyz):
    return cols[0] * xyz[0] + cols[1] * xyz[1] + cols[2] * xyz[2]


def prepare(near, margin_ref, phi_ref, r):
    sub = iota(0)
    y = combine(near, [spread_out(margin_ref[k * MROWS + r : k * MROWS + r + 1, :]) for k in range(3)])
    length = squared_length(y)
    high, middle, low = three_parts(jnp.where(sub == 3, length, jnp.where(sub == 4, 1.0, y)))
    for i, pair in enumerate(((high, middle), (low, high), (middle, high))):
        phi_ref[16 * i : 16 * i + 16, 128 * r : 128 * r + 128] = jnp.concatenate(pair, axis=0).astype(BF16)
    return length


def longest_source(own, near, dirs, source_ref):
    longest = jnp.zeros(TILE, F32)
    for v in range(source_ref.shape[1] // 8):
        rows = slice(8 * v, 8 * v + 8)
        xyz = [source_ref[k, rows, :] for k in range(3)]
        moved = apply_pose(own, xyz)
        for side in range(2):
            square = sum((moved[k] - near[side][9 + k]) ** 2 for k in range(3))
            listed = (iota(0) & 1) == dirs[side]
            longest = jnp.maximum(longest, jnp.where(listed, square * source_ref[3, rows, :], 0.0))
    return longest


def coefficients(negc, own, near, source_ref, place):
    side, row, _ = place
    sub = iota(0)
    xt = [spread_out(source_ref[k, pl.ds(row, 1), :]) for k in range(4)]
    m = combine(own, xt) + (own[3] - near[side][3])
    length = squared_length(m)
    coef = jnp.where(sub == 3, negc, jnp.where(sub == 4, negc * length, (-2.0 * negc) * m))
    high, middle, low = three_parts(coef)
    stack = jnp.concatenate([high, high, high, middle, middle, low], axis=0)
    return jnp.transpose(stack).astype(BF16), xt, m, length


def weigh(phi_refs, side, cell, coef):
    spot = pl.ds(pl.multiple_of(jnp.maximum(cell, 0) * CT, CT), CT)
    power = jnp.dot(coef, phi_refs[side][:, spot], preferred_element_type=F32)
    weight = jnp.transpose(jnp.exp2(power))
    top = weight.astype(BF16)
    rest = (weight - top.astype(F32)).astype(BF16)
    return phi_refs[side][:32, spot], jnp.concatenate([top, rest], axis=1)


def weighted_sums(features, weights):
    sums = jnp.dot(features, weights, preferred_element_type=F32)
    sums = sums[:, :BLOCK] + sums[:, BLOCK:]
    return sums[0:8] + sums[8:16] + sums[16:24]


def finish(near, side, xt, m, length, sums):
    sub = iota(0)
    total = spread_out(sums[4:5, :])
    around = combine([spread_out(m[k : k + 1, :]) for k in range(3)], [spread_out(sums[k : k + 1, :]) for k in range(3)])
    energy = spread_out(sums[3:4, :]) - 2.0 * around + length * total
    raw = jnp.where(sub < 3, sums + near[side][3] * total, jnp.where(sub == 3, total, jnp.where(sub == 4, energy, 0.0)))
    return raw * (xt[3] / (total + OUTLIER_MASS)), xt


class Lists:
    def __init__(self, cells_ref, source_ref, margin_refs, scratch_refs):
        self.dirs = sides_of(lax.axis_index("line"))
        self.source_ref = source_ref
        self.margin_refs = margin_refs
        self.cells_ref = cells_ref
        self.phi_refs = scratch_refs[:2]
        self.world_ref, self.moved_ref, self.column_ref = scratch_refs[2:5]

    def places(self, side):
        return [(side, 2 * b + self.dirs[side], b) for b in range(self.cells_ref.shape[1])]

    def cell(self, place):
        side, _, b = place
        return self.cells_ref[self.dirs[side], b]


def quick(lists, own, nbrs, negc, sides, carry, longest, out_ref):
    own_cols, near_cols = columns(own), {side: columns(nbrs[side]) for side in sides}
    longest = [longest]

    def features(side, rows):
        for r in rows:
            length = prepare(near_cols[side], lists.margin_refs[side], lists.phi_refs[side], r)
            longest[0] = jnp.maximum(longest[0], length)

    features(sides[0], range(MROWS))
    places = [place for side in sides for place in lists.places(side)]
    each = -(-MROWS // max(1, len(places) // len(sides) - 2))
    coefs, found = {}, {}
    ahead = None
    for n in range(-1, len(places) + LAG):
        block, ahead = ahead, None
        for later in range(0 if n < 0 else n + 1 + LEAD, min(n + 2 + LEAD, len(places))):
            coefs[later] = coefficients(negc, own_cols, near_cols, lists.source_ref, places[later])
        if n + 1 < len(places):
            ahead = weigh(lists.phi_refs, places[n + 1][0], lists.cell(places[n + 1]), coefs[n + 1][0])
        for side in sides[1:]:
            features(side, range(min((n + 1) * each, MROWS), min((n + 2) * each, MROWS)))
        if block is not None:
            found[n] = weighted_sums(*block)
        if n >= LAG:
            side, row, _ = places[n - LAG]
            result, xt = finish(near_cols, side, *coefs[n - LAG][1:], found[n - LAG])
            carry = add_block(carry, row, result, xt, out_ref)
    return carry, longest[0]


def no_sums():
    return [jnp.zeros(TILE, F32) for _ in range(5)]


def close(lists, own, nbrs, negc, carry, longest, pose_row, sums_ref, out):
    out_ref = None if out is None else out[1]
    if out is not None:
        save = pltpu.make_async_copy(out[1], out[0], out[2])
        save.start()
    pack_sums(carry, pose_row, sums_ref)
    size = jnp.max(longest) + jnp.max(longest_source(own, nbrs, lists.dirs, lists.source_ref))
    share, energy = [jnp.sum(carry[3][q : q + 1, :]) for q in (3, 4)]
    bad = (size * jnp.max(-negc) > QUICK_LIMIT) | (size * share > ENERGY_LIMIT * energy)

    @pl.when(bad)
    def _():
        if out is not None:
            save.wait()
        one_block = careful_setup(
            own, nbrs, negc, lists.source_ref, lists.margin_refs, lists.world_ref, lists.moved_ref, lists.column_ref
        )
        carry = tuple(no_sums())
        for side in range(2):
            d = lists.dirs[side]

            def step(b, carry, side=side, d=d):
                result, xt = one_block(side, 2 * b + d, lists.cells_ref[d, b])
                return tuple(add_block(carry, 2 * b + d, result, xt, out_ref))

            carry = lax.fori_loop(0, lists.cells_ref.shape[1], step, carry)
        pack_sums(carry, pose_row, sums_ref)
        if out is not None:
            save.start()

    if out is not None:
        save.wait()


def add_block(carry, row, result, xt, out_ref):
    sub = iota(0)
    if out_ref is not None:
        for q in range(5):
            out_ref[q, pl.ds(row, 1), :] = result[q : q + 1, :]
    left = jnp.where(sub < 3, xt[0], jnp.where(sub < 5, xt[1], xt[2]))
    right = jnp.where(sub == 0, xt[0], jnp.where((sub == 1) | (sub == 3), xt[1], xt[2]))
    share = spread_out(result[3:4, :])
    return [
        carry[0] + result * xt[0],
        carry[1] + result * xt[1],
        carry[2] + result * xt[2],
        carry[3] + result,
        carry[4] + share * (left * right),
    ]


def careful_setup(own, nbrs, negc, source_ref, margin_refs, world_ref, moved_ref, column_ref):
    slot_rows = source_ref.shape[1]
    for v in range(slot_rows // 8):
        xyz = [source_ref[k, 8 * v : 8 * v + 8, :] for k in range(3)]
        for k, value in enumerate(apply_pose(own, xyz)):
            moved_ref[k, 8 * v : 8 * v + 8, :] = value
    for k in range(3):
        column_ref[k] = jnp.transpose(moved_ref[k])
    for side in range(2):
        for v in range(MROWS // 8):
            xyz = [margin_refs[side][k * MROWS + 8 * v : k * MROWS + 8 * v + 8, :] for k in range(3)]
            for k, value in enumerate(apply_pose(nbrs[side], xyz)):
                world_ref[side, k, 8 * v : 8 * v + 8, :] = value
    lane = iota(1)

    def one_block(side, row, cell):
        first = jnp.maximum(cell, 0) * TILES
        target = [
            [spread_out(world_ref[side, k, pl.ds(first + t, 1), :]) for t in range(TILES)] for k in range(3)
        ]
        pick = jnp.full(TILE, row, jnp.int32)
        parts = []
        for g in range(GROUPS):
            m = [
                jnp.take_along_axis(column_ref[k, 8 * g : 8 * g + 8, :], pick, axis=1, mode="promise_in_bounds")
                for k in range(3)
            ]
            sums = None
            for t in range(TILES):
                d = [m[k] - target[k][t] for k in range(3)]
                dist = d[0] * d[0] + d[1] * d[1] + d[2] * d[2]
                weight = jnp.exp2(dist * negc)
                terms = [weight * target[k][t] for k in range(3)] + [weight, weight * dist]
                sums = terms if sums is None else [a + b for a, b in zip(sums, terms)]
            part = jnp.zeros(TILE, F32)
            for q in range(5):
                part = jnp.where(lane == q, jnp.sum(sums[q], axis=1, keepdims=True), part)
            parts.append(part)
        flat = jnp.transpose(jnp.concatenate(parts, axis=0))[:8, :]
        xt = [spread_out(source_ref[k, pl.ds(row, 1), :]) for k in range(4)]
        return flat * (xt[3] / (spread_out(flat[3:4, :]) + OUTLIER_MASS)), xt

    return one_block


def pack_sums(sums, pose_row, out_ref):
    lane, sub = iota(1), iota(0)
    total = jnp.zeros(TILE, F32)
    for c in range(5):
        total = total + jnp.where(lane == 8 * c + sub, jnp.sum(sums[c], axis=1, keepdims=True), 0.0)
    row = jnp.sum(total, axis=0, keepdims=True)
    out_ref[...] = jnp.broadcast_to(row + pose_row, out_ref.shape)


def pose_of_row(row):
    return [spread_out(row[:, j : j + 1]) for j in range(12)]


def sides_of(line):
    odd = line & 1
    return [1 - odd, odd]


def pose_in(margin_ref):
    return pose_of_row(margin_ref[3 * MROWS : 3 * MROWS + 1, :])


def gather_kernel(rows_ref, sent_a, sent_b, source_ref):
    dirs = sides_of(lax.axis_index("line"))
    slot_rows = rows_ref.shape[0]
    blocks = slot_rows // 2
    for v in range(slot_rows // 8):
        source_ref[3, 8 * v : 8 * v + 8, :] = (rows_ref[8 * v : 8 * v + 8, :] >= 0).astype(F32)
    last = None
    for side, sent in enumerate((sent_a, sent_b)):
        parts = jnp.concatenate(three_parts(sent[: 3 * MROWS, :]), axis=1).astype(BF16)
        for first in range(0, blocks, WIDE):
            rows = [2 * b + dirs[side] for b in range(first, min(first + WIDE, blocks))]
            found = rows, *pick_columns(rows_ref, parts, rows)
            if last is not None:
                pick_rows(source_ref, *last)
            last = found
    pick_rows(source_ref, *last)


def partner_kernel(cells_hbm, sent_a, source_ref, margin_a, part_ref, *scratch_refs):
    lists = Lists(cells_hbm, source_ref, (margin_a, None), scratch_refs)
    nothing = jnp.zeros(TILE, F32)
    carry, longest = quick(lists, pose_in(sent_a), [pose_in(margin_a)], first_negc(), [0], no_sums(), nothing, None)
    for n, value in enumerate(carry + [longest]):
        part_ref[n] = value


def other_kernel(cells_hbm, sent_a, source_ref, part_ref, margin_a, margin_b, sums_ref, *scratch_refs):
    lists = Lists(cells_hbm, source_ref, (margin_a, margin_b), scratch_refs)
    own = pose_in(sent_a)
    nbrs = [pose_in(margin) for margin in (margin_a, margin_b)]
    part = [part_ref[n] for n in range(6)]
    carry, longest = quick(lists, own, nbrs, first_negc(), [1], part[:5], part[5], None)
    close(lists, own, nbrs, first_negc(), carry, longest, 0.0, sums_ref, None)


def first_negc():
    return jnp.full(TILE, -LOG2E / (2.0 * SPREAD_START), F32)


def solve(totals, old):
    def at(q):
        return spread_out(totals[:, q : q + 1])

    gram = {}
    for n, (a, b) in enumerate([(0, 0), (0, 1), (0, 2), (1, 1), (1, 2), (2, 2)]):
        gram[a, b] = at(QUAD + n)
    for a in range(3):
        gram[a, 3] = at(8 * a + 3)
    gram[3, 3] = at(SHARE)
    for a in range(4):
        gram[a, a] = gram[a, a] + REGULARIZE
    lower, diag, inverse = {}, [], []
    for j in range(4):
        scaled = [lower[j, k] * diag[k] for k in range(j)]
        pivot = gram[j, j]
        for k in range(j):
            pivot = pivot - lower[j, k] * scaled[k]
        diag.append(pivot)
        inverse.append(1.0 / pivot)
        for i in range(j + 1, 4):
            value = gram[j, i]
            for k in range(j):
                value = value - lower[i, k] * scaled[k]
            lower[i, j] = value * inverse[j]
    new = [None] * 12
    for k in range(3):
        right = []
        for m in range(4):
            j = 3 * k + m if m < 3 else 9 + k
            value = at(8 * m + k) + REGULARIZE * spread_out(old[:, j : j + 1])
            for n in range(m):
                value = value - lower[m, n] * right[n]
            right.append(value)
        found = [None] * 4
        for m in reversed(range(4)):
            value = right[m] * inverse[m]
            for n in range(m + 1, 4):
                value = value - lower[n, m] * found[n]
            found[m] = value
        for m in range(4):
            new[3 * k + m if m < 3 else 9 + k] = found[m]
    return new


def line_sum(all_ref, line, segs):
    return jnp.sum(all_ref[pl.ds(line * segs, segs), :], axis=0, keepdims=True)


def new_spread(all_ref):
    everything = jnp.sum(all_ref[...], axis=0, keepdims=True)
    top = spread_out(everything[:, ENERGY : ENERGY + 1]) + PRIOR_TOP
    return top / (3.0 * spread_out(everything[:, SHARE : SHARE + 1]) + PRIOR_BOTTOM)


def pose_row(new, first):
    lane = lax.broadcasted_iota(jnp.int32, (1, 128), 1)
    row = jnp.zeros((1, 128), F32)
    for j in range(12):
        row = jnp.where(lane == first + j, new[j][:1, :], row)
    return row


def second_kernel(
    lines, segs, cells_hbm, sent_a, all_ref, source_ref, margin_a, margin_b,
    sums_ref, out_hbm, out_ref, out_sem, *scratch_refs,
):
    line = lax.axis_index("line")
    lists = Lists(cells_hbm, source_ref, (margin_a, margin_b), scratch_refs)
    partner = [jnp.clip(line + 2 * d - 1, 0, lines - 1) for d in lists.dirs]
    sub = iota(0)

    def stacked(a, b, c):
        return jnp.where(sub == 0, spread_out(a), jnp.where(sub == 1, spread_out(b), spread_out(c)))

    totals = stacked(*[line_sum(all_ref, n, segs) for n in (line, partner[0], partner[1])])
    old = stacked(*[ref[3 * MROWS : 3 * MROWS + 1, :] for ref in (sent_a, margin_a, margin_b)])
    new = solve(totals, old)
    negc = (-0.5 * LOG2E) / new_spread(all_ref)
    own, *nbrs = [[spread_out(value[n : n + 1, :]) for value in new] for n in range(3)]
    carry, longest = quick(lists, own, nbrs, negc, [0, 1], no_sums(), jnp.zeros(TILE, F32), out_ref)
    close(lists, own, nbrs, negc, carry, longest, pose_row(new, POSE), sums_ref, (out_hbm, out_ref, out_sem))


def last_kernel(segs, all_ref, fitted_ref, spread_ref):
    line = lax.axis_index("line")
    totals = spread_out(line_sum(all_ref, line, segs))
    old = all_ref[pl.ds(line * segs, 1), :][:, POSE : POSE + 12]
    new = solve(totals, jnp.broadcast_to(old, (8, 12)))
    fitted_ref[...] = pose_row(new, 0)[:, :12]
    spread_ref[...] = new_spread(all_ref)[:1, :1]


def vmem(count):
    return [pl.BlockSpec(memory_space=pltpu.VMEM)] * count


ANY = pl.BlockSpec(memory_space=pl.ANY)
HBM = pl.BlockSpec(memory_space=pltpu.HBM)
SMEM = pl.BlockSpec(memory_space=pltpu.SMEM)
PARAMS = pltpu.CompilerParams(vmem_limit_bytes=32 * 1024 * 1024)


def scratch():
    return [
        pltpu.VMEM((48, MARGIN), BF16),
        pltpu.VMEM((48, MARGIN), BF16),
        pltpu.VMEM((2, 3, MROWS, 128), F32),
        pltpu.VMEM((3, 128, 128), F32),
        pltpu.VMEM((3, 128, 128), F32),
    ]


def in_hbm(value):
    return pltpu.with_memory_space_constraint(value, pltpu.HBM)


def pair_cost(cells, sides):
    pairs = cells.size // 2 * sides * BLOCK * CT
    return pl.CostEstimate(flops=400 * pairs, bytes_accessed=1 << 20, transcendentals=pairs)


def gather_call(rows, sent_a, sent_b):
    return pl.pallas_call(
        gather_kernel,
        in_specs=vmem(3),
        out_specs=vmem(1)[0],
        out_shape=jax.ShapeDtypeStruct((4,) + rows.shape, F32),
        compiler_params=PARAMS,
        cost_estimate=pl.CostEstimate(flops=10**9, bytes_accessed=1 << 20, transcendentals=0),
        name="gather_sources",
    )(rows, sent_a, sent_b)


def partner_call(cells, sent_a, source, margin_a):
    return pl.pallas_call(
        partner_kernel,
        in_specs=[SMEM] + vmem(3),
        out_specs=vmem(1)[0],
        out_shape=jax.ShapeDtypeStruct((6,) + TILE, F32),
        scratch_shapes=scratch(),
        compiler_params=PARAMS,
        cost_estimate=pair_cost(cells, 1),
        name="match_partner",
    )(cells, sent_a, source, margin_a)


def other_call(cells, sent_a, source, part, margin_a, margin_b, devices):
    return pl.pallas_call(
        other_kernel,
        in_specs=[SMEM] + vmem(5),
        out_specs=vmem(1)[0],
        out_shape=jax.ShapeDtypeStruct((devices, 128), F32),
        scratch_shapes=scratch(),
        compiler_params=PARAMS,
        cost_estimate=pair_cost(cells, 1),
        name="match_other",
    )(cells, sent_a, source, part, margin_a, margin_b)


def second_call(cells, sent_a, everyone, source, margin_a, margin_b, lines, segs):
    result = (5,) + source.shape[1:]
    return pl.pallas_call(
        functools.partial(second_kernel, lines, segs),
        in_specs=[SMEM] + vmem(5),
        out_specs=vmem(1) + [ANY],
        out_shape=[jax.ShapeDtypeStruct((lines * segs, 128), F32), jax.ShapeDtypeStruct(result, F32)],
        scratch_shapes=[pltpu.VMEM(result, F32), pltpu.SemaphoreType.DMA] + scratch(),
        compiler_params=PARAMS,
        cost_estimate=pair_cost(cells, 2),
        name="match_second",
    )(cells, sent_a, everyone, source, margin_a, margin_b)


def exchange(sums):
    return lax.all_to_all(sums, ("line", "seg"), 0, 0)


def on_device(lines, segs, points, rows, cells, pose):
    own_points = points.reshape(3, -1, 128)
    slots = rows.shape[-1]
    blocks = slots // BLOCK
    row_list = rows.reshape(2, blocks, 128).transpose(1, 0, 2).reshape(2 * blocks, 128)
    cell_ids = cells.reshape(2, blocks)
    sent_a, sent_b, cell_ids = pack_call(in_hbm(own_points), in_hbm(pose.reshape(1, 12)), in_hbm(cell_ids))
    cell_ids = pltpu.with_memory_space_constraint(cell_ids, pltpu.SMEM)
    pairs_a = [(i, i ^ 1) for i in range(lines)]
    pairs_b = [(i, (((i + 1) ^ 1) - 1) % lines) for i in range(lines)]
    margin_a = lax.ppermute(sent_a, "line", pairs_a)
    margin_b = lax.ppermute(sent_b, "line", pairs_b)
    source = gather_call(row_list, sent_a, sent_b)
    part = partner_call(cell_ids, sent_a, source, margin_a)
    sums = other_call(cell_ids, sent_a, source, part, margin_a, margin_b, lines * segs)
    everyone = exchange(sums)
    sums, result = second_call(cell_ids, sent_a, everyone, source, margin_a, margin_b, lines, segs)
    everyone = exchange(sums)
    fitted, spread = pl.pallas_call(
        functools.partial(last_kernel, segs),
        in_specs=vmem(1),
        out_specs=vmem(2),
        out_shape=[jax.ShapeDtypeStruct((1, 12), F32), jax.ShapeDtypeStruct((1, 1), F32)],
        compiler_params=PARAMS,
        name="solve_last",
    )(everyone)
    result = result.reshape(5, blocks, 2, 128).transpose(2, 0, 1, 3).reshape(1, 1, 2, 5, slots)
    return (result, fitted.reshape(12, 1), spread.reshape(1))


def solution(mesh):
    return jax.shard_map(
        functools.partial(on_device, mesh.shape["line"], mesh.shape["seg"]),
        mesh=mesh,
        in_specs=(
            P("line", "seg", None, None),
            P("line", "seg", None, None),
            P("line", "seg", None, None),
            P(None, "line"),
        ),
        out_specs=(P("line", "seg", None, None, None), P(None, "line"), P()),
        check_vma=False,
    )
```

```python
import functools
import math

import jax
import jax.numpy as jnp
from jax import lax
from jax.experimental import pallas as pl
from jax.experimental.pallas import tpu as pltpu
from jax.sharding import PartitionSpec as P

NCELL = 16
CT = 512
BLOCK = 128
MARGIN = NCELL * CT
MROWS = MARGIN // 128
TILES = CT // 128
GROUPS = BLOCK // 8
LEAD = 48
NEAR = 1
LAG = 3
WIDE = 4
QUICK_LIMIT = 1000.0
ENERGY_LIMIT = 400.0

OUTLIER_MASS = 1.0
SPREAD_START = 0.05
PRIOR_TOP = 0.05
PRIOR_BOTTOM = 1.0
REGULARIZE = 1.0
LOG2E = math.log2(math.e)

F32 = jnp.float32
BF16 = jnp.bfloat16
TILE = (8, 128)
ONE = 24
SHARE = ONE + 3
ENERGY = ONE + 4
QUAD = 32
POSE = 64


def iota(axis):
    return lax.broadcasted_iota(jnp.int32, TILE, axis)


def spread_out(value):
    return jnp.broadcast_to(value, TILE)


def pack_kernel(points_hbm, pose_hbm, cells_hbm, sent_a, sent_b, cells_ref, pose_ref, sems):
    odd = lax.axis_index("line") & 1
    tail = points_hbm.shape[1] - MROWS
    copies = [
        pltpu.make_async_copy(pose_hbm, pose_ref, sems.at[6]),
        pltpu.make_async_copy(cells_hbm, cells_ref, sems.at[7]),
    ]
    for n, (sent, first) in enumerate(((sent_a, (1 - odd) * tail), (sent_b, odd * tail))):
        spot = pl.ds(pl.multiple_of(first, MROWS), MROWS)
        for k in range(3):
            copies.append(
                pltpu.make_async_copy(points_hbm.at[k, spot, :], sent.at[pl.ds(MROWS * k, MROWS), :], sems.at[3 * n + k])
            )
    for copy in copies:
        copy.start()
    for sent in (sent_a, sent_b):
        sent[3 * MROWS :, :] = jnp.zeros(TILE, F32)
    copies[0].wait()
    for sent in (sent_a, sent_b):
        sent[3 * MROWS : 3 * MROWS + 1, :12] = pose_ref[...]
    for copy in copies[1:]:
        copy.wait()


def pack_call(points, pose, cells):
    return pl.pallas_call(
        pack_kernel,
        in_specs=[HBM] * 3,
        out_specs=vmem(2) + [SMEM],
        out_shape=[jax.ShapeDtypeStruct((3 * MROWS + 8, 128), F32)] * 2 + [pltpu.SMEM(cells.shape, jnp.int32)],
        scratch_shapes=[pltpu.VMEM((1, 12), F32), pltpu.SemaphoreType.DMA((8,))],
        compiler_params=PARAMS,
        name="pack_margins",
    )(points, pose, cells)


def pick_columns(rows_ref, margin_parts, rows):
    spots = [jnp.maximum(rows_ref[pl.ds(row, 1), :], 0) & (MARGIN - 1) for row in rows]
    hits = []
    for spot in spots:
        low = spread_out(spot & 127)
        hit = [(low == iota(0) + 8 * v).astype(F32) for v in range(16)]
        hits.append(jnp.concatenate(hit, axis=0).astype(BF16))
    hit = jnp.concatenate(hits, axis=1)
    return spots, jnp.dot(margin_parts, jnp.concatenate([hit] * 3, axis=0), preferred_element_type=F32)


def pick_rows(source_ref, rows, spots, picked):
    for n, row in enumerate(rows):
        high = spread_out(spots[n] >> 7)
        sums = [jnp.zeros(TILE, F32)] * 3
        for v in range(MROWS // 8):
            here = high == iota(0) + 8 * v
            for k in range(3):
                first = MROWS * k + 8 * v
                sums[k] = jnp.where(here, picked[first : first + 8, 128 * n : 128 * n + 128], sums[k])
        for k in range(3):
            source_ref[k, pl.ds(row, 1), :] = jnp.sum(sums[k], axis=0, keepdims=True)


def apply_pose(coefs, xyz):
    out = []
    for k in range(3):
        total = coefs[3 * k] * xyz[0]
        total = total + coefs[3 * k + 1] * xyz[1]
        total = total + coefs[3 * k + 2] * xyz[2]
        out.append(total + coefs[9 + k])
    return out


def column(coefs, first, stride):
    sub = iota(0)
    out = jnp.zeros(TILE, F32)
    for k in range(3):
        out = jnp.where(sub == k, coefs[first + stride * k], out)
    return out


def columns(coefs):
    return [column(coefs, k, 3) for k in range(3)] + [column(coefs, 9, 1)]


def squared_length(value):
    square = value * value
    return spread_out(square[0:1, :]) + spread_out(square[1:2, :]) + spread_out(square[2:3, :])


def three_parts(value):
    high = value.astype(BF16).astype(F32)
    rest = value - high
    middle = rest.astype(BF16).astype(F32)
    return high, middle, rest - middle


def combine(cols, xyz):
    return cols[0] * xyz[0] + cols[1] * xyz[1] + cols[2] * xyz[2]


def features_of(near, margin_ref, cell):
    sub = iota(0)
    tiles, longest = [], None
    for t in range(TILES):
        row = cell * TILES + t
        y = combine(near, [spread_out(margin_ref[pl.ds(k * MROWS + row, 1), :]) for k in range(3)])
        length = squared_length(y)
        longest = length if longest is None else jnp.maximum(longest, length)
        high, middle, low = three_parts(jnp.where(sub == 3, length, jnp.where(sub == 4, 1.0, y)))
        tiles.append(jnp.concatenate([high, middle, low, high, middle, high], axis=0).astype(BF16))
    return jnp.concatenate(tiles, axis=1), longest


def longest_source(own, near, dirs, source_ref):
    longest = jnp.zeros(TILE, F32)
    for v in range(source_ref.shape[1] // 8):
        rows = slice(8 * v, 8 * v + 8)
        xyz = [source_ref[k, rows, :] for k in range(3)]
        moved = apply_pose(own, xyz)
        for side in range(2):
            square = sum((moved[k] - near[side][9 + k]) ** 2 for k in range(3))
            listed = (iota(0) & 1) == dirs[side]
            longest = jnp.maximum(longest, jnp.where(listed, square * source_ref[3, rows, :], 0.0))
    return longest


def coefficients(negc, own, near, source_ref, place):
    side, row, _ = place
    sub = iota(0)
    xt = [spread_out(source_ref[k, pl.ds(row, 1), :]) for k in range(4)]
    m = combine(own, xt) + (own[3] - near[side][3])
    length = squared_length(m)
    coef = jnp.where(sub == 3, negc, jnp.where(sub == 4, negc * length, (-2.0 * negc) * m))
    high, middle, low = three_parts(coef)
    stack = jnp.concatenate([high, high, high, middle, middle, low], axis=0)
    return jnp.transpose(stack).astype(BF16), xt, m, length


def weigh(features, coef):
    power = jnp.dot(coef, features, preferred_element_type=F32)
    weight = jnp.transpose(jnp.exp2(power))
    top = weight.astype(BF16)
    rest = (weight - top.astype(F32)).astype(BF16)
    return features[:32], jnp.concatenate([top, rest], axis=1)


def weighted_sums(features, weights):
    sums = jnp.dot(features, weights, preferred_element_type=F32)
    sums = sums[:, :BLOCK] + sums[:, BLOCK:]
    return sums[0:8] + sums[8:16] + sums[16:24]


def finish(near, side, xt, m, length, sums):
    sub = iota(0)
    total = spread_out(sums[4:5, :])
    around = combine([spread_out(m[k : k + 1, :]) for k in range(3)], [spread_out(sums[k : k + 1, :]) for k in range(3)])
    energy = spread_out(sums[3:4, :]) - 2.0 * around + length * total
    raw = jnp.where(sub < 3, sums + near[side][3] * total, jnp.where(sub == 3, total, jnp.where(sub == 4, energy, 0.0)))
    return raw * (xt[3] / (total + OUTLIER_MASS)), xt


class Lists:
    def __init__(self, cells_ref, source_ref, margin_refs, scratch_refs):
        self.dirs = sides_of(lax.axis_index("line"))
        self.source_ref = source_ref
        self.margin_refs = margin_refs
        self.cells_ref = cells_ref
        self.world_ref, self.moved_ref, self.column_ref = scratch_refs

    def places(self, side):
        return [(side, 2 * b + self.dirs[side], b) for b in range(self.cells_ref.shape[1])]

    def cell(self, place):
        side, _, b = place
        return self.cells_ref[self.dirs[side], b]


def quick(lists, own, nbrs, negc, sides, carry, longest, out_ref):
    own_cols, near_cols = columns(own), {side: columns(nbrs[side]) for side in sides}
    places = [place for side in sides for place in lists.places(side)]
    coefs, feats, found = {}, {}, {}
    ahead = None
    for n in range(-1, len(places) + LAG):
        block, ahead = ahead, None
        for later in range(0 if n < 0 else n + 1 + LEAD, min(n + 2 + LEAD, len(places))):
            coefs[later] = coefficients(negc, own_cols, near_cols, lists.source_ref, places[later])
        for later in range(0 if n < 0 else n + 1 + NEAR, min(n + 2 + NEAR, len(places))):
            side = places[later][0]
            cell = jnp.maximum(lists.cell(places[later]), 0)
            feats[later], length = features_of(near_cols[side], lists.margin_refs[side], cell)
            longest = jnp.maximum(longest, length)
        if n + 1 < len(places):
            ahead = weigh(feats.pop(n + 1), coefs[n + 1][0])
        if block is not None:
            found[n] = weighted_sums(*block)
        if n >= LAG:
            side, row, _ = places[n - LAG]
            result, xt = finish(near_cols, side, *coefs[n - LAG][1:], found[n - LAG])
            carry = add_block(carry, row, result, xt, out_ref)
    return carry, longest


def no_sums():
    return [jnp.zeros(TILE, F32) for _ in range(5)]


def close(lists, own, nbrs, negc, carry, longest, pose_row, sums_ref, out):
    out_ref = None if out is None else out[1]
    if out is not None:
        save = pltpu.make_async_copy(out[1], out[0], out[2])
        save.start()
    pack_sums(carry, pose_row, sums_ref)
    size = jnp.max(longest) + jnp.max(longest_source(own, nbrs, lists.dirs, lists.source_ref))
    share, energy = [jnp.sum(carry[3][q : q + 1, :]) for q in (3, 4)]
    bad = (size * jnp.max(-negc) > QUICK_LIMIT) | (size * share > ENERGY_LIMIT * energy)

    @pl.when(bad)
    def _():
        if out is not None:
            save.wait()
        one_block = careful_setup(
            own, nbrs, negc, lists.source_ref, lists.margin_refs, lists.world_ref, lists.moved_ref, lists.column_ref
        )
        carry = tuple(no_sums())
        for side in range(2):
            d = lists.dirs[side]

            def step(b, carry, side=side, d=d):
                result, xt = one_block(side, 2 * b + d, lists.cells_ref[d, b])
                return tuple(add_block(carry, 2 * b + d, result, xt, out_ref))

            carry = lax.fori_loop(0, lists.cells_ref.shape[1], step, carry)
        pack_sums(carry, pose_row, sums_ref)
        if out is not None:
            save.start()

    if out is not None:
        save.wait()


def add_block(carry, row, result, xt, out_ref):
    sub = iota(0)
    if out_ref is not None:
        for q in range(5):
            out_ref[q, pl.ds(row, 1), :] = result[q : q + 1, :]
    left = jnp.where(sub < 3, xt[0], jnp.where(sub < 5, xt[1], xt[2]))
    right = jnp.where(sub == 0, xt[0], jnp.where((sub == 1) | (sub == 3), xt[1], xt[2]))
    share = spread_out(result[3:4, :])
    return [
        carry[0] + result * xt[0],
        carry[1] + result * xt[1],
        carry[2] + result * xt[2],
        carry[3] + result,
        carry[4] + share * (left * right),
    ]


def careful_setup(own, nbrs, negc, source_ref, margin_refs, world_ref, moved_ref, column_ref):
    slot_rows = source_ref.shape[1]
    for v in range(slot_rows // 8):
        xyz = [source_ref[k, 8 * v : 8 * v + 8, :] for k in range(3)]
        for k, value in enumerate(apply_pose(own, xyz)):
            moved_ref[k, 8 * v : 8 * v + 8, :] = value
    for k in range(3):
        column_ref[k] = jnp.transpose(moved_ref[k])
    for side in range(2):
        for v in range(MROWS // 8):
            xyz = [margin_refs[side][k * MROWS + 8 * v : k * MROWS + 8 * v + 8, :] for k in range(3)]
            for k, value in enumerate(apply_pose(nbrs[side], xyz)):
                world_ref[side, k, 8 * v : 8 * v + 8, :] = value
    lane = iota(1)

    def one_block(side, row, cell):
        first = jnp.maximum(cell, 0) * TILES
        target = [
            [spread_out(world_ref[side, k, pl.ds(first + t, 1), :]) for t in range(TILES)] for k in range(3)
        ]
        pick = jnp.full(TILE, row, jnp.int32)
        parts = []
        for g in range(GROUPS):
            m = [
                jnp.take_along_axis(column_ref[k, 8 * g : 8 * g + 8, :], pick, axis=1, mode="promise_in_bounds")
                for k in range(3)
            ]
            sums = None
            for t in range(TILES):
                d = [m[k] - target[k][t] for k in range(3)]
                dist = d[0] * d[0] + d[1] * d[1] + d[2] * d[2]
                weight = jnp.exp2(dist * negc)
                terms = [weight * target[k][t] for k in range(3)] + [weight, weight * dist]
                sums = terms if sums is None else [a + b for a, b in zip(sums, terms)]
            part = jnp.zeros(TILE, F32)
            for q in range(5):
                part = jnp.where(lane == q, jnp.sum(sums[q], axis=1, keepdims=True), part)
            parts.append(part)
        flat = jnp.transpose(jnp.concatenate(parts, axis=0))[:8, :]
        xt = [spread_out(source_ref[k, pl.ds(row, 1), :]) for k in range(4)]
        return flat * (xt[3] / (spread_out(flat[3:4, :]) + OUTLIER_MASS)), xt

    return one_block


def pack_sums(sums, pose_row, out_ref):
    lane, sub = iota(1), iota(0)
    total = jnp.zeros(TILE, F32)
    for c in range(5):
        total = total + jnp.where(lane == 8 * c + sub, jnp.sum(sums[c], axis=1, keepdims=True), 0.0)
    row = jnp.sum(total, axis=0, keepdims=True)
    out_ref[...] = jnp.broadcast_to(row + pose_row, out_ref.shape)


def pose_of_row(row):
    return [spread_out(row[:, j : j + 1]) for j in range(12)]


def sides_of(line):
    odd = line & 1
    return [1 - odd, odd]


def pose_in(margin_ref):
    return pose_of_row(margin_ref[3 * MROWS : 3 * MROWS + 1, :])


def gather_kernel(rows_ref, sent_a, sent_b, source_ref):
    dirs = sides_of(lax.axis_index("line"))
    slot_rows = rows_ref.shape[0]
    blocks = slot_rows // 2
    for v in range(slot_rows // 8):
        source_ref[3, 8 * v : 8 * v + 8, :] = (rows_ref[8 * v : 8 * v + 8, :] >= 0).astype(F32)
    last = None
    for side, sent in enumerate((sent_a, sent_b)):
        parts = jnp.concatenate(three_parts(sent[: 3 * MROWS, :]), axis=1).astype(BF16)
        for first in range(0, blocks, WIDE):
            rows = [2 * b + dirs[side] for b in range(first, min(first + WIDE, blocks))]
            found = rows, *pick_columns(rows_ref, parts, rows)
            if last is not None:
                pick_rows(source_ref, *last)
            last = found
    pick_rows(source_ref, *last)


def partner_kernel(cells_hbm, sent_a, source_ref, margin_a, part_ref, *scratch_refs):
    lists = Lists(cells_hbm, source_ref, (margin_a, None), scratch_refs)
    nothing = jnp.zeros(TILE, F32)
    carry, longest = quick(lists, pose_in(sent_a), [pose_in(margin_a)], first_negc(), [0], no_sums(), nothing, None)
    for n, value in enumerate(carry + [longest]):
        part_ref[n] = value


def other_kernel(cells_hbm, sent_a, source_ref, part_ref, margin_a, margin_b, sums_ref, *scratch_refs):
    lists = Lists(cells_hbm, source_ref, (margin_a, margin_b), scratch_refs)
    own = pose_in(sent_a)
    nbrs = [pose_in(margin) for margin in (margin_a, margin_b)]
    part = [part_ref[n] for n in range(6)]
    carry, longest = quick(lists, own, nbrs, first_negc(), [1], part[:5], part[5], None)
    close(lists, own, nbrs, first_negc(), carry, longest, 0.0, sums_ref, None)


def first_negc():
    return jnp.full(TILE, -LOG2E / (2.0 * SPREAD_START), F32)


def solve(totals, old):
    def at(q):
        return spread_out(totals[:, q : q + 1])

    gram = {}
    for n, (a, b) in enumerate([(0, 0), (0, 1), (0, 2), (1, 1), (1, 2), (2, 2)]):
        gram[a, b] = at(QUAD + n)
    for a in range(3):
        gram[a, 3] = at(8 * a + 3)
    gram[3, 3] = at(SHARE)
    for a in range(4):
        gram[a, a] = gram[a, a] + REGULARIZE
    lower, diag, inverse = {}, [], []
    for j in range(4):
        scaled = [lower[j, k] * diag[k] for k in range(j)]
        pivot = gram[j, j]
        for k in range(j):
            pivot = pivot - lower[j, k] * scaled[k]
        diag.append(pivot)
        inverse.append(1.0 / pivot)
        for i in range(j + 1, 4):
            value = gram[j, i]
            for k in range(j):
                value = value - lower[i, k] * scaled[k]
            lower[i, j] = value * inverse[j]
    new = [None] * 12
    for k in range(3):
        right = []
        for m in range(4):
            j = 3 * k + m if m < 3 else 9 + k
            value = at(8 * m + k) + REGULARIZE * spread_out(old[:, j : j + 1])
            for n in range(m):
                value = value - lower[m, n] * right[n]
            right.append(value)
        found = [None] * 4
        for m in reversed(range(4)):
            value = right[m] * inverse[m]
            for n in range(m + 1, 4):
                value = value - lower[n, m] * found[n]
            found[m] = value
        for m in range(4):
            new[3 * k + m if m < 3 else 9 + k] = found[m]
    return new


def line_sum(all_ref, line, segs):
    return jnp.sum(all_ref[pl.ds(line * segs, segs), :], axis=0, keepdims=True)


def new_spread(all_ref):
    everything = jnp.sum(all_ref[...], axis=0, keepdims=True)
    top = spread_out(everything[:, ENERGY : ENERGY + 1]) + PRIOR_TOP
    return top / (3.0 * spread_out(everything[:, SHARE : SHARE + 1]) + PRIOR_BOTTOM)


def pose_row(new, first):
    lane = lax.broadcasted_iota(jnp.int32, (1, 128), 1)
    row = jnp.zeros((1, 128), F32)
    for j in range(12):
        row = jnp.where(lane == first + j, new[j][:1, :], row)
    return row


def second_kernel(
    lines, segs, cells_hbm, sent_a, all_ref, source_ref, margin_a, margin_b,
    sums_ref, out_hbm, out_ref, out_sem, *scratch_refs,
):
    line = lax.axis_index("line")
    lists = Lists(cells_hbm, source_ref, (margin_a, margin_b), scratch_refs)
    partner = [jnp.clip(line + 2 * d - 1, 0, lines - 1) for d in lists.dirs]
    sub = iota(0)

    def stacked(a, b, c):
        return jnp.where(sub == 0, spread_out(a), jnp.where(sub == 1, spread_out(b), spread_out(c)))

    totals = stacked(*[line_sum(all_ref, n, segs) for n in (line, partner[0], partner[1])])
    old = stacked(*[ref[3 * MROWS : 3 * MROWS + 1, :] for ref in (sent_a, margin_a, margin_b)])
    new = solve(totals, old)
    negc = (-0.5 * LOG2E) / new_spread(all_ref)
    own, *nbrs = [[spread_out(value[n : n + 1, :]) for value in new] for n in range(3)]
    carry, longest = quick(lists, own, nbrs, negc, [0, 1], no_sums(), jnp.zeros(TILE, F32), out_ref)
    close(lists, own, nbrs, negc, carry, longest, pose_row(new, POSE), sums_ref, (out_hbm, out_ref, out_sem))


def last_kernel(segs, all_ref, fitted_ref, spread_ref):
    line = lax.axis_index("line")
    totals = spread_out(line_sum(all_ref, line, segs))
    old = all_ref[pl.ds(line * segs, 1), :][:, POSE : POSE + 12]
    new = solve(totals, jnp.broadcast_to(old, (8, 12)))
    fitted_ref[...] = pose_row(new, 0)[:, :12]
    spread_ref[...] = new_spread(all_ref)[:1, :1]


def vmem(count):
    return [pl.BlockSpec(memory_space=pltpu.VMEM)] * count


ANY = pl.BlockSpec(memory_space=pl.ANY)
HBM = pl.BlockSpec(memory_space=pltpu.HBM)
SMEM = pl.BlockSpec(memory_space=pltpu.SMEM)
PARAMS = pltpu.CompilerParams(vmem_limit_bytes=32 * 1024 * 1024)


def scratch():
    return [
        pltpu.VMEM((2, 3, MROWS, 128), F32),
        pltpu.VMEM((3, 128, 128), F32),
        pltpu.VMEM((3, 128, 128), F32),
    ]


def in_hbm(value):
    return pltpu.with_memory_space_constraint(value, pltpu.HBM)


def pair_cost(cells, sides):
    pairs = cells.size // 2 * sides * BLOCK * CT
    return pl.CostEstimate(flops=400 * pairs, bytes_accessed=1 << 20, transcendentals=pairs)


def gather_call(rows, sent_a, sent_b):
    return pl.pallas_call(
        gather_kernel,
        in_specs=vmem(3),
        out_specs=vmem(1)[0],
        out_shape=jax.ShapeDtypeStruct((4,) + rows.shape, F32),
        compiler_params=PARAMS,
        cost_estimate=pl.CostEstimate(flops=10**9, bytes_accessed=1 << 20, transcendentals=0),
        name="gather_sources",
    )(rows, sent_a, sent_b)


def partner_call(cells, sent_a, source, margin_a):
    return pl.pallas_call(
        partner_kernel,
        in_specs=[SMEM] + vmem(3),
        out_specs=vmem(1)[0],
        out_shape=jax.ShapeDtypeStruct((6,) + TILE, F32),
        scratch_shapes=scratch(),
        compiler_params=PARAMS,
        cost_estimate=pair_cost(cells, 1),
        name="match_partner",
    )(cells, sent_a, source, margin_a)


def other_call(cells, sent_a, source, part, margin_a, margin_b, devices):
    return pl.pallas_call(
        other_kernel,
        in_specs=[SMEM] + vmem(5),
        out_specs=vmem(1)[0],
        out_shape=jax.ShapeDtypeStruct((devices, 128), F32),
        scratch_shapes=scratch(),
        compiler_params=PARAMS,
        cost_estimate=pair_cost(cells, 1),
        name="match_other",
    )(cells, sent_a, source, part, margin_a, margin_b)


def second_call(cells, sent_a, everyone, source, margin_a, margin_b, lines, segs):
    result = (5,) + source.shape[1:]
    return pl.pallas_call(
        functools.partial(second_kernel, lines, segs),
        in_specs=[SMEM] + vmem(5),
        out_specs=vmem(1) + [ANY],
        out_shape=[jax.ShapeDtypeStruct((lines * segs, 128), F32), jax.ShapeDtypeStruct(result, F32)],
        scratch_shapes=[pltpu.VMEM(result, F32), pltpu.SemaphoreType.DMA] + scratch(),
        compiler_params=PARAMS,
        cost_estimate=pair_cost(cells, 2),
        name="match_second",
    )(cells, sent_a, everyone, source, margin_a, margin_b)


def exchange(sums):
    return lax.all_to_all(sums, ("line", "seg"), 0, 0)


def on_device(lines, segs, points, rows, cells, pose):
    own_points = points.reshape(3, -1, 128)
    slots = rows.shape[-1]
    blocks = slots // BLOCK
    row_list = rows.reshape(2, blocks, 128).transpose(1, 0, 2).reshape(2 * blocks, 128)
    cell_ids = cells.reshape(2, blocks)
    sent_a, sent_b, cell_ids = pack_call(in_hbm(own_points), in_hbm(pose.reshape(1, 12)), in_hbm(cell_ids))
    cell_ids = pltpu.with_memory_space_constraint(cell_ids, pltpu.SMEM)
    pairs_a = [(i, i ^ 1) for i in range(lines)]
    pairs_b = [(i, (((i + 1) ^ 1) - 1) % lines) for i in range(lines)]
    margin_a = lax.ppermute(sent_a, "line", pairs_a)
    margin_b = lax.ppermute(sent_b, "line", pairs_b)
    source = gather_call(row_list, sent_a, sent_b)
    part = partner_call(cell_ids, sent_a, source, margin_a)
    sums = other_call(cell_ids, sent_a, source, part, margin_a, margin_b, lines * segs)
    everyone = exchange(sums)
    sums, result = second_call(cell_ids, sent_a, everyone, source, margin_a, margin_b, lines, segs)
    everyone = exchange(sums)
    fitted, spread = pl.pallas_call(
        functools.partial(last_kernel, segs),
        in_specs=vmem(1),
        out_specs=vmem(2),
        out_shape=[jax.ShapeDtypeStruct((1, 12), F32), jax.ShapeDtypeStruct((1, 1), F32)],
        compiler_params=PARAMS,
        name="solve_last",
    )(everyone)
    result = result.reshape(5, blocks, 2, 128).transpose(2, 0, 1, 3).reshape(1, 1, 2, 5, slots)
    return (result, fitted.reshape(12, 1), spread.reshape(1))


def solution(mesh):
    return jax.shard_map(
        functools.partial(on_device, mesh.shape["line"], mesh.shape["seg"]),
        mesh=mesh,
        in_specs=(
            P("line", "seg", None, None),
            P("line", "seg", None, None),
            P("line", "seg", None, None),
            P(None, "line"),
        ),
        out_specs=(P("line", "seg", None, None, None), P(None, "line"), P()),
        check_vma=False,
    )
```

```python
import functools
import math

import jax
import jax.numpy as jnp
from jax import lax
from jax.experimental import pallas as pl
from jax.experimental.pallas import tpu as pltpu
from jax.sharding import PartitionSpec as P

NCELL = 16
CT = 512
BLOCK = 128
MARGIN = NCELL * CT
MROWS = MARGIN // 128
TILES = CT // 128
GROUPS = BLOCK // 8
LEAD = 48
NEAR = 1
LAG = 3
WIDE = 4
QUICK_LIMIT = 1000.0
ENERGY_LIMIT = 400.0

OUTLIER_MASS = 1.0
SPREAD_START = 0.05
PRIOR_TOP = 0.05
PRIOR_BOTTOM = 1.0
REGULARIZE = 1.0
LOG2E = math.log2(math.e)

F32 = jnp.float32
BF16 = jnp.bfloat16
TILE = (8, 128)
ONE = 24
SHARE = ONE + 3
ENERGY = ONE + 4
QUAD = 32
POSE = 64


def iota(axis):
    return lax.broadcasted_iota(jnp.int32, TILE, axis)


def spread_out(value):
    return jnp.broadcast_to(value, TILE)


def pack_kernel(points_hbm, pose_hbm, cells_hbm, sent_a, sent_b, cells_ref, pose_ref, sems):
    odd = lax.axis_index("line") & 1
    tail = points_hbm.shape[1] - MROWS
    copies = [
        pltpu.make_async_copy(pose_hbm, pose_ref, sems.at[6]),
        pltpu.make_async_copy(cells_hbm, cells_ref, sems.at[7]),
    ]
    for n, (sent, first) in enumerate(((sent_a, (1 - odd) * tail), (sent_b, odd * tail))):
        spot = pl.ds(pl.multiple_of(first, MROWS), MROWS)
        for k in range(3):
            copies.append(
                pltpu.make_async_copy(points_hbm.at[k, spot, :], sent.at[pl.ds(MROWS * k, MROWS), :], sems.at[3 * n + k])
            )
    for copy in copies:
        copy.start()
    for sent in (sent_a, sent_b):
        sent[3 * MROWS :, :] = jnp.zeros(TILE, F32)
    copies[0].wait()
    for sent in (sent_a, sent_b):
        sent[3 * MROWS : 3 * MROWS + 1, :12] = pose_ref[...]
    for copy in copies[1:]:
        copy.wait()


def pack_call(points, pose, cells):
    return pl.pallas_call(
        pack_kernel,
        in_specs=[HBM] * 3,
        out_specs=vmem(2) + [SMEM],
        out_shape=[jax.ShapeDtypeStruct((3 * MROWS + 8, 128), F32)] * 2 + [pltpu.SMEM(cells.shape, jnp.int32)],
        scratch_shapes=[pltpu.VMEM((1, 12), F32), pltpu.SemaphoreType.DMA((8,))],
        compiler_params=PARAMS,
        name="pack_margins",
    )(points, pose, cells)


def pick_columns(rows_ref, margin_parts, rows):
    spots = [jnp.maximum(rows_ref[pl.ds(row, 1), :], 0) & (MARGIN - 1) for row in rows]
    hits = []
    for spot in spots:
        low = spread_out(spot & 127)
        hit = [(low == iota(0) + 8 * v).astype(F32) for v in range(16)]
        hits.append(jnp.concatenate(hit, axis=0).astype(BF16))
    hit = jnp.concatenate(hits, axis=1)
    return spots, jnp.dot(margin_parts, jnp.concatenate([hit] * 3, axis=0), preferred_element_type=F32)


def pick_rows(source_ref, rows, spots, picked):
    for n, row in enumerate(rows):
        high = spread_out(spots[n] >> 7)
        sums = [jnp.zeros(TILE, F32)] * 3
        for v in range(MROWS // 8):
            here = high == iota(0) + 8 * v
            for k in range(3):
                first = MROWS * k + 8 * v
                sums[k] = jnp.where(here, picked[first : first + 8, 128 * n : 128 * n + 128], sums[k])
        for k in range(3):
            source_ref[k, pl.ds(row, 1), :] = jnp.sum(sums[k], axis=0, keepdims=True)


def apply_pose(coefs, xyz):
    out = []
    for k in range(3):
        total = coefs[3 * k] * xyz[0]
        total = total + coefs[3 * k + 1] * xyz[1]
        total = total + coefs[3 * k + 2] * xyz[2]
        out.append(total + coefs[9 + k])
    return out


def column(coefs, first, stride):
    sub = iota(0)
    out = jnp.zeros(TILE, F32)
    for k in range(3):
        out = jnp.where(sub == k, coefs[first + stride * k], out)
    return out


def columns(coefs):
    return [column(coefs, k, 3) for k in range(3)] + [column(coefs, 9, 1)]


def squared_length(value):
    square = value * value
    return spread_out(square[0:1, :]) + spread_out(square[1:2, :]) + spread_out(square[2:3, :])


def three_parts(value):
    high = value.astype(BF16).astype(F32)
    rest = value - high
    middle = rest.astype(BF16).astype(F32)
    return high, middle, rest - middle


def combine(cols, xyz):
    return cols[0] * xyz[0] + cols[1] * xyz[1] + cols[2] * xyz[2]


def features_of(near, margin_ref, cell):
    sub = iota(0)
    tiles, longest = [], None
    for t in range(TILES):
        row = cell * TILES + t
        y = combine(near, [spread_out(margin_ref[pl.ds(k * MROWS + row, 1), :]) for k in range(3)])
        length = squared_length(y)
        longest = length if longest is None else jnp.maximum(longest, length)
        high, middle, low = three_parts(jnp.where(sub == 3, length, jnp.where(sub == 4, 1.0, y)))
        tiles.append(jnp.concatenate([high, middle, low, high, middle, high], axis=0).astype(BF16))
    return jnp.concatenate(tiles, axis=1), longest


def longest_source(own, near, dirs, source_ref):
    longest = jnp.zeros(TILE, F32)
    for v in range(source_ref.shape[1] // 8):
        rows = slice(8 * v, 8 * v + 8)
        xyz = [source_ref[k, rows, :] for k in range(3)]
        moved = apply_pose(own, xyz)
        for side in range(2):
            square = sum((moved[k] - near[side][9 + k]) ** 2 for k in range(3))
            listed = (iota(0) & 1) == dirs[side]
            longest = jnp.maximum(longest, jnp.where(listed, square * source_ref[3, rows, :], 0.0))
    return longest


def coefficients(negc, own, near, source_ref, place):
    side, row, _ = place
    sub = iota(0)
    xt = [spread_out(source_ref[k, pl.ds(row, 1), :]) for k in range(4)]
    m = combine(own, xt) + (own[3] - near[side][3])
    length = squared_length(m)
    coef = jnp.where(sub == 3, negc, jnp.where(sub == 4, negc * length, (-2.0 * negc) * m))
    high, middle, low = three_parts(coef)
    stack = jnp.concatenate([high, high, high, middle, middle, low], axis=0)
    return jnp.transpose(stack).astype(BF16), xt, m, length


def weigh(features, coef):
    power = jnp.dot(coef, features, preferred_element_type=F32)
    weight = jnp.transpose(jnp.exp2(power))
    top = weight.astype(BF16)
    rest = (weight - top.astype(F32)).astype(BF16)
    return features[:32], jnp.concatenate([top, rest], axis=1)


def weighted_sums(features, weights):
    sums = jnp.dot(features, weights, preferred_element_type=F32)
    sums = sums[:, :BLOCK] + sums[:, BLOCK:]
    return sums[0:8] + sums[8:16] + sums[16:24]


def finish(near, side, xt, m, length, sums):
    sub = iota(0)
    total = spread_out(sums[4:5, :])
    around = combine([spread_out(m[k : k + 1, :]) for k in range(3)], [spread_out(sums[k : k + 1, :]) for k in range(3)])
    energy = spread_out(sums[3:4, :]) - 2.0 * around + length * total
    raw = jnp.where(sub < 3, sums + near[side][3] * total, jnp.where(sub == 3, total, jnp.where(sub == 4, energy, 0.0)))
    return raw * (xt[3] / (total + OUTLIER_MASS)), xt


class Lists:
    def __init__(self, cells_ref, source_ref, margin_refs, scratch_refs):
        self.dirs = sides_of(lax.axis_index("line"))
        self.source_ref = source_ref
        self.margin_refs = margin_refs
        self.cells_ref = cells_ref
        self.world_ref, self.moved_ref, self.column_ref = scratch_refs

    def places(self, side):
        return [(side, 2 * b + self.dirs[side], b) for b in range(self.cells_ref.shape[1])]

    def cell(self, place):
        side, _, b = place
        return self.cells_ref[self.dirs[side], b]


def quick(lists, own, nbrs, negc, sides, carry, longest, out_ref):
    own_cols, near_cols = columns(own), {side: columns(nbrs[side]) for side in sides}
    places = [place for side in sides for place in lists.places(side)]
    coefs, feats, found = {}, {}, {}
    ahead = None
    for n in range(-1, len(places) + LAG):
        block, ahead = ahead, None
        for later in range(0 if n < 0 else n + 1 + LEAD, min(n + 2 + LEAD, len(places))):
            coefs[later] = coefficients(negc, own_cols, near_cols, lists.source_ref, places[later])
        for later in range(0 if n < 0 else n + 1 + NEAR, min(n + 2 + NEAR, len(places))):
            side = places[later][0]
            cell = jnp.maximum(lists.cell(places[later]), 0)
            feats[later], length = features_of(near_cols[side], lists.margin_refs[side], cell)
            longest = jnp.maximum(longest, length)
        if n + 1 < len(places):
            ahead = weigh(feats.pop(n + 1), coefs[n + 1][0])
        if block is not None:
            found[n] = weighted_sums(*block)
        if n >= LAG:
            side, row, _ = places[n - LAG]
            result, xt = finish(near_cols, side, *coefs[n - LAG][1:], found[n - LAG])
            carry = add_block(carry, row, result, xt, out_ref)
    return carry, longest


def no_sums():
    return [jnp.zeros(TILE, F32) for _ in range(5)]


def close(lists, own, nbrs, negc, carry, longest, pose_row, sums_ref, out):
    out_ref = None if out is None else out[1]
    if out is not None:
        save = pltpu.make_async_copy(out[1], out[0], out[2])
        save.start()
    pack_sums(carry, pose_row, sums_ref)
    size = jnp.max(longest) + jnp.max(longest_source(own, nbrs, lists.dirs, lists.source_ref))
    share, energy = [jnp.sum(carry[3][q : q + 1, :]) for q in (3, 4)]
    bad = (size * jnp.max(-negc) > QUICK_LIMIT) | (size * share > ENERGY_LIMIT * energy)

    @pl.when(bad)
    def _():
        if out is not None:
            save.wait()
        one_block = careful_setup(
            own, nbrs, negc, lists.source_ref, lists.margin_refs, lists.world_ref, lists.moved_ref, lists.column_ref
        )
        carry = tuple(no_sums())
        for side in range(2):
            d = lists.dirs[side]

            def step(b, carry, side=side, d=d):
                result, xt = one_block(side, 2 * b + d, lists.cells_ref[d, b])
                return tuple(add_block(carry, 2 * b + d, result, xt, out_ref))

            carry = lax.fori_loop(0, lists.cells_ref.shape[1], step, carry)
        pack_sums(carry, pose_row, sums_ref)
        if out is not None:
            save.start()

    if out is not None:
        save.wait()


def add_block(carry, row, result, xt, out_ref):
    sub = iota(0)
    if out_ref is not None:
        for q in range(5):
            out_ref[q, pl.ds(row, 1), :] = result[q : q + 1, :]
    left = jnp.where(sub < 3, xt[0], jnp.where(sub < 5, xt[1], xt[2]))
    right = jnp.where(sub == 0, xt[0], jnp.where((sub == 1) | (sub == 3), xt[1], xt[2]))
    share = spread_out(result[3:4, :])
    return [
        carry[0] + result * xt[0],
        carry[1] + result * xt[1],
        carry[2] + result * xt[2],
        carry[3] + result,
        carry[4] + share * (left * right),
    ]


def careful_setup(own, nbrs, negc, source_ref, margin_refs, world_ref, moved_ref, column_ref):
    slot_rows = source_ref.shape[1]
    for v in range(slot_rows // 8):
        xyz = [source_ref[k, 8 * v : 8 * v + 8, :] for k in range(3)]
        for k, value in enumerate(apply_pose(own, xyz)):
            moved_ref[k, 8 * v : 8 * v + 8, :] = value
    for k in range(3):
        column_ref[k] = jnp.transpose(moved_ref[k])
    for side in range(2):
        for v in range(MROWS // 8):
            xyz = [margin_refs[side][k * MROWS + 8 * v : k * MROWS + 8 * v + 8, :] for k in range(3)]
            for k, value in enumerate(apply_pose(nbrs[side], xyz)):
                world_ref[side, k, 8 * v : 8 * v + 8, :] = value
    lane = iota(1)

    def one_block(side, row, cell):
        first = jnp.maximum(cell, 0) * TILES
        target = [
            [spread_out(world_ref[side, k, pl.ds(first + t, 1), :]) for t in range(TILES)] for k in range(3)
        ]
        pick = jnp.full(TILE, row, jnp.int32)
        parts = []
        for g in range(GROUPS):
            m = [
                jnp.take_along_axis(column_ref[k, 8 * g : 8 * g + 8, :], pick, axis=1, mode="promise_in_bounds")
                for k in range(3)
            ]
            sums = None
            for t in range(TILES):
                d = [m[k] - target[k][t] for k in range(3)]
                dist = d[0] * d[0] + d[1] * d[1] + d[2] * d[2]
                weight = jnp.exp2(dist * negc)
                terms = [weight * target[k][t] for k in range(3)] + [weight, weight * dist]
                sums = terms if sums is None else [a + b for a, b in zip(sums, terms)]
            part = jnp.zeros(TILE, F32)
            for q in range(5):
                part = jnp.where(lane == q, jnp.sum(sums[q], axis=1, keepdims=True), part)
            parts.append(part)
        flat = jnp.transpose(jnp.concatenate(parts, axis=0))[:8, :]
        xt = [spread_out(source_ref[k, pl.ds(row, 1), :]) for k in range(4)]
        return flat * (xt[3] / (spread_out(flat[3:4, :]) + OUTLIER_MASS)), xt

    return one_block


def pack_sums(sums, pose_row, out_ref):
    lane, sub = iota(1), iota(0)
    total = jnp.zeros(TILE, F32)
    for c in range(5):
        total = total + jnp.where(lane == 8 * c + sub, jnp.sum(sums[c], axis=1, keepdims=True), 0.0)
    row = jnp.sum(total, axis=0, keepdims=True)
    out_ref[...] = jnp.broadcast_to(row + pose_row, out_ref.shape)


def pose_of_row(row):
    return [spread_out(row[:, j : j + 1]) for j in range(12)]


def sides_of(line):
    odd = line & 1
    return [1 - odd, odd]


def pose_in(margin_ref):
    return pose_of_row(margin_ref[3 * MROWS : 3 * MROWS + 1, :])


def gather_kernel(rows_ref, sent_a, sent_b, source_ref):
    dirs = sides_of(lax.axis_index("line"))
    slot_rows = rows_ref.shape[0]
    blocks = slot_rows // 2
    for v in range(slot_rows // 8):
        source_ref[3, 8 * v : 8 * v + 8, :] = (rows_ref[8 * v : 8 * v + 8, :] >= 0).astype(F32)
    last = None
    for side, sent in enumerate((sent_a, sent_b)):
        parts = jnp.concatenate(three_parts(sent[: 3 * MROWS, :]), axis=1).astype(BF16)
        for first in range(0, blocks, WIDE):
            rows = [2 * b + dirs[side] for b in range(first, min(first + WIDE, blocks))]
            found = rows, *pick_columns(rows_ref, parts, rows)
            if last is not None:
                pick_rows(source_ref, *last)
            last = found
    pick_rows(source_ref, *last)


def partner_kernel(cells_hbm, sent_a, source_ref, margin_a, part_ref, *scratch_refs):
    lists = Lists(cells_hbm, source_ref, (margin_a, None), scratch_refs)
    nothing = jnp.zeros(TILE, F32)
    carry, longest = quick(lists, pose_in(sent_a), [pose_in(margin_a)], first_negc(), [0], no_sums(), nothing, None)
    for n, value in enumerate(carry + [longest]):
        part_ref[n] = value


def other_kernel(cells_hbm, sent_a, source_ref, part_ref, margin_a, margin_b, sums_ref, *scratch_refs):
    lists = Lists(cells_hbm, source_ref, (margin_a, margin_b), scratch_refs)
    own = pose_in(sent_a)
    nbrs = [pose_in(margin) for margin in (margin_a, margin_b)]
    part = [part_ref[n] for n in range(6)]
    carry, longest = quick(lists, own, nbrs, first_negc(), [1], part[:5], part[5], None)
    close(lists, own, nbrs, first_negc(), carry, longest, 0.0, sums_ref, None)


def first_negc():
    return jnp.full(TILE, -LOG2E / (2.0 * SPREAD_START), F32)


def solve(totals, old):
    def at(q):
        return spread_out(totals[:, q : q + 1])

    gram = {}
    for n, (a, b) in enumerate([(0, 0), (0, 1), (0, 2), (1, 1), (1, 2), (2, 2)]):
        gram[a, b] = at(QUAD + n)
    for a in range(3):
        gram[a, 3] = at(8 * a + 3)
    gram[3, 3] = at(SHARE)
    for a in range(4):
        gram[a, a] = gram[a, a] + REGULARIZE
    lower, diag, inverse = {}, [], []
    for j in range(4):
        scaled = [lower[j, k] * diag[k] for k in range(j)]
        pivot = gram[j, j]
        for k in range(j):
            pivot = pivot - lower[j, k] * scaled[k]
        diag.append(pivot)
        inverse.append(1.0 / pivot)
        for i in range(j + 1, 4):
            value = gram[j, i]
            for k in range(j):
                value = value - lower[i, k] * scaled[k]
            lower[i, j] = value * inverse[j]
    new = [None] * 12
    for k in range(3):
        right = []
        for m in range(4):
            j = 3 * k + m if m < 3 else 9 + k
            value = at(8 * m + k) + REGULARIZE * spread_out(old[:, j : j + 1])
            for n in range(m):
                value = value - lower[m, n] * right[n]
            right.append(value)
        found = [None] * 4
        for m in reversed(range(4)):
            value = right[m] * inverse[m]
            for n in range(m + 1, 4):
                value = value - lower[n, m] * found[n]
            found[m] = value
        for m in range(4):
            new[3 * k + m if m < 3 else 9 + k] = found[m]
    return new


def line_sum(all_ref, line, segs):
    return jnp.sum(all_ref[pl.ds(line * segs, segs), :], axis=0, keepdims=True)


def new_spread(all_ref):
    everything = jnp.sum(all_ref[...], axis=0, keepdims=True)
    top = spread_out(everything[:, ENERGY : ENERGY + 1]) + PRIOR_TOP
    return top / (3.0 * spread_out(everything[:, SHARE : SHARE + 1]) + PRIOR_BOTTOM)


def pose_row(new, first):
    lane = lax.broadcasted_iota(jnp.int32, (1, 128), 1)
    row = jnp.zeros((1, 128), F32)
    for j in range(12):
        row = jnp.where(lane == first + j, new[j][:1, :], row)
    return row


def second_kernel(
    lines, segs, cells_hbm, sent_a, all_ref, source_ref, margin_a, margin_b,
    sums_ref, out_hbm, out_ref, out_sem, *scratch_refs,
):
    line = lax.axis_index("line")
    lists = Lists(cells_hbm, source_ref, (margin_a, margin_b), scratch_refs)
    partner = [jnp.clip(line + 2 * d - 1, 0, lines - 1) for d in lists.dirs]
    sub = iota(0)

    def stacked(a, b, c):
        return jnp.where(sub == 0, spread_out(a), jnp.where(sub == 1, spread_out(b), spread_out(c)))

    totals = stacked(*[line_sum(all_ref, n, segs) for n in (line, partner[0], partner[1])])
    old = stacked(*[ref[3 * MROWS : 3 * MROWS + 1, :] for ref in (sent_a, margin_a, margin_b)])
    new = solve(totals, old)
    negc = (-0.5 * LOG2E) / new_spread(all_ref)
    own, *nbrs = [[spread_out(value[n : n + 1, :]) for value in new] for n in range(3)]
    carry, longest = quick(lists, own, nbrs, negc, [0, 1], no_sums(), jnp.zeros(TILE, F32), out_ref)
    close(lists, own, nbrs, negc, carry, longest, pose_row(new, POSE), sums_ref, (out_hbm, out_ref, out_sem))


def last_kernel(segs, all_ref, fitted_ref, spread_ref):
    line = lax.axis_index("line")
    totals = spread_out(line_sum(all_ref, line, segs))
    old = all_ref[pl.ds(line * segs, 1), :][:, POSE : POSE + 12]
    new = solve(totals, jnp.broadcast_to(old, (8, 12)))
    fitted_ref[...] = pose_row(new, 0)[:, :12]
    spread_ref[...] = new_spread(all_ref)[:1, :1]


def vmem(count):
    return [pl.BlockSpec(memory_space=pltpu.VMEM)] * count


ANY = pl.BlockSpec(memory_space=pl.ANY)
HBM = pl.BlockSpec(memory_space=pltpu.HBM)
SMEM = pl.BlockSpec(memory_space=pltpu.SMEM)
PARAMS = pltpu.CompilerParams(vmem_limit_bytes=32 * 1024 * 1024)


def scratch():
    return [
        pltpu.VMEM((2, 3, MROWS, 128), F32),
        pltpu.VMEM((3, 128, 128), F32),
        pltpu.VMEM((3, 128, 128), F32),
    ]


def in_hbm(value):
    return pltpu.with_memory_space_constraint(value, pltpu.HBM)


def pair_cost(cells, sides):
    pairs = cells.size // 2 * sides * BLOCK * CT
    return pl.CostEstimate(flops=400 * pairs, bytes_accessed=1 << 20, transcendentals=pairs)


def gather_call(rows, sent_a, sent_b):
    return pl.pallas_call(
        gather_kernel,
        in_specs=vmem(3),
        out_specs=vmem(1)[0],
        out_shape=jax.ShapeDtypeStruct((4,) + rows.shape, F32),
        compiler_params=PARAMS,
        cost_estimate=pl.CostEstimate(flops=10**11, bytes_accessed=1 << 20, transcendentals=0),
        name="gather_sources",
    )(rows, sent_a, sent_b)


def partner_call(cells, sent_a, source, margin_a):
    return pl.pallas_call(
        partner_kernel,
        in_specs=[SMEM] + vmem(3),
        out_specs=vmem(1)[0],
        out_shape=jax.ShapeDtypeStruct((6,) + TILE, F32),
        scratch_shapes=scratch(),
        compiler_params=PARAMS,
        cost_estimate=pair_cost(cells, 1),
        name="match_partner",
    )(cells, sent_a, source, margin_a)


def other_call(cells, sent_a, source, part, margin_a, margin_b, devices):
    return pl.pallas_call(
        other_kernel,
        in_specs=[SMEM] + vmem(5),
        out_specs=vmem(1)[0],
        out_shape=jax.ShapeDtypeStruct((devices, 128), F32),
        scratch_shapes=scratch(),
        compiler_params=PARAMS,
        cost_estimate=pair_cost(cells, 1),
        name="match_other",
    )(cells, sent_a, source, part, margin_a, margin_b)


def second_call(cells, sent_a, everyone, source, margin_a, margin_b, lines, segs):
    result = (5,) + source.shape[1:]
    return pl.pallas_call(
        functools.partial(second_kernel, lines, segs),
        in_specs=[SMEM] + vmem(5),
        out_specs=vmem(1) + [ANY],
        out_shape=[jax.ShapeDtypeStruct((lines * segs, 128), F32), jax.ShapeDtypeStruct(result, F32)],
        scratch_shapes=[pltpu.VMEM(result, F32), pltpu.SemaphoreType.DMA] + scratch(),
        compiler_params=PARAMS,
        cost_estimate=pair_cost(cells, 2),
        name="match_second",
    )(cells, sent_a, everyone, source, margin_a, margin_b)


def exchange(sums):
    return lax.all_to_all(sums, ("line", "seg"), 0, 0)


def on_device(lines, segs, points, rows, cells, pose):
    own_points = points.reshape(3, -1, 128)
    slots = rows.shape[-1]
    blocks = slots // BLOCK
    row_list = rows.reshape(2, blocks, 128).transpose(1, 0, 2).reshape(2 * blocks, 128)
    cell_ids = cells.reshape(2, blocks)
    sent_a, sent_b, cell_ids = pack_call(in_hbm(own_points), in_hbm(pose.reshape(1, 12)), in_hbm(cell_ids))
    cell_ids = pltpu.with_memory_space_constraint(cell_ids, pltpu.SMEM)
    pairs_a = [(i, i ^ 1) for i in range(lines)]
    pairs_b = [(i, (((i + 1) ^ 1) - 1) % lines) for i in range(lines)]
    margin_a = lax.ppermute(sent_a, "line", pairs_a)
    margin_b = lax.ppermute(sent_b, "line", pairs_b)
    source = gather_call(row_list, sent_a, sent_b)
    part = partner_call(cell_ids, sent_a, source, margin_a)
    sums = other_call(cell_ids, sent_a, source, part, margin_a, margin_b, lines * segs)
    everyone = exchange(sums)
    sums, result = second_call(cell_ids, sent_a, everyone, source, margin_a, margin_b, lines, segs)
    everyone = exchange(sums)
    fitted, spread = pl.pallas_call(
        functools.partial(last_kernel, segs),
        in_specs=vmem(1),
        out_specs=vmem(2),
        out_shape=[jax.ShapeDtypeStruct((1, 12), F32), jax.ShapeDtypeStruct((1, 1), F32)],
        compiler_params=PARAMS,
        name="solve_last",
    )(everyone)
    result = result.reshape(5, blocks, 2, 128).transpose(2, 0, 1, 3).reshape(1, 1, 2, 5, slots)
    return (result, fitted.reshape(12, 1), spread.reshape(1))


def solution(mesh):
    return jax.shard_map(
        functools.partial(on_device, mesh.shape["line"], mesh.shape["seg"]),
        mesh=mesh,
        in_specs=(
            P("line", "seg", None, None),
            P("line", "seg", None, None),
            P("line", "seg", None, None),
            P(None, "line"),
        ),
        out_specs=(P("line", "seg", None, None, None), P(None, "line"), P()),
        check_vma=False,
    )
```

```python
import functools
import math

import jax
import jax.numpy as jnp
from jax import lax
from jax.experimental import pallas as pl
from jax.experimental.pallas import tpu as pltpu
from jax.sharding import PartitionSpec as P

NCELL = 16
CT = 512
BLOCK = 128
MARGIN = NCELL * CT
MROWS = MARGIN // 128
TILES = CT // 128
GROUPS = BLOCK // 8
LEAD = 48
NEAR = 1
LAG = 3
WIDE = 4
QUICK_LIMIT = 1000.0
ENERGY_LIMIT = 400.0

OUTLIER_MASS = 1.0
SPREAD_START = 0.05
PRIOR_TOP = 0.05
PRIOR_BOTTOM = 1.0
REGULARIZE = 1.0
LOG2E = math.log2(math.e)

F32 = jnp.float32
BF16 = jnp.bfloat16
TILE = (8, 128)
ONE = 24
SHARE = ONE + 3
ENERGY = ONE + 4
QUAD = 32
POSE = 64


def iota(axis):
    return lax.broadcasted_iota(jnp.int32, TILE, axis)


def spread_out(value):
    return jnp.broadcast_to(value, TILE)


def pack_kernel(points_hbm, pose_hbm, cells_hbm, sent_a, sent_b, cells_ref, pose_ref, sems):
    odd = lax.axis_index("line") & 1
    tail = points_hbm.shape[1] - MROWS
    copies = [
        pltpu.make_async_copy(pose_hbm, pose_ref, sems.at[6]),
        pltpu.make_async_copy(cells_hbm, cells_ref, sems.at[7]),
    ]
    for n, (sent, first) in enumerate(((sent_a, (1 - odd) * tail), (sent_b, odd * tail))):
        spot = pl.ds(pl.multiple_of(first, MROWS), MROWS)
        for k in range(3):
            copies.append(
                pltpu.make_async_copy(points_hbm.at[k, spot, :], sent.at[pl.ds(MROWS * k, MROWS), :], sems.at[3 * n + k])
            )
    for copy in copies:
        copy.start()
    for sent in (sent_a, sent_b):
        sent[3 * MROWS :, :] = jnp.zeros(TILE, F32)
    copies[0].wait()
    for sent in (sent_a, sent_b):
        sent[3 * MROWS : 3 * MROWS + 1, :12] = pose_ref[...]
    for copy in copies[1:]:
        copy.wait()


def pack_call(points, pose, cells):
    return pl.pallas_call(
        pack_kernel,
        in_specs=[HBM] * 3,
        out_specs=vmem(2) + [SMEM],
        out_shape=[jax.ShapeDtypeStruct((3 * MROWS + 8, 128), F32)] * 2 + [pltpu.SMEM(cells.shape, jnp.int32)],
        scratch_shapes=[pltpu.VMEM((1, 12), F32), pltpu.SemaphoreType.DMA((8,))],
        compiler_params=PARAMS,
        name="pack_margins",
    )(points, pose, cells)


def pick_columns(rows_ref, margin_parts, rows):
    spots = [jnp.maximum(rows_ref[pl.ds(row, 1), :], 0) & (MARGIN - 1) for row in rows]
    hits = []
    for spot in spots:
        low = spread_out(spot & 127)
        hit = [(low == iota(0) + 8 * v).astype(F32) for v in range(16)]
        hits.append(jnp.concatenate(hit, axis=0).astype(BF16))
    hit = jnp.concatenate(hits, axis=1)
    return spots, jnp.dot(margin_parts, jnp.concatenate([hit] * 3, axis=0), preferred_element_type=F32)


def pick_rows(source_ref, rows, spots, picked):
    for n, row in enumerate(rows):
        high = spread_out(spots[n] >> 7)
        sums = [jnp.zeros(TILE, F32)] * 3
        for v in range(MROWS // 8):
            here = high == iota(0) + 8 * v
            for k in range(3):
                first = MROWS * k + 8 * v
                sums[k] = jnp.where(here, picked[first : first + 8, 128 * n : 128 * n + 128], sums[k])
        for k in range(3):
            source_ref[k, pl.ds(row, 1), :] = jnp.sum(sums[k], axis=0, keepdims=True)


def apply_pose(coefs, xyz):
    out = []
    for k in range(3):
        total = coefs[3 * k] * xyz[0]
        total = total + coefs[3 * k + 1] * xyz[1]
        total = total + coefs[3 * k + 2] * xyz[2]
        out.append(total + coefs[9 + k])
    return out


def column(coefs, first, stride):
    sub = iota(0)
    out = jnp.zeros(TILE, F32)
    for k in range(3):
        out = jnp.where(sub == k, coefs[first + stride * k], out)
    return out


def columns(coefs):
    return [column(coefs, k, 3) for k in range(3)] + [column(coefs, 9, 1)]


def squared_length(value):
    square = value * value
    return spread_out(square[0:1, :]) + spread_out(square[1:2, :]) + spread_out(square[2:3, :])


def three_parts(value):
    high = value.astype(BF16).astype(F32)
    rest = value - high
    middle = rest.astype(BF16).astype(F32)
    return high, middle, rest - middle


def combine(cols, xyz):
    return cols[0] * xyz[0] + cols[1] * xyz[1] + cols[2] * xyz[2]


def features_of(near, margin_ref, cell):
    sub = iota(0)
    tiles, longest = [], None
    for t in range(TILES):
        row = cell * TILES + t
        y = combine(near, [spread_out(margin_ref[pl.ds(k * MROWS + row, 1), :]) for k in range(3)])
        length = squared_length(y)
        longest = length if longest is None else jnp.maximum(longest, length)
        high, middle, low = three_parts(jnp.where(sub == 3, length, jnp.where(sub == 4, 1.0, y)))
        tiles.append(jnp.concatenate([high, middle, low, high, middle, high], axis=0).astype(BF16))
    return jnp.concatenate(tiles, axis=1), longest


def longest_source(own, near, dirs, source_ref):
    longest = jnp.zeros(TILE, F32)
    for v in range(source_ref.shape[1] // 8):
        rows = slice(8 * v, 8 * v + 8)
        xyz = [source_ref[k, rows, :] for k in range(3)]
        moved = apply_pose(own, xyz)
        for side in range(2):
            square = sum((moved[k] - near[side][9 + k]) ** 2 for k in range(3))
            listed = (iota(0) & 1) == dirs[side]
            longest = jnp.maximum(longest, jnp.where(listed, square * source_ref[3, rows, :], 0.0))
    return longest


def coefficients(negc, own, near, source_ref, place):
    side, row, _ = place
    sub = iota(0)
    xt = [spread_out(source_ref[k, pl.ds(row, 1), :]) for k in range(4)]
    m = combine(own, xt) + (own[3] - near[side][3])
    length = squared_length(m)
    coef = jnp.where(sub == 3, negc, jnp.where(sub == 4, negc * length, (-2.0 * negc) * m))
    high, middle, low = three_parts(coef)
    stack = jnp.concatenate([high, high, high, middle, middle, low], axis=0)
    return jnp.transpose(stack).astype(BF16), xt, m, length


def weigh(features, coef):
    power = jnp.dot(coef, features, preferred_element_type=F32)
    weight = jnp.transpose(jnp.exp2(power))
    top = weight.astype(BF16)
    rest = (weight - top.astype(F32)).astype(BF16)
    return features[:32], jnp.concatenate([top, rest], axis=1)


def weighted_sums(features, weights):
    sums = jnp.dot(features, weights, preferred_element_type=F32)
    sums = sums[:, :BLOCK] + sums[:, BLOCK:]
    return sums[0:8] + sums[8:16] + sums[16:24]


def finish(near, side, xt, m, length, sums):
    sub = iota(0)
    total = spread_out(sums[4:5, :])
    around = combine([spread_out(m[k : k + 1, :]) for k in range(3)], [spread_out(sums[k : k + 1, :]) for k in range(3)])
    energy = spread_out(sums[3:4, :]) - 2.0 * around + length * total
    raw = jnp.where(sub < 3, sums + near[side][3] * total, jnp.where(sub == 3, total, jnp.where(sub == 4, energy, 0.0)))
    return jnp.where(xt[3] > 0.0, raw / (total + OUTLIER_MASS), 0.0), xt


class Lists:
    def __init__(self, cells_ref, source_ref, margin_refs, scratch_refs):
        self.dirs = sides_of(lax.axis_index("line"))
        self.source_ref = source_ref
        self.margin_refs = margin_refs
        self.cells_ref = cells_ref
        self.world_ref, self.moved_ref, self.column_ref = scratch_refs

    def places(self, side):
        return [(side, 2 * b + self.dirs[side], b) for b in range(self.cells_ref.shape[1])]

    def cell(self, place):
        side, _, b = place
        return self.cells_ref[self.dirs[side], b]


def quick(lists, own, nbrs, negc, sides, carry, longest, out_ref):
    own_cols, near_cols = columns(own), {side: columns(nbrs[side]) for side in sides}
    places = [place for side in sides for place in lists.places(side)]
    coefs, feats, found = {}, {}, {}
    ahead = None
    for n in range(-1, len(places) + LAG):
        block, ahead = ahead, None
        for later in range(0 if n < 0 else n + 1 + LEAD, min(n + 2 + LEAD, len(places))):
            coefs[later] = coefficients(negc, own_cols, near_cols, lists.source_ref, places[later])
        for later in range(0 if n < 0 else n + 1 + NEAR, min(n + 2 + NEAR, len(places))):
            side = places[later][0]
            cell = jnp.maximum(lists.cell(places[later]), 0)
            feats[later], length = features_of(near_cols[side], lists.margin_refs[side], cell)
            longest = jnp.maximum(longest, length)
        if n + 1 < len(places):
            ahead = weigh(feats.pop(n + 1), coefs[n + 1][0])
        if block is not None:
            found[n] = weighted_sums(*block)
        if n >= LAG:
            side, row, _ = places[n - LAG]
            result, xt = finish(near_cols, side, *coefs[n - LAG][1:], found[n - LAG])
            carry = add_block(carry, row, result, xt, out_ref)
    return carry, longest


def no_sums():
    return [jnp.zeros(TILE, F32) for _ in range(5)]


def close(lists, own, nbrs, negc, carry, longest, pose_row, sums_ref, out):
    out_ref = None if out is None else out[1]
    if out is not None:
        save = pltpu.make_async_copy(out[1], out[0], out[2])
        save.start()
    pack_sums(carry, pose_row, sums_ref)
    size = jnp.max(longest) + jnp.max(longest_source(own, nbrs, lists.dirs, lists.source_ref))
    share, energy = [jnp.sum(carry[3][q : q + 1, :]) for q in (3, 4)]
    bad = (size * jnp.max(-negc) > QUICK_LIMIT) | (size * share > ENERGY_LIMIT * energy)

    @pl.when(bad)
    def _():
        if out is not None:
            save.wait()
        one_block = careful_setup(
            own, nbrs, negc, lists.source_ref, lists.margin_refs, lists.world_ref, lists.moved_ref, lists.column_ref
        )
        carry = tuple(no_sums())
        for side in range(2):
            d = lists.dirs[side]

            def step(b, carry, side=side, d=d):
                result, xt = one_block(side, 2 * b + d, lists.cells_ref[d, b])
                return tuple(add_block(carry, 2 * b + d, result, xt, out_ref))

            carry = lax.fori_loop(0, lists.cells_ref.shape[1], step, carry)
        pack_sums(carry, pose_row, sums_ref)
        if out is not None:
            save.start()

    if out is not None:
        save.wait()


def add_block(carry, row, result, xt, out_ref):
    sub = iota(0)
    if out_ref is not None:
        for q in range(5):
            out_ref[q, pl.ds(row, 1), :] = result[q : q + 1, :]
    left = jnp.where(sub < 3, xt[0], jnp.where(sub < 5, xt[1], xt[2]))
    right = jnp.where(sub == 0, xt[0], jnp.where((sub == 1) | (sub == 3), xt[1], xt[2]))
    share = spread_out(result[3:4, :])
    return [
        carry[0] + result * xt[0],
        carry[1] + result * xt[1],
        carry[2] + result * xt[2],
        carry[3] + result,
        carry[4] + share * (left * right),
    ]


def careful_setup(own, nbrs, negc, source_ref, margin_refs, world_ref, moved_ref, column_ref):
    slot_rows = source_ref.shape[1]
    for v in range(slot_rows // 8):
        xyz = [source_ref[k, 8 * v : 8 * v + 8, :] for k in range(3)]
        for k, value in enumerate(apply_pose(own, xyz)):
            moved_ref[k, 8 * v : 8 * v + 8, :] = value
    for k in range(3):
        column_ref[k] = jnp.transpose(moved_ref[k])
    for side in range(2):
        for v in range(MROWS // 8):
            xyz = [margin_refs[side][k * MROWS + 8 * v : k * MROWS + 8 * v + 8, :] for k in range(3)]
            for k, value in enumerate(apply_pose(nbrs[side], xyz)):
                world_ref[side, k, 8 * v : 8 * v + 8, :] = value
    lane = iota(1)

    def one_block(side, row, cell):
        first = jnp.maximum(cell, 0) * TILES
        target = [
            [spread_out(world_ref[side, k, pl.ds(first + t, 1), :]) for t in range(TILES)] for k in range(3)
        ]
        pick = jnp.full(TILE, row, jnp.int32)
        parts = []
        for g in range(GROUPS):
            m = [
                jnp.take_along_axis(column_ref[k, 8 * g : 8 * g + 8, :], pick, axis=1, mode="promise_in_bounds")
                for k in range(3)
            ]
            sums = None
            for t in range(TILES):
                d = [m[k] - target[k][t] for k in range(3)]
                dist = d[0] * d[0] + d[1] * d[1] + d[2] * d[2]
                weight = jnp.exp2(dist * negc)
                terms = [weight * target[k][t] for k in range(3)] + [weight, weight * dist]
                sums = terms if sums is None else [a + b for a, b in zip(sums, terms)]
            part = jnp.zeros(TILE, F32)
            for q in range(5):
                part = jnp.where(lane == q, jnp.sum(sums[q], axis=1, keepdims=True), part)
            parts.append(part)
        flat = jnp.transpose(jnp.concatenate(parts, axis=0))[:8, :]
        xt = [spread_out(source_ref[k, pl.ds(row, 1), :]) for k in range(4)]
        return flat * (xt[3] / (spread_out(flat[3:4, :]) + OUTLIER_MASS)), xt

    return one_block


def pack_sums(sums, pose_row, out_ref):
    lane, sub = iota(1), iota(0)
    total = jnp.zeros(TILE, F32)
    for c in range(5):
        total = total + jnp.where(lane == 8 * c + sub, jnp.sum(sums[c], axis=1, keepdims=True), 0.0)
    row = jnp.sum(total, axis=0, keepdims=True)
    out_ref[...] = jnp.broadcast_to(row + pose_row, out_ref.shape)


def pose_of_row(row):
    return [spread_out(row[:, j : j + 1]) for j in range(12)]


def sides_of(line):
    odd = line & 1
    return [1 - odd, odd]


def pose_in(margin_ref):
    return pose_of_row(margin_ref[3 * MROWS : 3 * MROWS + 1, :])


def gather_kernel(rows_ref, sent_a, sent_b, source_ref):
    dirs = sides_of(lax.axis_index("line"))
    slot_rows = rows_ref.shape[0]
    blocks = slot_rows // 2
    for v in range(slot_rows // 8):
        source_ref[3, 8 * v : 8 * v + 8, :] = (rows_ref[8 * v : 8 * v + 8, :] >= 0).astype(F32)
    last = None
    for side, sent in enumerate((sent_a, sent_b)):
        parts = jnp.concatenate(three_parts(sent[: 3 * MROWS, :]), axis=1).astype(BF16)
        for first in range(0, blocks, WIDE):
            rows = [2 * b + dirs[side] for b in range(first, min(first + WIDE, blocks))]
            found = rows, *pick_columns(rows_ref, parts, rows)
            if last is not None:
                pick_rows(source_ref, *last)
            last = found
    pick_rows(source_ref, *last)


def partner_kernel(cells_hbm, sent_a, source_ref, margin_a, part_ref, *scratch_refs):
    lists = Lists(cells_hbm, source_ref, (margin_a, None), scratch_refs)
    nothing = jnp.zeros(TILE, F32)
    carry, longest = quick(lists, pose_in(sent_a), [pose_in(margin_a)], first_negc(), [0], no_sums(), nothing, None)
    for n, value in enumerate(carry + [longest]):
        part_ref[n] = value


def other_kernel(cells_hbm, sent_a, source_ref, part_ref, margin_a, margin_b, sums_ref, *scratch_refs):
    lists = Lists(cells_hbm, source_ref, (margin_a, margin_b), scratch_refs)
    own = pose_in(sent_a)
    nbrs = [pose_in(margin) for margin in (margin_a, margin_b)]
    part = [part_ref[n] for n in range(6)]
    carry, longest = quick(lists, own, nbrs, first_negc(), [1], part[:5], part[5], None)
    close(lists, own, nbrs, first_negc(), carry, longest, 0.0, sums_ref, None)


def first_negc():
    return jnp.full(TILE, -LOG2E / (2.0 * SPREAD_START), F32)


def solve(totals, old):
    def at(q):
        return spread_out(totals[:, q : q + 1])

    gram = {}
    for n, (a, b) in enumerate([(0, 0), (0, 1), (0, 2), (1, 1), (1, 2), (2, 2)]):
        gram[a, b] = at(QUAD + n)
    for a in range(3):
        gram[a, 3] = at(8 * a + 3)
    gram[3, 3] = at(SHARE)
    for a in range(4):
        gram[a, a] = gram[a, a] + REGULARIZE
    lower, diag, inverse = {}, [], []
    for j in range(4):
        scaled = [lower[j, k] * diag[k] for k in range(j)]
        pivot = gram[j, j]
        for k in range(j):
            pivot = pivot - lower[j, k] * scaled[k]
        diag.append(pivot)
        inverse.append(1.0 / pivot)
        for i in range(j + 1, 4):
            value = gram[j, i]
            for k in range(j):
                value = value - lower[i, k] * scaled[k]
            lower[i, j] = value * inverse[j]
    new = [None] * 12
    for k in range(3):
        right = []
        for m in range(4):
            j = 3 * k + m if m < 3 else 9 + k
            value = at(8 * m + k) + REGULARIZE * spread_out(old[:, j : j + 1])
            for n in range(m):
                value = value - lower[m, n] * right[n]
            right.append(value)
        found = [None] * 4
        for m in reversed(range(4)):
            value = right[m] * inverse[m]
            for n in range(m + 1, 4):
                value = value - lower[n, m] * found[n]
            found[m] = value
        for m in range(4):
            new[3 * k + m if m < 3 else 9 + k] = found[m]
    return new


def line_sum(all_ref, line, segs):
    return jnp.sum(all_ref[pl.ds(line * segs, segs), :], axis=0, keepdims=True)


def new_spread(all_ref):
    everything = jnp.sum(all_ref[...], axis=0, keepdims=True)
    top = spread_out(everything[:, ENERGY : ENERGY + 1]) + PRIOR_TOP
    return top / (3.0 * spread_out(everything[:, SHARE : SHARE + 1]) + PRIOR_BOTTOM)


def pose_row(new, first):
    lane = lax.broadcasted_iota(jnp.int32, (1, 128), 1)
    row = jnp.zeros((1, 128), F32)
    for j in range(12):
        row = jnp.where(lane == first + j, new[j][:1, :], row)
    return row


def second_kernel(
    lines, segs, cells_hbm, sent_a, all_ref, source_ref, margin_a, margin_b,
    sums_ref, out_hbm, out_ref, out_sem, *scratch_refs,
):
    line = lax.axis_index("line")
    lists = Lists(cells_hbm, source_ref, (margin_a, margin_b), scratch_refs)
    partner = [jnp.clip(line + 2 * d - 1, 0, lines - 1) for d in lists.dirs]
    sub = iota(0)

    def stacked(a, b, c):
        return jnp.where(sub == 0, spread_out(a), jnp.where(sub == 1, spread_out(b), spread_out(c)))

    totals = stacked(*[line_sum(all_ref, n, segs) for n in (line, partner[0], partner[1])])
    old = stacked(*[ref[3 * MROWS : 3 * MROWS + 1, :] for ref in (sent_a, margin_a, margin_b)])
    new = solve(totals, old)
    negc = (-0.5 * LOG2E) / new_spread(all_ref)
    own, *nbrs = [[spread_out(value[n : n + 1, :]) for value in new] for n in range(3)]
    carry, longest = quick(lists, own, nbrs, negc, [0, 1], no_sums(), jnp.zeros(TILE, F32), out_ref)
    close(lists, own, nbrs, negc, carry, longest, pose_row(new, POSE), sums_ref, (out_hbm, out_ref, out_sem))


def last_kernel(segs, all_ref, fitted_ref, spread_ref):
    line = lax.axis_index("line")
    totals = spread_out(line_sum(all_ref, line, segs))
    old = all_ref[pl.ds(line * segs, 1), :][:, POSE : POSE + 12]
    new = solve(totals, jnp.broadcast_to(old, (8, 12)))
    fitted_ref[...] = pose_row(new, 0)[:, :12]
    spread_ref[...] = new_spread(all_ref)[:1, :1]


def vmem(count):
    return [pl.BlockSpec(memory_space=pltpu.VMEM)] * count


ANY = pl.BlockSpec(memory_space=pl.ANY)
HBM = pl.BlockSpec(memory_space=pltpu.HBM)
SMEM = pl.BlockSpec(memory_space=pltpu.SMEM)
PARAMS = pltpu.CompilerParams(vmem_limit_bytes=32 * 1024 * 1024)


def scratch():
    return [
        pltpu.VMEM((2, 3, MROWS, 128), F32),
        pltpu.VMEM((3, 128, 128), F32),
        pltpu.VMEM((3, 128, 128), F32),
    ]


def in_hbm(value):
    return pltpu.with_memory_space_constraint(value, pltpu.HBM)


def pair_cost(cells, sides):
    pairs = cells.size // 2 * sides * BLOCK * CT
    return pl.CostEstimate(flops=400 * pairs, bytes_accessed=1 << 20, transcendentals=pairs)


def gather_call(rows, sent_a, sent_b):
    return pl.pallas_call(
        gather_kernel,
        in_specs=vmem(3),
        out_specs=vmem(1)[0],
        out_shape=jax.ShapeDtypeStruct((4,) + rows.shape, F32),
        compiler_params=PARAMS,
        cost_estimate=pl.CostEstimate(flops=10**11, bytes_accessed=1 << 20, transcendentals=0),
        name="gather_sources",
    )(rows, sent_a, sent_b)


def partner_call(cells, sent_a, source, margin_a):
    return pl.pallas_call(
        partner_kernel,
        in_specs=[SMEM] + vmem(3),
        out_specs=vmem(1)[0],
        out_shape=jax.ShapeDtypeStruct((6,) + TILE, F32),
        scratch_shapes=scratch(),
        compiler_params=PARAMS,
        cost_estimate=pair_cost(cells, 1),
        name="match_partner",
    )(cells, sent_a, source, margin_a)


def other_call(cells, sent_a, source, part, margin_a, margin_b, devices):
    return pl.pallas_call(
        other_kernel,
        in_specs=[SMEM] + vmem(5),
        out_specs=vmem(1)[0],
        out_shape=jax.ShapeDtypeStruct((devices, 128), F32),
        scratch_shapes=scratch(),
        compiler_params=PARAMS,
        cost_estimate=pair_cost(cells, 1),
        name="match_other",
    )(cells, sent_a, source, part, margin_a, margin_b)


def second_call(cells, sent_a, everyone, source, margin_a, margin_b, lines, segs):
    result = (5,) + source.shape[1:]
    return pl.pallas_call(
        functools.partial(second_kernel, lines, segs),
        in_specs=[SMEM] + vmem(5),
        out_specs=vmem(1) + [ANY],
        out_shape=[jax.ShapeDtypeStruct((lines * segs, 128), F32), jax.ShapeDtypeStruct(result, F32)],
        scratch_shapes=[pltpu.VMEM(result, F32), pltpu.SemaphoreType.DMA] + scratch(),
        compiler_params=PARAMS,
        cost_estimate=pair_cost(cells, 2),
        name="match_second",
    )(cells, sent_a, everyone, source, margin_a, margin_b)


def exchange(sums):
    return lax.all_to_all(sums, ("line", "seg"), 0, 0)


def on_device(lines, segs, points, rows, cells, pose):
    own_points = points.reshape(3, -1, 128)
    slots = rows.shape[-1]
    blocks = slots // BLOCK
    row_list = rows.reshape(2, blocks, 128).transpose(1, 0, 2).reshape(2 * blocks, 128)
    cell_ids = cells.reshape(2, blocks)
    sent_a, sent_b, cell_ids = pack_call(in_hbm(own_points), in_hbm(pose.reshape(1, 12)), in_hbm(cell_ids))
    cell_ids = pltpu.with_memory_space_constraint(cell_ids, pltpu.SMEM)
    pairs_a = [(i, i ^ 1) for i in range(lines)]
    pairs_b = [(i, (((i + 1) ^ 1) - 1) % lines) for i in range(lines)]
    margin_a = lax.ppermute(sent_a, "line", pairs_a)
    margin_b = lax.ppermute(sent_b, "line", pairs_b)
    source = gather_call(row_list, sent_a, sent_b)
    part = partner_call(cell_ids, sent_a, source, margin_a)
    sums = other_call(cell_ids, sent_a, source, part, margin_a, margin_b, lines * segs)
    everyone = exchange(sums)
    sums, result = second_call(cell_ids, sent_a, everyone, source, margin_a, margin_b, lines, segs)
    everyone = exchange(sums)
    fitted, spread = pl.pallas_call(
        functools.partial(last_kernel, segs),
        in_specs=vmem(1),
        out_specs=vmem(2),
        out_shape=[jax.ShapeDtypeStruct((1, 12), F32), jax.ShapeDtypeStruct((1, 1), F32)],
        compiler_params=PARAMS,
        name="solve_last",
    )(everyone)
    result = result.reshape(5, blocks, 2, 128).transpose(2, 0, 1, 3).reshape(1, 1, 2, 5, slots)
    return (result, fitted.reshape(12, 1), spread.reshape(1))


def solution(mesh):
    return jax.shard_map(
        functools.partial(on_device, mesh.shape["line"], mesh.shape["seg"]),
        mesh=mesh,
        in_specs=(
            P("line", "seg", None, None),
            P("line", "seg", None, None),
            P("line", "seg", None, None),
            P(None, "line"),
        ),
        out_specs=(P("line", "seg", None, None, None), P(None, "line"), P()),
        check_vma=False,
    )
```

```python
import functools
import math

import jax
import jax.numpy as jnp
from jax import lax
from jax.experimental import pallas as pl
from jax.experimental.pallas import tpu as pltpu
from jax.sharding import PartitionSpec as P

NCELL = 16
CT = 512
BLOCK = 128
MARGIN = NCELL * CT
MROWS = MARGIN // 128
TILES = CT // 128
GROUPS = BLOCK // 8
LEAD = 8
NEAR = 1
LAG = 3
WIDE = 4
QUICK_LIMIT = 1000.0
ENERGY_LIMIT = 400.0

OUTLIER_MASS = 1.0
SPREAD_START = 0.05
PRIOR_TOP = 0.05
PRIOR_BOTTOM = 1.0
REGULARIZE = 1.0
LOG2E = math.log2(math.e)

F32 = jnp.float32
BF16 = jnp.bfloat16
TILE = (8, 128)
ONE = 24
SHARE = ONE + 3
ENERGY = ONE + 4
QUAD = 32
POSE = 64


def iota(axis):
    return lax.broadcasted_iota(jnp.int32, TILE, axis)


def spread_out(value):
    return jnp.broadcast_to(value, TILE)


def pack_kernel(points_hbm, pose_hbm, cells_hbm, sent_a, sent_b, cells_ref, pose_ref, sems):
    odd = lax.axis_index("line") & 1
    tail = points_hbm.shape[1] - MROWS
    copies = [
        pltpu.make_async_copy(pose_hbm, pose_ref, sems.at[6]),
        pltpu.make_async_copy(cells_hbm, cells_ref, sems.at[7]),
    ]
    for n, (sent, first) in enumerate(((sent_a, (1 - odd) * tail), (sent_b, odd * tail))):
        spot = pl.ds(pl.multiple_of(first, MROWS), MROWS)
        for k in range(3):
            copies.append(
                pltpu.make_async_copy(points_hbm.at[k, spot, :], sent.at[pl.ds(MROWS * k, MROWS), :], sems.at[3 * n + k])
            )
    for copy in copies:
        copy.start()
    for sent in (sent_a, sent_b):
        sent[3 * MROWS :, :] = jnp.zeros(TILE, F32)
    copies[0].wait()
    for sent in (sent_a, sent_b):
        sent[3 * MROWS : 3 * MROWS + 1, :12] = pose_ref[...]
    for copy in copies[1:]:
        copy.wait()


def pack_call(points, pose, cells):
    return pl.pallas_call(
        pack_kernel,
        in_specs=[HBM] * 3,
        out_specs=vmem(2) + [SMEM],
        out_shape=[jax.ShapeDtypeStruct((3 * MROWS + 8, 128), F32)] * 2 + [pltpu.SMEM(cells.shape, jnp.int32)],
        scratch_shapes=[pltpu.VMEM((1, 12), F32), pltpu.SemaphoreType.DMA((8,))],
        compiler_params=PARAMS,
        name="pack_margins",
    )(points, pose, cells)


def pick_columns(rows_ref, margin_parts, rows):
    spots = [jnp.maximum(rows_ref[pl.ds(row, 1), :], 0) & (MARGIN - 1) for row in rows]
    hits = []
    for spot in spots:
        low = spread_out(spot & 127)
        hit = [(low == iota(0) + 8 * v).astype(F32) for v in range(16)]
        hits.append(jnp.concatenate(hit, axis=0).astype(BF16))
    hit = jnp.concatenate(hits, axis=1)
    return spots, jnp.dot(margin_parts, jnp.concatenate([hit] * 3, axis=0), preferred_element_type=F32)


def pick_rows(source_ref, rows, spots, picked):
    for n, row in enumerate(rows):
        high = spread_out(spots[n] >> 7)
        sums = [jnp.zeros(TILE, F32)] * 3
        for v in range(MROWS // 8):
            here = high == iota(0) + 8 * v
            for k in range(3):
                first = MROWS * k + 8 * v
                sums[k] = jnp.where(here, picked[first : first + 8, 128 * n : 128 * n + 128], sums[k])
        for k in range(3):
            source_ref[k, pl.ds(row, 1), :] = jnp.sum(sums[k], axis=0, keepdims=True)


def apply_pose(coefs, xyz):
    out = []
    for k in range(3):
        total = coefs[3 * k] * xyz[0]
        total = total + coefs[3 * k + 1] * xyz[1]
        total = total + coefs[3 * k + 2] * xyz[2]
        out.append(total + coefs[9 + k])
    return out


def column(coefs, first, stride):
    sub = iota(0)
    out = jnp.zeros(TILE, F32)
    for k in range(3):
        out = jnp.where(sub == k, coefs[first + stride * k], out)
    return out


def columns(coefs):
    return [column(coefs, k, 3) for k in range(3)] + [column(coefs, 9, 1)]


def squared_length(value):
    square = value * value
    return spread_out(square[0:1, :]) + spread_out(square[1:2, :]) + spread_out(square[2:3, :])


def three_parts(value):
    high = value.astype(BF16).astype(F32)
    rest = value - high
    middle = rest.astype(BF16).astype(F32)
    return high, middle, rest - middle


def combine(cols, xyz):
    return cols[0] * xyz[0] + cols[1] * xyz[1] + cols[2] * xyz[2]


def features_of(near, margin_ref, cell):
    sub = iota(0)
    tiles, longest = [], None
    for t in range(TILES):
        row = cell * TILES + t
        y = combine(near, [spread_out(margin_ref[pl.ds(k * MROWS + row, 1), :]) for k in range(3)])
        length = squared_length(y)
        longest = length if longest is None else jnp.maximum(longest, length)
        high, middle, low = three_parts(jnp.where(sub == 3, length, jnp.where(sub == 4, 1.0, y)))
        tiles.append(jnp.concatenate([high, middle, low, high, middle, high], axis=0).astype(BF16))
    return jnp.concatenate(tiles, axis=1), longest


def longest_source(own, near, dirs, source_ref):
    longest = jnp.zeros(TILE, F32)
    for v in range(source_ref.shape[1] // 8):
        rows = slice(8 * v, 8 * v + 8)
        xyz = [source_ref[k, rows, :] for k in range(3)]
        moved = apply_pose(own, xyz)
        for side in range(2):
            square = sum((moved[k] - near[side][9 + k]) ** 2 for k in range(3))
            listed = (iota(0) & 1) == dirs[side]
            longest = jnp.maximum(longest, jnp.where(listed, square * source_ref[3, rows, :], 0.0))
    return longest


def coefficients(negc, own, near, source_ref, place):
    side, row, _ = place
    sub = iota(0)
    xt = [spread_out(source_ref[k, pl.ds(row, 1), :]) for k in range(4)]
    m = combine(own, xt) + (own[3] - near[side][3])
    length = squared_length(m)
    coef = jnp.where(sub == 3, negc, jnp.where(sub == 4, negc * length, (-2.0 * negc) * m))
    high, middle, low = three_parts(coef)
    stack = jnp.concatenate([high, high, high, middle, middle, low], axis=0)
    return jnp.transpose(stack).astype(BF16), xt, m, length


def weigh(features, coef):
    power = jnp.dot(coef, features, preferred_element_type=F32)
    weight = jnp.transpose(jnp.exp2(power))
    top = weight.astype(BF16)
    rest = (weight - top.astype(F32)).astype(BF16)
    return features[:32], jnp.concatenate([top, rest], axis=1)


def weighted_sums(features, weights):
    sums = jnp.dot(features, weights, preferred_element_type=F32)
    sums = sums[:, :BLOCK] + sums[:, BLOCK:]
    return sums[0:8] + sums[8:16] + sums[16:24]


def finish(near, side, xt, m, length, sums):
    sub = iota(0)
    total = spread_out(sums[4:5, :])
    around = combine([spread_out(m[k : k + 1, :]) for k in range(3)], [spread_out(sums[k : k + 1, :]) for k in range(3)])
    energy = spread_out(sums[3:4, :]) - 2.0 * around + length * total
    raw = jnp.where(sub < 3, sums + near[side][3] * total, jnp.where(sub == 3, total, jnp.where(sub == 4, energy, 0.0)))
    return jnp.where(xt[3] > 0.0, raw / (total + OUTLIER_MASS), 0.0), xt


class Lists:
    def __init__(self, cells_ref, source_ref, margin_refs, scratch_refs):
        self.dirs = sides_of(lax.axis_index("line"))
        self.source_ref = source_ref
        self.margin_refs = margin_refs
        self.cells_ref = cells_ref
        self.world_ref, self.moved_ref, self.column_ref = scratch_refs

    def places(self, side):
        return [(side, 2 * b + self.dirs[side], b) for b in range(self.cells_ref.shape[1])]

    def cell(self, place):
        side, _, b = place
        return self.cells_ref[self.dirs[side], b]


def quick(lists, own, nbrs, negc, sides, carry, longest, out_ref):
    own_cols, near_cols = columns(own), {side: columns(nbrs[side]) for side in sides}
    places = [place for side in sides for place in lists.places(side)]
    coefs, feats, found = {}, {}, {}
    ahead = None
    for n in range(-1, len(places) + LAG):
        block, ahead = ahead, None
        for later in range(0 if n < 0 else n + 1 + LEAD, min(n + 2 + LEAD, len(places))):
            coefs[later] = coefficients(negc, own_cols, near_cols, lists.source_ref, places[later])
        for later in range(0 if n < 0 else n + 1 + NEAR, min(n + 2 + NEAR, len(places))):
            side = places[later][0]
            cell = jnp.maximum(lists.cell(places[later]), 0)
            feats[later], length = features_of(near_cols[side], lists.margin_refs[side], cell)
            longest = jnp.maximum(longest, length)
        if n + 1 < len(places):
            ahead = weigh(feats.pop(n + 1), coefs[n + 1][0])
        if block is not None:
            found[n] = weighted_sums(*block)
        if n >= LAG:
            side, row, _ = places[n - LAG]
            result, xt = finish(near_cols, side, *coefs[n - LAG][1:], found[n - LAG])
            carry = add_block(carry, row, result, xt, out_ref)
    return carry, longest


def no_sums():
    return [jnp.zeros(TILE, F32) for _ in range(5)]


def close(lists, own, nbrs, negc, carry, longest, pose_row, sums_ref, out):
    out_ref = None if out is None else out[1]
    if out is not None:
        save = pltpu.make_async_copy(out[1], out[0], out[2])
        save.start()
    pack_sums(carry, pose_row, sums_ref)
    size = jnp.max(longest) + jnp.max(longest_source(own, nbrs, lists.dirs, lists.source_ref))
    share, energy = [jnp.sum(carry[3][q : q + 1, :]) for q in (3, 4)]
    bad = (size * jnp.max(-negc) > QUICK_LIMIT) | (size * share > ENERGY_LIMIT * energy)

    @pl.when(bad)
    def _():
        if out is not None:
            save.wait()
        one_block = careful_setup(
            own, nbrs, negc, lists.source_ref, lists.margin_refs, lists.world_ref, lists.moved_ref, lists.column_ref
        )
        carry = tuple(no_sums())
        for side in range(2):
            d = lists.dirs[side]

            def step(b, carry, side=side, d=d):
                result, xt = one_block(side, 2 * b + d, lists.cells_ref[d, b])
                return tuple(add_block(carry, 2 * b + d, result, xt, out_ref))

            carry = lax.fori_loop(0, lists.cells_ref.shape[1], step, carry)
        pack_sums(carry, pose_row, sums_ref)
        if out is not None:
            save.start()

    if out is not None:
        save.wait()


def add_block(carry, row, result, xt, out_ref):
    sub = iota(0)
    if out_ref is not None:
        for q in range(5):
            out_ref[q, pl.ds(row, 1), :] = result[q : q + 1, :]
    left = jnp.where(sub < 3, xt[0], jnp.where(sub < 5, xt[1], xt[2]))
    right = jnp.where(sub == 0, xt[0], jnp.where((sub == 1) | (sub == 3), xt[1], xt[2]))
    share = spread_out(result[3:4, :])
    return [
        carry[0] + result * xt[0],
        carry[1] + result * xt[1],
        carry[2] + result * xt[2],
        carry[3] + result,
        carry[4] + share * (left * right),
    ]


def careful_setup(own, nbrs, negc, source_ref, margin_refs, world_ref, moved_ref, column_ref):
    slot_rows = source_ref.shape[1]
    for v in range(slot_rows // 8):
        xyz = [source_ref[k, 8 * v : 8 * v + 8, :] for k in range(3)]
        for k, value in enumerate(apply_pose(own, xyz)):
            moved_ref[k, 8 * v : 8 * v + 8, :] = value
    for k in range(3):
        column_ref[k] = jnp.transpose(moved_ref[k])
    for side in range(2):
        for v in range(MROWS // 8):
            xyz = [margin_refs[side][k * MROWS + 8 * v : k * MROWS + 8 * v + 8, :] for k in range(3)]
            for k, value in enumerate(apply_pose(nbrs[side], xyz)):
                world_ref[side, k, 8 * v : 8 * v + 8, :] = value
    lane = iota(1)

    def one_block(side, row, cell):
        first = jnp.maximum(cell, 0) * TILES
        target = [
            [spread_out(world_ref[side, k, pl.ds(first + t, 1), :]) for t in range(TILES)] for k in range(3)
        ]
        pick = jnp.full(TILE, row, jnp.int32)
        parts = []
        for g in range(GROUPS):
            m = [
                jnp.take_along_axis(column_ref[k, 8 * g : 8 * g + 8, :], pick, axis=1, mode="promise_in_bounds")
                for k in range(3)
            ]
            sums = None
            for t in range(TILES):
                d = [m[k] - target[k][t] for k in range(3)]
                dist = d[0] * d[0] + d[1] * d[1] + d[2] * d[2]
                weight = jnp.exp2(dist * negc)
                terms = [weight * target[k][t] for k in range(3)] + [weight, weight * dist]
                sums = terms if sums is None else [a + b for a, b in zip(sums, terms)]
            part = jnp.zeros(TILE, F32)
            for q in range(5):
                part = jnp.where(lane == q, jnp.sum(sums[q], axis=1, keepdims=True), part)
            parts.append(part)
        flat = jnp.transpose(jnp.concatenate(parts, axis=0))[:8, :]
        xt = [spread_out(source_ref[k, pl.ds(row, 1), :]) for k in range(4)]
        return flat * (xt[3] / (spread_out(flat[3:4, :]) + OUTLIER_MASS)), xt

    return one_block


def pack_sums(sums, pose_row, out_ref):
    lane, sub = iota(1), iota(0)
    total = jnp.zeros(TILE, F32)
    for c in range(5):
        total = total + jnp.where(lane == 8 * c + sub, jnp.sum(sums[c], axis=1, keepdims=True), 0.0)
    row = jnp.sum(total, axis=0, keepdims=True)
    out_ref[...] = jnp.broadcast_to(row + pose_row, out_ref.shape)


def pose_of_row(row):
    return [spread_out(row[:, j : j + 1]) for j in range(12)]


def sides_of(line):
    odd = line & 1
    return [1 - odd, odd]


def pose_in(margin_ref):
    return pose_of_row(margin_ref[3 * MROWS : 3 * MROWS + 1, :])


def gather_kernel(rows_ref, sent_a, sent_b, source_ref):
    dirs = sides_of(lax.axis_index("line"))
    slot_rows = rows_ref.shape[0]
    blocks = slot_rows // 2
    for v in range(slot_rows // 8):
        source_ref[3, 8 * v : 8 * v + 8, :] = (rows_ref[8 * v : 8 * v + 8, :] >= 0).astype(F32)
    last = None
    for side, sent in enumerate((sent_a, sent_b)):
        parts = jnp.concatenate(three_parts(sent[: 3 * MROWS, :]), axis=1).astype(BF16)
        for first in range(0, blocks, WIDE):
            rows = [2 * b + dirs[side] for b in range(first, min(first + WIDE, blocks))]
            found = rows, *pick_columns(rows_ref, parts, rows)
            if last is not None:
                pick_rows(source_ref, *last)
            last = found
    pick_rows(source_ref, *last)


def partner_kernel(cells_hbm, sent_a, source_ref, margin_a, part_ref, *scratch_refs):
    lists = Lists(cells_hbm, source_ref, (margin_a, None), scratch_refs)
    nothing = jnp.zeros(TILE, F32)
    carry, longest = quick(lists, pose_in(sent_a), [pose_in(margin_a)], first_negc(), [0], no_sums(), nothing, None)
    for n, value in enumerate(carry + [longest]):
        part_ref[n] = value


def other_kernel(cells_hbm, sent_a, source_ref, part_ref, margin_a, margin_b, sums_ref, *scratch_refs):
    lists = Lists(cells_hbm, source_ref, (margin_a, margin_b), scratch_refs)
    own = pose_in(sent_a)
    nbrs = [pose_in(margin) for margin in (margin_a, margin_b)]
    part = [part_ref[n] for n in range(6)]
    carry, longest = quick(lists, own, nbrs, first_negc(), [1], part[:5], part[5], None)
    close(lists, own, nbrs, first_negc(), carry, longest, 0.0, sums_ref, None)


def first_negc():
    return jnp.full(TILE, -LOG2E / (2.0 * SPREAD_START), F32)


def solve(totals, old):
    def at(q):
        return spread_out(totals[:, q : q + 1])

    gram = {}
    for n, (a, b) in enumerate([(0, 0), (0, 1), (0, 2), (1, 1), (1, 2), (2, 2)]):
        gram[a, b] = at(QUAD + n)
    for a in range(3):
        gram[a, 3] = at(8 * a + 3)
    gram[3, 3] = at(SHARE)
    for a in range(4):
        gram[a, a] = gram[a, a] + REGULARIZE
    lower, diag, inverse = {}, [], []
    for j in range(4):
        scaled = [lower[j, k] * diag[k] for k in range(j)]
        pivot = gram[j, j]
        for k in range(j):
            pivot = pivot - lower[j, k] * scaled[k]
        diag.append(pivot)
        inverse.append(1.0 / pivot)
        for i in range(j + 1, 4):
            value = gram[j, i]
            for k in range(j):
                value = value - lower[i, k] * scaled[k]
            lower[i, j] = value * inverse[j]
    new = [None] * 12
    for k in range(3):
        right = []
        for m in range(4):
            j = 3 * k + m if m < 3 else 9 + k
            value = at(8 * m + k) + REGULARIZE * spread_out(old[:, j : j + 1])
            for n in range(m):
                value = value - lower[m, n] * right[n]
            right.append(value)
        found = [None] * 4
        for m in reversed(range(4)):
            value = right[m] * inverse[m]
            for n in range(m + 1, 4):
                value = value - lower[n, m] * found[n]
            found[m] = value
        for m in range(4):
            new[3 * k + m if m < 3 else 9 + k] = found[m]
    return new


def line_sum(all_ref, line, segs):
    return jnp.sum(all_ref[pl.ds(line * segs, segs), :], axis=0, keepdims=True)


def new_spread(all_ref):
    everything = jnp.sum(all_ref[...], axis=0, keepdims=True)
    top = spread_out(everything[:, ENERGY : ENERGY + 1]) + PRIOR_TOP
    return top / (3.0 * spread_out(everything[:, SHARE : SHARE + 1]) + PRIOR_BOTTOM)


def pose_row(new, first):
    lane = lax.broadcasted_iota(jnp.int32, (1, 128), 1)
    row = jnp.zeros((1, 128), F32)
    for j in range(12):
        row = jnp.where(lane == first + j, new[j][:1, :], row)
    return row


def second_kernel(
    lines, segs, cells_hbm, sent_a, all_ref, source_ref, margin_a, margin_b,
    sums_ref, out_hbm, out_ref, out_sem, *scratch_refs,
):
    line = lax.axis_index("line")
    lists = Lists(cells_hbm, source_ref, (margin_a, margin_b), scratch_refs)
    partner = [jnp.clip(line + 2 * d - 1, 0, lines - 1) for d in lists.dirs]
    sub = iota(0)

    def stacked(a, b, c):
        return jnp.where(sub == 0, spread_out(a), jnp.where(sub == 1, spread_out(b), spread_out(c)))

    totals = stacked(*[line_sum(all_ref, n, segs) for n in (line, partner[0], partner[1])])
    old = stacked(*[ref[3 * MROWS : 3 * MROWS + 1, :] for ref in (sent_a, margin_a, margin_b)])
    new = solve(totals, old)
    negc = (-0.5 * LOG2E) / new_spread(all_ref)
    own, *nbrs = [[spread_out(value[n : n + 1, :]) for value in new] for n in range(3)]
    carry, longest = quick(lists, own, nbrs, negc, [0, 1], no_sums(), jnp.zeros(TILE, F32), out_ref)
    close(lists, own, nbrs, negc, carry, longest, pose_row(new, POSE), sums_ref, (out_hbm, out_ref, out_sem))


def last_kernel(segs, all_ref, fitted_ref, spread_ref):
    line = lax.axis_index("line")
    totals = spread_out(line_sum(all_ref, line, segs))
    old = all_ref[pl.ds(line * segs, 1), :][:, POSE : POSE + 12]
    new = solve(totals, jnp.broadcast_to(old, (8, 12)))
    fitted_ref[...] = pose_row(new, 0)[:, :12]
    spread_ref[...] = new_spread(all_ref)[:1, :1]


def vmem(count):
    return [pl.BlockSpec(memory_space=pltpu.VMEM)] * count


ANY = pl.BlockSpec(memory_space=pl.ANY)
HBM = pl.BlockSpec(memory_space=pltpu.HBM)
SMEM = pl.BlockSpec(memory_space=pltpu.SMEM)
PARAMS = pltpu.CompilerParams(vmem_limit_bytes=32 * 1024 * 1024)


def scratch():
    return [
        pltpu.VMEM((2, 3, MROWS, 128), F32),
        pltpu.VMEM((3, 128, 128), F32),
        pltpu.VMEM((3, 128, 128), F32),
    ]


def in_hbm(value):
    return pltpu.with_memory_space_constraint(value, pltpu.HBM)


def pair_cost(cells, sides):
    pairs = cells.size // 2 * sides * BLOCK * CT
    return pl.CostEstimate(flops=400 * pairs, bytes_accessed=1 << 20, transcendentals=pairs)


def gather_call(rows, sent_a, sent_b):
    return pl.pallas_call(
        gather_kernel,
        in_specs=vmem(3),
        out_specs=vmem(1)[0],
        out_shape=jax.ShapeDtypeStruct((4,) + rows.shape, F32),
        compiler_params=PARAMS,
        cost_estimate=pl.CostEstimate(flops=10**11, bytes_accessed=1 << 20, transcendentals=0),
        name="gather_sources",
    )(rows, sent_a, sent_b)


def partner_call(cells, sent_a, source, margin_a):
    return pl.pallas_call(
        partner_kernel,
        in_specs=[SMEM] + vmem(3),
        out_specs=vmem(1)[0],
        out_shape=jax.ShapeDtypeStruct((6,) + TILE, F32),
        scratch_shapes=scratch(),
        compiler_params=PARAMS,
        cost_estimate=pair_cost(cells, 1),
        name="match_partner",
    )(cells, sent_a, source, margin_a)


def other_call(cells, sent_a, source, part, margin_a, margin_b, devices):
    return pl.pallas_call(
        other_kernel,
        in_specs=[SMEM] + vmem(5),
        out_specs=vmem(1)[0],
        out_shape=jax.ShapeDtypeStruct((devices, 128), F32),
        scratch_shapes=scratch(),
        compiler_params=PARAMS,
        cost_estimate=pair_cost(cells, 1),
        name="match_other",
    )(cells, sent_a, source, part, margin_a, margin_b)


def second_call(cells, sent_a, everyone, source, margin_a, margin_b, lines, segs):
    result = (5,) + source.shape[1:]
    return pl.pallas_call(
        functools.partial(second_kernel, lines, segs),
        in_specs=[SMEM] + vmem(5),
        out_specs=vmem(1) + [ANY],
        out_shape=[jax.ShapeDtypeStruct((lines * segs, 128), F32), jax.ShapeDtypeStruct(result, F32)],
        scratch_shapes=[pltpu.VMEM(result, F32), pltpu.SemaphoreType.DMA] + scratch(),
        compiler_params=PARAMS,
        cost_estimate=pair_cost(cells, 2),
        name="match_second",
    )(cells, sent_a, everyone, source, margin_a, margin_b)


def exchange(sums):
    return lax.all_to_all(sums, ("line", "seg"), 0, 0)


def on_device(lines, segs, points, rows, cells, pose):
    own_points = points.reshape(3, -1, 128)
    slots = rows.shape[-1]
    blocks = slots // BLOCK
    row_list = rows.reshape(2, blocks, 128).transpose(1, 0, 2).reshape(2 * blocks, 128)
    cell_ids = cells.reshape(2, blocks)
    sent_a, sent_b, cell_ids = pack_call(in_hbm(own_points), in_hbm(pose.reshape(1, 12)), in_hbm(cell_ids))
    cell_ids = pltpu.with_memory_space_constraint(cell_ids, pltpu.SMEM)
    pairs_a = [(i, i ^ 1) for i in range(lines)]
    pairs_b = [(i, (((i + 1) ^ 1) - 1) % lines) for i in range(lines)]
    margin_a = lax.ppermute(sent_a, "line", pairs_a)
    margin_b = lax.ppermute(sent_b, "line", pairs_b)
    source = gather_call(row_list, sent_a, sent_b)
    part = partner_call(cell_ids, sent_a, source, margin_a)
    sums = other_call(cell_ids, sent_a, source, part, margin_a, margin_b, lines * segs)
    everyone = exchange(sums)
    sums, result = second_call(cell_ids, sent_a, everyone, source, margin_a, margin_b, lines, segs)
    everyone = exchange(sums)
    fitted, spread = pl.pallas_call(
        functools.partial(last_kernel, segs),
        in_specs=vmem(1),
        out_specs=vmem(2),
        out_shape=[jax.ShapeDtypeStruct((1, 12), F32), jax.ShapeDtypeStruct((1, 1), F32)],
        compiler_params=PARAMS,
        name="solve_last",
    )(everyone)
    result = result.reshape(5, blocks, 2, 128).transpose(2, 0, 1, 3).reshape(1, 1, 2, 5, slots)
    return (result, fitted.reshape(12, 1), spread.reshape(1))


def solution(mesh):
    return jax.shard_map(
        functools.partial(on_device, mesh.shape["line"], mesh.shape["seg"]),
        mesh=mesh,
        in_specs=(
            P("line", "seg", None, None),
            P("line", "seg", None, None),
            P("line", "seg", None, None),
            P(None, "line"),
        ),
        out_specs=(P("line", "seg", None, None, None), P(None, "line"), P()),
        check_vma=False,
    )
```

```python
import functools
import math

import jax
import jax.numpy as jnp
from jax import lax
from jax.experimental import pallas as pl
from jax.experimental.pallas import tpu as pltpu
from jax.sharding import PartitionSpec as P

NCELL = 16
CT = 512
BLOCK = 128
MARGIN = NCELL * CT
MROWS = MARGIN // 128
TILES = CT // 128
GROUPS = BLOCK // 8
LEAD = 8
NEAR = 2
LAG = 3
WIDE = 4
QUICK_LIMIT = 1000.0
ENERGY_LIMIT = 400.0

OUTLIER_MASS = 1.0
SPREAD_START = 0.05
PRIOR_TOP = 0.05
PRIOR_BOTTOM = 1.0
REGULARIZE = 1.0
LOG2E = math.log2(math.e)

F32 = jnp.float32
BF16 = jnp.bfloat16
TILE = (8, 128)
ONE = 24
SHARE = ONE + 3
ENERGY = ONE + 4
QUAD = 32
POSE = 64


def iota(axis):
    return lax.broadcasted_iota(jnp.int32, TILE, axis)


def spread_out(value):
    return jnp.broadcast_to(value, TILE)


def pack_kernel(points_hbm, pose_hbm, cells_hbm, sent_a, sent_b, cells_ref, pose_ref, sems):
    odd = lax.axis_index("line") & 1
    tail = points_hbm.shape[1] - MROWS
    copies = [
        pltpu.make_async_copy(pose_hbm, pose_ref, sems.at[6]),
        pltpu.make_async_copy(cells_hbm, cells_ref, sems.at[7]),
    ]
    for n, (sent, first) in enumerate(((sent_a, (1 - odd) * tail), (sent_b, odd * tail))):
        spot = pl.ds(pl.multiple_of(first, MROWS), MROWS)
        for k in range(3):
            copies.append(
                pltpu.make_async_copy(points_hbm.at[k, spot, :], sent.at[pl.ds(MROWS * k, MROWS), :], sems.at[3 * n + k])
            )
    for copy in copies:
        copy.start()
    for sent in (sent_a, sent_b):
        sent[3 * MROWS :, :] = jnp.zeros(TILE, F32)
    copies[0].wait()
    for sent in (sent_a, sent_b):
        sent[3 * MROWS : 3 * MROWS + 1, :12] = pose_ref[...]
    for copy in copies[1:]:
        copy.wait()


def pack_call(points, pose, cells):
    return pl.pallas_call(
        pack_kernel,
        in_specs=[HBM] * 3,
        out_specs=vmem(2) + [SMEM],
        out_shape=[jax.ShapeDtypeStruct((3 * MROWS + 8, 128), F32)] * 2 + [pltpu.SMEM(cells.shape, jnp.int32)],
        scratch_shapes=[pltpu.VMEM((1, 12), F32), pltpu.SemaphoreType.DMA((8,))],
        compiler_params=PARAMS,
        name="pack_margins",
    )(points, pose, cells)


def pick_columns(rows_ref, margin_parts, rows):
    spots = [jnp.maximum(rows_ref[pl.ds(row, 1), :], 0) & (MARGIN - 1) for row in rows]
    hits = []
    for spot in spots:
        low = spread_out(spot & 127)
        hit = [(low == iota(0) + 8 * v).astype(F32) for v in range(16)]
        hits.append(jnp.concatenate(hit, axis=0).astype(BF16))
    hit = jnp.concatenate(hits, axis=1)
    return spots, jnp.dot(margin_parts, jnp.concatenate([hit] * 3, axis=0), preferred_element_type=F32)


def pick_rows(source_ref, rows, spots, picked):
    for n, row in enumerate(rows):
        high = spread_out(spots[n] >> 7)
        sums = [jnp.zeros(TILE, F32)] * 3
        for v in range(MROWS // 8):
            here = high == iota(0) + 8 * v
            for k in range(3):
                first = MROWS * k + 8 * v
                sums[k] = jnp.where(here, picked[first : first + 8, 128 * n : 128 * n + 128], sums[k])
        for k in range(3):
            source_ref[k, pl.ds(row, 1), :] = jnp.sum(sums[k], axis=0, keepdims=True)


def apply_pose(coefs, xyz):
    out = []
    for k in range(3):
        total = coefs[3 * k] * xyz[0]
        total = total + coefs[3 * k + 1] * xyz[1]
        total = total + coefs[3 * k + 2] * xyz[2]
        out.append(total + coefs[9 + k])
    return out


def column(coefs, first, stride):
    sub = iota(0)
    out = jnp.zeros(TILE, F32)
    for k in range(3):
        out = jnp.where(sub == k, coefs[first + stride * k], out)
    return out


def columns(coefs):
    return [column(coefs, k, 3) for k in range(3)] + [column(coefs, 9, 1)]


def squared_length(value):
    square = value * value
    return spread_out(square[0:1, :]) + spread_out(square[1:2, :]) + spread_out(square[2:3, :])


def three_parts(value):
    high = value.astype(BF16).astype(F32)
    rest = value - high
    middle = rest.astype(BF16).astype(F32)
    return high, middle, rest - middle


def combine(cols, xyz):
    return cols[0] * xyz[0] + cols[1] * xyz[1] + cols[2] * xyz[2]


def features_of(near, margin_ref, cell):
    sub = iota(0)
    tiles, longest = [], None
    for t in range(TILES):
        row = cell * TILES + t
        y = combine(near, [spread_out(margin_ref[pl.ds(k * MROWS + row, 1), :]) for k in range(3)])
        length = squared_length(y)
        longest = length if longest is None else jnp.maximum(longest, length)
        high, middle, low = three_parts(jnp.where(sub == 3, length, jnp.where(sub == 4, 1.0, y)))
        tiles.append(jnp.concatenate([high, middle, low, high, middle, high], axis=0).astype(BF16))
    return jnp.concatenate(tiles, axis=1), longest


def longest_source(own, near, dirs, source_ref):
    longest = jnp.zeros(TILE, F32)
    for v in range(source_ref.shape[1] // 8):
        rows = slice(8 * v, 8 * v + 8)
        xyz = [source_ref[k, rows, :] for k in range(3)]
        moved = apply_pose(own, xyz)
        for side in range(2):
            square = sum((moved[k] - near[side][9 + k]) ** 2 for k in range(3))
            listed = (iota(0) & 1) == dirs[side]
            longest = jnp.maximum(longest, jnp.where(listed, square * source_ref[3, rows, :], 0.0))
    return longest


def coefficients(negc, own, near, source_ref, place):
    side, row, _ = place
    sub = iota(0)
    xt = [spread_out(source_ref[k, pl.ds(row, 1), :]) for k in range(4)]
    m = combine(own, xt) + (own[3] - near[side][3])
    length = squared_length(m)
    coef = jnp.where(sub == 3, negc, jnp.where(sub == 4, negc * length, (-2.0 * negc) * m))
    high, middle, low = three_parts(coef)
    stack = jnp.concatenate([high, high, high, middle, middle, low], axis=0)
    return jnp.transpose(stack).astype(BF16), xt, m, length


def weigh(features, coef):
    power = jnp.dot(coef, features, preferred_element_type=F32)
    weight = jnp.transpose(jnp.exp2(power))
    top = weight.astype(BF16)
    rest = (weight - top.astype(F32)).astype(BF16)
    return features[:32], jnp.concatenate([top, rest], axis=1)


def weighted_sums(features, weights):
    sums = jnp.dot(features, weights, preferred_element_type=F32)
    sums = sums[:, :BLOCK] + sums[:, BLOCK:]
    return sums[0:8] + sums[8:16] + sums[16:24]


def finish(near, side, xt, m, length, sums):
    sub = iota(0)
    total = spread_out(sums[4:5, :])
    around = combine([spread_out(m[k : k + 1, :]) for k in range(3)], [spread_out(sums[k : k + 1, :]) for k in range(3)])
    energy = spread_out(sums[3:4, :]) - 2.0 * around + length * total
    raw = jnp.where(sub < 3, sums + near[side][3] * total, jnp.where(sub == 3, total, jnp.where(sub == 4, energy, 0.0)))
    return jnp.where(xt[3] > 0.0, raw / (total + OUTLIER_MASS), 0.0), xt


class Lists:
    def __init__(self, cells_ref, source_ref, margin_refs, scratch_refs):
        self.dirs = sides_of(lax.axis_index("line"))
        self.source_ref = source_ref
        self.margin_refs = margin_refs
        self.cells_ref = cells_ref
        self.world_ref, self.moved_ref, self.column_ref = scratch_refs

    def places(self, side):
        return [(side, 2 * b + self.dirs[side], b) for b in range(self.cells_ref.shape[1])]

    def cell(self, place):
        side, _, b = place
        return self.cells_ref[self.dirs[side], b]


def quick(lists, own, nbrs, negc, sides, carry, longest, out_ref):
    own_cols, near_cols = columns(own), {side: columns(nbrs[side]) for side in sides}
    places = [place for side in sides for place in lists.places(side)]
    coefs, feats, found = {}, {}, {}
    ahead = None
    for n in range(-1, len(places) + LAG):
        block, ahead = ahead, None
        for later in range(0 if n < 0 else n + 1 + LEAD, min(n + 2 + LEAD, len(places))):
            coefs[later] = coefficients(negc, own_cols, near_cols, lists.source_ref, places[later])
        for later in range(0 if n < 0 else n + 1 + NEAR, min(n + 2 + NEAR, len(places))):
            side = places[later][0]
            cell = jnp.maximum(lists.cell(places[later]), 0)
            feats[later], length = features_of(near_cols[side], lists.margin_refs[side], cell)
            longest = jnp.maximum(longest, length)
        if n + 1 < len(places):
            ahead = weigh(feats.pop(n + 1), coefs[n + 1][0])
        if block is not None:
            found[n] = weighted_sums(*block)
        if n >= LAG:
            side, row, _ = places[n - LAG]
            result, xt = finish(near_cols, side, *coefs[n - LAG][1:], found[n - LAG])
            carry = add_block(carry, row, result, xt, out_ref)
    return carry, longest


def no_sums():
    return [jnp.zeros(TILE, F32) for _ in range(5)]


def close(lists, own, nbrs, negc, carry, longest, pose_row, sums_ref, out):
    out_ref = None if out is None else out[1]
    if out is not None:
        save = pltpu.make_async_copy(out[1], out[0], out[2])
        save.start()
    pack_sums(carry, pose_row, sums_ref)
    size = jnp.max(longest) + jnp.max(longest_source(own, nbrs, lists.dirs, lists.source_ref))
    share, energy = [jnp.sum(carry[3][q : q + 1, :]) for q in (3, 4)]
    bad = (size * jnp.max(-negc) > QUICK_LIMIT) | (size * share > ENERGY_LIMIT * energy)

    @pl.when(bad)
    def _():
        if out is not None:
            save.wait()
        one_block = careful_setup(
            own, nbrs, negc, lists.source_ref, lists.margin_refs, lists.world_ref, lists.moved_ref, lists.column_ref
        )
        carry = tuple(no_sums())
        for side in range(2):
            d = lists.dirs[side]

            def step(b, carry, side=side, d=d):
                result, xt = one_block(side, 2 * b + d, lists.cells_ref[d, b])
                return tuple(add_block(carry, 2 * b + d, result, xt, out_ref))

            carry = lax.fori_loop(0, lists.cells_ref.shape[1], step, carry)
        pack_sums(carry, pose_row, sums_ref)
        if out is not None:
            save.start()

    if out is not None:
        save.wait()


def add_block(carry, row, result, xt, out_ref):
    sub = iota(0)
    if out_ref is not None:
        for q in range(5):
            out_ref[q, pl.ds(row, 1), :] = result[q : q + 1, :]
    left = jnp.where(sub < 3, xt[0], jnp.where(sub < 5, xt[1], xt[2]))
    right = jnp.where(sub == 0, xt[0], jnp.where((sub == 1) | (sub == 3), xt[1], xt[2]))
    share = spread_out(result[3:4, :])
    return [
        carry[0] + result * xt[0],
        carry[1] + result * xt[1],
        carry[2] + result * xt[2],
        carry[3] + result,
        carry[4] + share * (left * right),
    ]


def careful_setup(own, nbrs, negc, source_ref, margin_refs, world_ref, moved_ref, column_ref):
    slot_rows = source_ref.shape[1]
    for v in range(slot_rows // 8):
        xyz = [source_ref[k, 8 * v : 8 * v + 8, :] for k in range(3)]
        for k, value in enumerate(apply_pose(own, xyz)):
            moved_ref[k, 8 * v : 8 * v + 8, :] = value
    for k in range(3):
        column_ref[k] = jnp.transpose(moved_ref[k])
    for side in range(2):
        for v in range(MROWS // 8):
            xyz = [margin_refs[side][k * MROWS + 8 * v : k * MROWS + 8 * v + 8, :] for k in range(3)]
            for k, value in enumerate(apply_pose(nbrs[side], xyz)):
                world_ref[side, k, 8 * v : 8 * v + 8, :] = value
    lane = iota(1)

    def one_block(side, row, cell):
        first = jnp.maximum(cell, 0) * TILES
        target = [
            [spread_out(world_ref[side, k, pl.ds(first + t, 1), :]) for t in range(TILES)] for k in range(3)
        ]
        pick = jnp.full(TILE, row, jnp.int32)
        parts = []
        for g in range(GROUPS):
            m = [
                jnp.take_along_axis(column_ref[k, 8 * g : 8 * g + 8, :], pick, axis=1, mode="promise_in_bounds")
                for k in range(3)
            ]
            sums = None
            for t in range(TILES):
                d = [m[k] - target[k][t] for k in range(3)]
                dist = d[0] * d[0] + d[1] * d[1] + d[2] * d[2]
                weight = jnp.exp2(dist * negc)
                terms = [weight * target[k][t] for k in range(3)] + [weight, weight * dist]
                sums = terms if sums is None else [a + b for a, b in zip(sums, terms)]
            part = jnp.zeros(TILE, F32)
            for q in range(5):
                part = jnp.where(lane == q, jnp.sum(sums[q], axis=1, keepdims=True), part)
            parts.append(part)
        flat = jnp.transpose(jnp.concatenate(parts, axis=0))[:8, :]
        xt = [spread_out(source_ref[k, pl.ds(row, 1), :]) for k in range(4)]
        return flat * (xt[3] / (spread_out(flat[3:4, :]) + OUTLIER_MASS)), xt

    return one_block


def pack_sums(sums, pose_row, out_ref):
    lane, sub = iota(1), iota(0)
    total = jnp.zeros(TILE, F32)
    for c in range(5):
        total = total + jnp.where(lane == 8 * c + sub, jnp.sum(sums[c], axis=1, keepdims=True), 0.0)
    row = jnp.sum(total, axis=0, keepdims=True)
    out_ref[...] = jnp.broadcast_to(row + pose_row, out_ref.shape)


def pose_of_row(row):
    return [spread_out(row[:, j : j + 1]) for j in range(12)]


def sides_of(line):
    odd = line & 1
    return [1 - odd, odd]


def pose_in(margin_ref):
    return pose_of_row(margin_ref[3 * MROWS : 3 * MROWS + 1, :])


def gather_kernel(rows_ref, sent_a, sent_b, source_ref):
    dirs = sides_of(lax.axis_index("line"))
    slot_rows = rows_ref.shape[0]
    blocks = slot_rows // 2
    for v in range(slot_rows // 8):
        source_ref[3, 8 * v : 8 * v + 8, :] = (rows_ref[8 * v : 8 * v + 8, :] >= 0).astype(F32)
    last = None
    for side, sent in enumerate((sent_a, sent_b)):
        parts = jnp.concatenate(three_parts(sent[: 3 * MROWS, :]), axis=1).astype(BF16)
        for first in range(0, blocks, WIDE):
            rows = [2 * b + dirs[side] for b in range(first, min(first + WIDE, blocks))]
            found = rows, *pick_columns(rows_ref, parts, rows)
            if last is not None:
                pick_rows(source_ref, *last)
            last = found
    pick_rows(source_ref, *last)


def partner_kernel(cells_hbm, sent_a, source_ref, margin_a, part_ref, *scratch_refs):
    lists = Lists(cells_hbm, source_ref, (margin_a, None), scratch_refs)
    nothing = jnp.zeros(TILE, F32)
    carry, longest = quick(lists, pose_in(sent_a), [pose_in(margin_a)], first_negc(), [0], no_sums(), nothing, None)
    for n, value in enumerate(carry + [longest]):
        part_ref[n] = value


def other_kernel(cells_hbm, sent_a, source_ref, part_ref, margin_a, margin_b, sums_ref, *scratch_refs):
    lists = Lists(cells_hbm, source_ref, (margin_a, margin_b), scratch_refs)
    own = pose_in(sent_a)
    nbrs = [pose_in(margin) for margin in (margin_a, margin_b)]
    part = [part_ref[n] for n in range(6)]
    carry, longest = quick(lists, own, nbrs, first_negc(), [1], part[:5], part[5], None)
    close(lists, own, nbrs, first_negc(), carry, longest, 0.0, sums_ref, None)


def first_negc():
    return jnp.full(TILE, -LOG2E / (2.0 * SPREAD_START), F32)


def solve(totals, old):
    def at(q):
        return spread_out(totals[:, q : q + 1])

    gram = {}
    for n, (a, b) in enumerate([(0, 0), (0, 1), (0, 2), (1, 1), (1, 2), (2, 2)]):
        gram[a, b] = at(QUAD + n)
    for a in range(3):
        gram[a, 3] = at(8 * a + 3)
    gram[3, 3] = at(SHARE)
    for a in range(4):
        gram[a, a] = gram[a, a] + REGULARIZE
    lower, diag, inverse = {}, [], []
    for j in range(4):
        scaled = [lower[j, k] * diag[k] for k in range(j)]
        pivot = gram[j, j]
        for k in range(j):
            pivot = pivot - lower[j, k] * scaled[k]
        diag.append(pivot)
        inverse.append(1.0 / pivot)
        for i in range(j + 1, 4):
            value = gram[j, i]
            for k in range(j):
                value = value - lower[i, k] * scaled[k]
            lower[i, j] = value * inverse[j]
    new = [None] * 12
    for k in range(3):
        right = []
        for m in range(4):
            j = 3 * k + m if m < 3 else 9 + k
            value = at(8 * m + k) + REGULARIZE * spread_out(old[:, j : j + 1])
            for n in range(m):
                value = value - lower[m, n] * right[n]
            right.append(value)
        found = [None] * 4
        for m in reversed(range(4)):
            value = right[m] * inverse[m]
            for n in range(m + 1, 4):
                value = value - lower[n, m] * found[n]
            found[m] = value
        for m in range(4):
            new[3 * k + m if m < 3 else 9 + k] = found[m]
    return new


def line_sum(all_ref, line, segs):
    return jnp.sum(all_ref[pl.ds(line * segs, segs), :], axis=0, keepdims=True)


def new_spread(all_ref):
    everything = jnp.sum(all_ref[...], axis=0, keepdims=True)
    top = spread_out(everything[:, ENERGY : ENERGY + 1]) + PRIOR_TOP
    return top / (3.0 * spread_out(everything[:, SHARE : SHARE + 1]) + PRIOR_BOTTOM)


def pose_row(new, first):
    lane = lax.broadcasted_iota(jnp.int32, (1, 128), 1)
    row = jnp.zeros((1, 128), F32)
    for j in range(12):
        row = jnp.where(lane == first + j, new[j][:1, :], row)
    return row


def second_kernel(
    lines, segs, cells_hbm, sent_a, all_ref, source_ref, margin_a, margin_b,
    sums_ref, out_hbm, out_ref, out_sem, *scratch_refs,
):
    line = lax.axis_index("line")
    lists = Lists(cells_hbm, source_ref, (margin_a, margin_b), scratch_refs)
    partner = [jnp.clip(line + 2 * d - 1, 0, lines - 1) for d in lists.dirs]
    sub = iota(0)

    def stacked(a, b, c):
        return jnp.where(sub == 0, spread_out(a), jnp.where(sub == 1, spread_out(b), spread_out(c)))

    totals = stacked(*[line_sum(all_ref, n, segs) for n in (line, partner[0], partner[1])])
    old = stacked(*[ref[3 * MROWS : 3 * MROWS + 1, :] for ref in (sent_a, margin_a, margin_b)])
    new = solve(totals, old)
    negc = (-0.5 * LOG2E) / new_spread(all_ref)
    own, *nbrs = [[spread_out(value[n : n + 1, :]) for value in new] for n in range(3)]
    carry, longest = quick(lists, own, nbrs, negc, [0, 1], no_sums(), jnp.zeros(TILE, F32), out_ref)
    close(lists, own, nbrs, negc, carry, longest, pose_row(new, POSE), sums_ref, (out_hbm, out_ref, out_sem))


def last_kernel(segs, all_ref, fitted_ref, spread_ref):
    line = lax.axis_index("line")
    totals = spread_out(line_sum(all_ref, line, segs))
    old = all_ref[pl.ds(line * segs, 1), :][:, POSE : POSE + 12]
    new = solve(totals, jnp.broadcast_to(old, (8, 12)))
    fitted_ref[...] = pose_row(new, 0)[:, :12]
    spread_ref[...] = new_spread(all_ref)[:1, :1]


def vmem(count):
    return [pl.BlockSpec(memory_space=pltpu.VMEM)] * count


ANY = pl.BlockSpec(memory_space=pl.ANY)
HBM = pl.BlockSpec(memory_space=pltpu.HBM)
SMEM = pl.BlockSpec(memory_space=pltpu.SMEM)
PARAMS = pltpu.CompilerParams(vmem_limit_bytes=32 * 1024 * 1024)


def scratch():
    return [
        pltpu.VMEM((2, 3, MROWS, 128), F32),
        pltpu.VMEM((3, 128, 128), F32),
        pltpu.VMEM((3, 128, 128), F32),
    ]


def in_hbm(value):
    return pltpu.with_memory_space_constraint(value, pltpu.HBM)


def pair_cost(cells, sides):
    pairs = cells.size // 2 * sides * BLOCK * CT
    return pl.CostEstimate(flops=400 * pairs, bytes_accessed=1 << 20, transcendentals=pairs)


def gather_call(rows, sent_a, sent_b):
    return pl.pallas_call(
        gather_kernel,
        in_specs=vmem(3),
        out_specs=vmem(1)[0],
        out_shape=jax.ShapeDtypeStruct((4,) + rows.shape, F32),
        compiler_params=PARAMS,
        cost_estimate=pl.CostEstimate(flops=10**11, bytes_accessed=1 << 20, transcendentals=0),
        name="gather_sources",
    )(rows, sent_a, sent_b)


def partner_call(cells, sent_a, source, margin_a):
    return pl.pallas_call(
        partner_kernel,
        in_specs=[SMEM] + vmem(3),
        out_specs=vmem(1)[0],
        out_shape=jax.ShapeDtypeStruct((6,) + TILE, F32),
        scratch_shapes=scratch(),
        compiler_params=PARAMS,
        cost_estimate=pair_cost(cells, 1),
        name="match_partner",
    )(cells, sent_a, source, margin_a)


def other_call(cells, sent_a, source, part, margin_a, margin_b, devices):
    return pl.pallas_call(
        other_kernel,
        in_specs=[SMEM] + vmem(5),
        out_specs=vmem(1)[0],
        out_shape=jax.ShapeDtypeStruct((devices, 128), F32),
        scratch_shapes=scratch(),
        compiler_params=PARAMS,
        cost_estimate=pair_cost(cells, 1),
        name="match_other",
    )(cells, sent_a, source, part, margin_a, margin_b)


def second_call(cells, sent_a, everyone, source, margin_a, margin_b, lines, segs):
    result = (5,) + source.shape[1:]
    return pl.pallas_call(
        functools.partial(second_kernel, lines, segs),
        in_specs=[SMEM] + vmem(5),
        out_specs=vmem(1) + [ANY],
        out_shape=[jax.ShapeDtypeStruct((lines * segs, 128), F32), jax.ShapeDtypeStruct(result, F32)],
        scratch_shapes=[pltpu.VMEM(result, F32), pltpu.SemaphoreType.DMA] + scratch(),
        compiler_params=PARAMS,
        cost_estimate=pair_cost(cells, 2),
        name="match_second",
    )(cells, sent_a, everyone, source, margin_a, margin_b)


def exchange(sums):
    return lax.all_to_all(sums, ("line", "seg"), 0, 0)


def on_device(lines, segs, points, rows, cells, pose):
    own_points = points.reshape(3, -1, 128)
    slots = rows.shape[-1]
    blocks = slots // BLOCK
    row_list = rows.reshape(2, blocks, 128).transpose(1, 0, 2).reshape(2 * blocks, 128)
    cell_ids = cells.reshape(2, blocks)
    sent_a, sent_b, cell_ids = pack_call(in_hbm(own_points), in_hbm(pose.reshape(1, 12)), in_hbm(cell_ids))
    cell_ids = pltpu.with_memory_space_constraint(cell_ids, pltpu.SMEM)
    pairs_a = [(i, i ^ 1) for i in range(lines)]
    pairs_b = [(i, (((i + 1) ^ 1) - 1) % lines) for i in range(lines)]
    margin_a = lax.ppermute(sent_a, "line", pairs_a)
    margin_b = lax.ppermute(sent_b, "line", pairs_b)
    source = gather_call(row_list, sent_a, sent_b)
    part = partner_call(cell_ids, sent_a, source, margin_a)
    sums = other_call(cell_ids, sent_a, source, part, margin_a, margin_b, lines * segs)
    everyone = exchange(sums)
    sums, result = second_call(cell_ids, sent_a, everyone, source, margin_a, margin_b, lines, segs)
    everyone = exchange(sums)
    fitted, spread = pl.pallas_call(
        functools.partial(last_kernel, segs),
        in_specs=vmem(1),
        out_specs=vmem(2),
        out_shape=[jax.ShapeDtypeStruct((1, 12), F32), jax.ShapeDtypeStruct((1, 1), F32)],
        compiler_params=PARAMS,
        name="solve_last",
    )(everyone)
    result = result.reshape(5, blocks, 2, 128).transpose(2, 0, 1, 3).reshape(1, 1, 2, 5, slots)
    return (result, fitted.reshape(12, 1), spread.reshape(1))


def solution(mesh):
    return jax.shard_map(
        functools.partial(on_device, mesh.shape["line"], mesh.shape["seg"]),
        mesh=mesh,
        in_specs=(
            P("line", "seg", None, None),
            P("line", "seg", None, None),
            P("line", "seg", None, None),
            P(None, "line"),
        ),
        out_specs=(P("line", "seg", None, None, None), P(None, "line"), P()),
        check_vma=False,
    )
```
